32 devices in a mesh: tm: 16 (over z, y, x), src: 2 (over core).
Axes of the slice: x: 2, y: 2, z: 4, core: 2. Of those that a mesh axis runs over, the one named last changes fastest.
Arguments:
- feats: bfloat16 [4, 16384, 128], P(None, ('tm', 'src')), may hold values from -6 to 6
- encoded: bfloat16 [4, 16384, 512], P(None, ('tm', 'src')), may hold values from 0.19921875 to 3
- seg_lengths: int32 [4, 8], replicated, may hold values from 256 to 7168, as said below
- owners: int32 [340, 1], replicated, may hold values from 0 to 31; in each aligned block of 340 rows (0 to 339, 340 to 679, ...) at most 11 rows name the same one
- master: float32 [352, 1024], P(('tm', 'src')), may hold values from -0.375 to 0.375
- moment_one: float32 [352, 1024], P(('tm', 'src')), may hold values from -80 to 80
- moment_two: float32 [352, 1024], P(('tm', 'src')), may hold values from 8.192 to 131.072
- out_cot: bfloat16 [4, 16384, 128], P(None, ('tm', 'src')), may hold values from -6 to 6
- wave_cot: bfloat16 [4, 2, 16384, 16], P(None, 'src', 'tm'), may hold values from -6 to 6
Outputs:
- block_out: bfloat16 [4, 16384, 128], P(None, ('tm', 'src'))
- feats_grad: bfloat16 [4, 16384, 128], P(None, ('tm', 'src'))
- waves: bfloat16 [4, 2, 16384, 16], P(None, 'src', 'tm')
- new_master: float32 [352, 1024], P(('tm', 'src'))
- new_one: float32 [352, 1024], P(('tm', 'src'))
- new_two: float32 [352, 1024], P(('tm', 'src'))
The draws below stay inside these ranges and needn't reach their ends.
Inputs may be any that keep to these rules, and one draw needn't show every extreme that they name: `seg_lengths`: each row sums to 16384. With u = 256, each row holds the lengths u, u, 2u, 3u, 5u, 8u, 16u and 16384 - 36u, in an order drawn from the seed. `owners`: every device owns one or more groups and none more than 11; some device owns exactly 11.
All inputs are finite; a program needn't handle non-finite values.
Results may differ from the reference program's by a relative error of at most 0.0065.
The reference program's roundings to bfloat16 on the way count: a program that leaves them out, or rounds other values in their place, can miss the bound.
Values may be sent and summed in bfloat16 or wider, within the bound.
No kernel may reach another device: no remote copies, remote signals or barrier semaphores. Data moves between devices by JAX's collectives and lax.ppermute only.
A program may use at most 128 MiB of HBM per device.

```python
import math
import jax
import jax.numpy as jnp
import numpy as np
from jax import lax

N = 512
L = 16
B = 128
SC = 128
HIDDEN_WIDTH = 512
C = 2
CONV_DILATION = 128
ROW = 1024
SEGS = 8
MICRO = 4
STEP = 10
STREAM_FRAMES = 16384
NCH = 340
KSLOT = 11
N_TM = 16
N_SRC = 2


def draw_seg_lengths(key, part):
    key = jax.random.fold_in(key, 7)
    unit = STREAM_FRAMES // 64
    table = jnp.array([1, 1, 2, 3, 5, 8, 16], dtype=jnp.int32) * unit
    longest_len = STREAM_FRAMES - 36 * unit
    full_row = jnp.concatenate([table, jnp.full((1,), longest_len, jnp.int32)]).astype(jnp.int32)
    row_keys = jax.random.split(key, MICRO)
    shuffled = jax.vmap(lambda row_key: jax.random.permutation(row_key, full_row))(row_keys)
    return shuffled.astype(jnp.int32)


def block_levels(rng, shape, shards, least, high):
    level = 1.0
    for dim, shards_of in shards:
        draws = jax.random.uniform(jax.random.fold_in(jax.random.fold_in(rng, 6), dim), (shards_of,), jnp.float32, least / len(shards), high / len(shards))
        level = level * jnp.repeat(jnp.exp(draws), shape[dim] // shards_of).reshape((-1,) + (1,) * (len(shape) - 1 - dim))
    return level


def shared_out(key, own, number, rows, amount, top, most, skew):
    ranking = jax.random.permutation(key, amount)
    crowded, usual = load_shares(amount, rows * top, most, skew, True), load_shares(amount, rows * top, most, skew, False)
    places = jnp.arange(amount)

    def named(sizes, turn):
        used = int((sizes > 0).sum())
        fixed = max(1, used // 4)
        moved = fixed + (places - fixed + turn * (used - fixed)) % max(1, amount - fixed)
        return jnp.zeros((amount,), jnp.int32).at[ranking[jnp.where(places < fixed, places, moved)]].set(jnp.asarray(sizes, jnp.int32))

    sizes = jnp.where(number % 4 == 0, named(crowded, number // 4), named(usual, number - number // 4 - 1))
    mixed = jax.random.permutation(jax.random.fold_in(own, 3), amount)
    donor, receiver = mixed[0:amount // 2 * 2:2], mixed[1:amount // 2 * 2:2]
    margin = jnp.minimum(sizes[donor] - 1, most - sizes[receiver]) // 2
    margin = jnp.where((donor == ranking[0]) | (receiver == ranking[0]) | (sizes[receiver] == 0), 0, jnp.maximum(margin, 0))
    moved = jax.random.randint(jax.random.fold_in(own, 4), (amount // 2,), 0, 1 << 20) % (margin + 1)
    sizes = sizes.at[donor].add(-moved).at[receiver].add(moved)
    members = jnp.searchsorted(jnp.cumsum(sizes), jnp.arange(rows * top), side="right").astype(jnp.int32)
    table = members.reshape(top, rows).T
    table = table[jax.random.permutation(jax.random.fold_in(own, 1), rows)]
    turn = jax.random.randint(jax.random.fold_in(own, 2), (rows, 1), 0, top)
    return jnp.take_along_axis(table, (jnp.arange(top)[None, :] + turn) % top, axis=1)


def load_shares(number_of, total, limit, skew, full):
    loads = [(1 << 20) // math.isqrt(grade ** skew) + 1 for grade in range(1, number_of + 1)]
    largest = limit if full else min(limit, max(-(-total // number_of), total * loads[0] // sum(loads)))
    least = 1 if total - largest >= number_of - 1 else 0
    given, surplus = [largest] + [least] * (number_of - 1), total - largest - least * (number_of - 1)
    while surplus > 0:
        candidates = [i for i in range(1, number_of) if given[i] < largest] or [i for i in range(1, number_of) if given[i] < limit]
        mass, budget = sum([loads[i] for i in candidates]), surplus
        for i in candidates:
            extra = min(limit - given[i], max(1, budget * loads[i] // mass), surplus)
            given[i] = given[i] + extra
            surplus = surplus - extra
    return np.array(given)


def gaussian(key, shape, scale, bound, cuts=(), held_as=jnp.bfloat16):
    level = block_levels(key, shape, cuts, -0.22, 0.18) if cuts else 1.0
    result = jax.random.normal(key, shape, jnp.float32) * scale * level
    return jnp.minimum(jnp.maximum(result, -bound), bound).astype(held_as)


def setup_inputs(seed: int = 0) -> dict:
    key_of = jax.random.split(jax.random.key(seed), 10)
    feats = gaussian(key_of[0], (MICRO, STREAM_FRAMES, B), 1.0, 6.0, ((1, 32),))
    encoded = jnp.clip(jnp.exp(math.log(3.0) - 2.7119641 * jax.random.uniform(key_of[1], (MICRO, STREAM_FRAMES, N), jnp.float32) ** block_levels(key_of[1], (MICRO, STREAM_FRAMES, N), ((1, 32),), -0.2, 0.2)), 0.19921875, 3.0).astype(jnp.bfloat16)
    seg_lengths = draw_seg_lengths(jax.random.fold_in(key_of[9], 71), 0)
    owners_keys = jax.random.split(jax.random.fold_in(key_of[3], 1), NCH // NCH)
    owners_turns = jax.random.permutation(jax.random.fold_in(key_of[3], 3), NCH // NCH)
    owners = jax.vmap(lambda own, number: shared_out(jax.random.fold_in(key_of[3], 2), own, number, NCH, N_TM * N_SRC, 1, KSLOT, 1))(owners_keys, owners_turns).reshape((NCH, 1))
    master = gaussian(key_of[4], (N_TM * N_SRC * KSLOT, ROW), 0.06, 0.375, ((0, 32),), jnp.float32)
    moment_one = gaussian(key_of[5], (N_TM * N_SRC * KSLOT, ROW), (0.055 * (MICRO * STREAM_FRAMES) ** 0.5), 80.0, ((0, 32),), jnp.float32)
    moment_two = jnp.clip(jnp.exp(math.log(131.072) - 2.7725887 * jax.random.uniform(key_of[6], (N_TM * N_SRC * KSLOT, ROW), jnp.float32) ** block_levels(key_of[6], (N_TM * N_SRC * KSLOT, ROW), ((0, 32),), -0.2, 0.2)), 8.192, 131.072)
    out_cot = gaussian(key_of[7], (MICRO, STREAM_FRAMES, B), 1.0, 6.0, ((1, 32),))
    wave_cot = gaussian(key_of[8], (MICRO, C, STREAM_FRAMES, L), 1.0, 6.0, ((1, 2), (2, 16)))
    return {"feats": feats, "encoded": encoded, "seg_lengths": seg_lengths, "owners": owners, "master": master, "moment_one": moment_one, "moment_two": moment_two, "out_cot": out_cot, "wave_cot": wave_cot}


@jax.custom_vjp
def low(v):
    return lax.optimization_barrier(v.astype(jnp.bfloat16)).astype(jnp.float32)

@jax.custom_vjp
def low_back(v):
    return v

def low_keep(v):
    return (low(v), None)

def low_pass(kept, grad):
    return (grad,)

def back_keep(v):
    return (v, None)

def back_low(kept, grad):
    return (low(grad),)
low.defvjp(low_keep, low_pass)
low_back.defvjp(back_keep, back_low)
highest = lax.Precision.HIGHEST
norm_eps = 1e-05
adam_eps = 1e-08
beta_one = 0.9
beta_two = 0.999
learn_rate = 0.2
weight_decay = 0.01

def matmul(left_side, right_side):
    return jnp.dot(left_side, right_side, precision=highest)

def unpack(flat_params):
    shapes = [(B, HIDDEN_WIDTH), (HIDDEN_WIDTH, B), (HIDDEN_WIDTH, SC), (C, SC, N), (C, N, L), (4, HIDDEN_WIDTH), (4, HIDDEN_WIDTH)]
    offset = 0
    pieces = []
    for piece_shape in shapes:
        piece_size = 1
        for extent in piece_shape:
            piece_size = piece_size * extent
        pieces.append(flat_params[offset:offset + piece_size].reshape(piece_shape))
        offset = offset + piece_size
    return pieces

def segment_ids(lengths):
    bounds = jnp.cumsum(lengths).astype(jnp.int32)
    position_list = jnp.arange(STREAM_FRAMES, dtype=jnp.int32)
    return lax.optimization_barrier(jnp.sum((position_list[:, None] >= bounds[None, :]).astype(jnp.int32), axis=1)).astype(jnp.int32)

def norm_apply(values, segment_labels, counts, gain, shift):
    first_sum = jax.ops.segment_sum(lax.optimization_barrier(jnp.sum(values, axis=1)), segment_labels, num_segments=SEGS)
    second = jax.ops.segment_sum(lax.optimization_barrier(jnp.sum(values * values, axis=1)), segment_labels, num_segments=SEGS)
    center = first_sum / counts
    factor = lax.rsqrt(second / counts - center * center + norm_eps)
    return (values - center[segment_labels][:, None]) * factor[segment_labels][:, None] * (1.0 + gain) + shift

def depthwise(normalized_rows, segment_labels, filter_tap_rows, filter_tap_bias):
    blank_rows = jnp.zeros((CONV_DILATION, HIDDEN_WIDTH), normalized_rows.dtype)
    padded_rows = jnp.concatenate([blank_rows, normalized_rows, blank_rows], axis=0)
    padding_value = jnp.full((CONV_DILATION,), -1, jnp.int32)
    segment_index_padded = jnp.concatenate([padding_value, segment_labels, padding_value]).astype(jnp.int32)
    before_valid = (segment_index_padded[:STREAM_FRAMES] == segment_labels).astype(normalized_rows.dtype)[:, None]
    after_valid = (segment_index_padded[2 * CONV_DILATION:] == segment_labels).astype(normalized_rows.dtype)[:, None]
    return filter_tap_rows[0] * padded_rows[:STREAM_FRAMES] * before_valid + filter_tap_rows[1] * normalized_rows + filter_tap_rows[2] * padded_rows[2 * CONV_DILATION:] * after_valid + filter_tap_bias

def micro_loss(flat_params, feats, encoded, lengths, out_cot, wave_cot):
    w_in, w_res, w_skip, w_mask, w_dec, norm_rows, depth_rows = unpack(flat_params)
    segment_labels = segment_ids(lengths)
    counts = lengths.astype(feats.dtype) * HIDDEN_WIDTH
    pre_in = low_back(matmul(feats, w_in))
    hidden = jax.nn.silu(pre_in)
    normalized_single = low(norm_apply(hidden, segment_labels, counts, norm_rows[0], norm_rows[1]))
    pre_depth = low_back(depthwise(normalized_single, segment_labels, depth_rows[:3], depth_rows[3]))
    normed_two = low(norm_apply(jax.nn.silu(pre_depth), segment_labels, counts, norm_rows[2], norm_rows[3]))
    block_val = feats + matmul(normed_two, w_res)
    skip_pre = low_back(matmul(normed_two, w_skip))
    gated_act = low(jax.nn.silu(skip_pre))
    wave_list = []
    for source in range(C):
        logits = low_back(matmul(gated_act, w_mask[source]))
        masked = low(jax.nn.sigmoid(logits) * encoded)
        wave_list.append(matmul(masked, w_dec[source]))
    wave_vals = jnp.stack(wave_list)
    loss_value = jnp.sum(block_val * out_cot) + jnp.sum(wave_vals * wave_cot)
    return (loss_value, (block_val, wave_vals))

def reference(feats, encoded, seg_lengths, owners, master, moment_one, moment_two, out_cot, wave_cot):
    owner_ids = owners[:, 0].astype(jnp.int32)
    slot_total = N_TM * N_SRC * KSLOT
    group_order = jnp.arange(NCH, dtype=jnp.int32)
    earlier = (owner_ids[:, None] == owner_ids[None, :]) & (group_order[None, :] < group_order[:, None])
    slot_rank = lax.optimization_barrier(jnp.sum(earlier.astype(jnp.int32), axis=1)).astype(jnp.int32)
    slot_place = (owner_ids * KSLOT + slot_rank).astype(jnp.int32)
    copies = master[slot_place].astype(jnp.bfloat16).astype(jnp.float32)
    flat_params = copies.reshape(-1)
    feats_f = feats.astype(jnp.float32)
    encoded_f = encoded.astype(jnp.float32)
    out_cot_f = out_cot.astype(jnp.float32)
    wave_cot_f = wave_cot.astype(jnp.float32)

    def total(params_now, feats_now):

        def micro_step(loss_sum, micro_batch):
            loss_value, extras = jax.checkpoint(micro_loss)(params_now, *micro_batch)
            return (loss_sum + loss_value, extras)
        loss_sum, extras = lax.scan(micro_step, jnp.zeros((), jnp.float32), (feats_now, encoded_f, seg_lengths, out_cot_f, wave_cot_f))
        return (loss_sum, extras)
    loss_sum, pullback, extras = jax.vjp(total, flat_params, feats_f, has_aux=True)
    grad_flat, grad_feats = pullback(jnp.ones_like(loss_sum))
    block_vals, wave_vals = extras
    grads = grad_flat.reshape(NCH, ROW)
    slot_grads = jnp.zeros((slot_total, ROW), jnp.float32).at[slot_place].set(grads)
    used_rows = jnp.zeros((slot_total,), jnp.float32).at[slot_place].set(1.0)[:, None]
    new_one = beta_one * moment_one + (1.0 - beta_one) * slot_grads
    new_two = beta_two * moment_two + (1.0 - beta_two) * slot_grads * slot_grads
    unbias_one = new_one / (1.0 - beta_one ** STEP)
    unbias_two = new_two / (1.0 - beta_two ** STEP)
    new_master = master - learn_rate * (unbias_one / (jnp.sqrt(unbias_two) + adam_eps) + weight_decay * master)
    return (block_vals.astype(jnp.bfloat16), grad_feats.astype(jnp.bfloat16), wave_vals.astype(jnp.bfloat16), new_master * used_rows, new_one * used_rows, new_two * used_rows)
```

```python
import functools

import jax
import jax.numpy as jnp
from jax import lax
from jax.experimental import pallas as pl
from jax.experimental.pallas import tpu as pltpu
from jax.sharding import PartitionSpec as P

N = 512
L = 16
B = 128
SC = 128
HW = 512
C = 2
DIL = 128
ROW = 1024
SEGS = 8
MICRO = 4
STEP = 10
NCH = 340
BLK = 256
KINDS = 8

norm_eps = 1e-05
adam_eps = 1e-08
beta_one = 0.9
beta_two = 0.999
learn_rate = 0.2
weight_decay = 0.01

AXES = ("tm", "src")
f32 = jnp.float32
bf16 = jnp.bfloat16
VMEM_LIMIT = 56 * 1024 * 1024

R_IN, R_RES, R_SKIP, R_MASK, R_DEC, R_VEC = 0, 512, 1024, 1536, 2560, 2688
ROWS_ALL = 2720


def mm(a, b):
    return lax.dot_general(a, b, (((1,), (0,)), ((), ())), preferred_element_type=f32)


def mm_t(a, b):
    return lax.dot_general(a, b, (((1,), (1,)), ((), ())), preferred_element_type=f32)


def mm_rows(a, b):
    return lax.dot_general(a, b, (((0,), (0,)), ((), ())), preferred_element_type=f32)


def sigmoid(v):
    return 0.5 * jnp.tanh(0.5 * v) + 0.5


def vmem():
    return pl.BlockSpec(memory_space=pltpu.VMEM)


def smem():
    return pl.BlockSpec(memory_space=pltpu.SMEM)


def stages(n_dev):
    bits = n_dev.bit_length() - 1
    groups = []
    hi = bits - 1
    while hi >= 1:
        lo = max(1, hi - 1)
        groups.append(tuple(range(lo, hi + 1)))
        hi = lo - 1
    groups.append((0,))
    return groups


def spread(bits, k):
    return sum(((k >> j) & 1) << b for j, b in enumerate(bits))


def swap(value, mask, n_dev):
    return lax.ppermute(value, AXES, [(i, i ^ mask) for i in range(n_dev)])


def gather_tiles(tiles, n_dev):
    z = tiles
    groups = stages(n_dev)
    for bits in groups[:-1]:
        parts = [z] + [swap(z, spread(bits, k), n_dev) for k in range(1, 1 << len(bits))]
        z = jnp.concatenate(parts, axis=0)
    return z, swap(z, 1, n_dev)


def relative_block(owner, me, n_dev):
    q = owner ^ me
    index = jnp.zeros_like(q)
    size = 1
    for bits in stages(n_dev):
        digit = sum(((q >> b) & 1) << j for j, b in enumerate(bits))
        index = index + digit * size
        size = size << len(bits)
    return index


def share_sums(rows, n_dev):
    return lax.all_to_all(rows, AXES, 0, 0, tiled=True)


def tile_kernel(m_ref, out_ref, buf):
    slots = m_ref.shape[0]
    for j in range(8):
        buf[pl.ds(j, slots, stride=8), :] = m_ref[:, 128 * j : 128 * j + 128]
    out_ref[...] = buf[...].astype(bf16)


def to_tiles(master):
    slots = master.shape[0]
    return pl.pallas_call(
        tile_kernel,
        out_shape=jax.ShapeDtypeStruct((slots * 8, 128), bf16),
        in_specs=[vmem()],
        out_specs=vmem(),
        scratch_shapes=[pltpu.VMEM((slots * 8, 128), f32)],
        name="to_tiles",
    )(master)


def stat_rows(values, shape):
    lane = lax.broadcasted_iota(jnp.int32, shape, 1)
    row = jnp.zeros(shape, f32)
    for where, v in values.items():
        row = jnp.where(lane == where, v, row)
    return row


def unpack_kernel(
    pos_ref, own_ref, got_ref, x_ref, w_in, w_rs, w_mask, w_dec, w_dect, vec, stats, g, t, wd
):
    half = own_ref.shape[0]
    g[0:half, :] = own_ref[...].astype(f32)
    g[half : 2 * half, :] = got_ref[...].astype(f32)
    for i in range(NCH):
        start = pl.multiple_of(pos_ref[i] * 8, 8)
        t[8 * i : 8 * i + 8, :] = g[pl.ds(start, 8), :]
    for k in range(4):
        cols = slice(128 * k, 128 * k + 128)
        w_in[:, cols] = t[pl.ds(R_IN + k, 128, stride=4), :].astype(bf16)
        for c in range(C):
            w_mask[:, 512 * c + 128 * k : 512 * c + 128 * k + 128] = t[
                pl.ds(R_MASK + 512 * c + k, 128, stride=4), :
            ].astype(bf16)
        vec[:, cols] = t[pl.ds(R_VEC + k, 8, stride=4), :]
    w_rs[:, 0:128] = t[R_RES : R_RES + 512, :].astype(bf16)
    w_rs[:, 128:256] = t[R_SKIP : R_SKIP + 512, :].astype(bf16)
    part = lax.broadcasted_iota(jnp.int32, (64, 128), 1) // L
    for s in range(8):
        for c in range(C):
            rows = t[R_DEC + 64 * c : R_DEC + 64 * c + 64, :]
            rows = pltpu.roll(rows, (L * (c - s)) % 128, 1)
            wd[pl.ds(512 * c + s, 64, stride=8), :] = jnp.where(part == c, rows, 0.0)
    dec = wd[...]
    w_dec[...] = dec.astype(bf16)
    w_dect[...] = dec.T.astype(bf16)
    micro, frames, _ = x_ref.shape
    nb = frames // BLK
    sums = {}
    for m in range(micro):
        for b in range(nb):
            a = mm(x_ref[m, b * BLK : (b + 1) * BLK, :], w_in[...])
            u = a * sigmoid(a)
            first = jnp.sum(jnp.sum(u, axis=0, keepdims=True), axis=1, keepdims=True)
            second = jnp.sum(jnp.sum(u * u, axis=0, keepdims=True), axis=1, keepdims=True)
            sums[(m * nb + b) * KINDS] = first
            sums[(m * nb + b) * KINDS + 1] = second
    row = stat_rows(sums, (1, 128))
    stats[...] = jnp.broadcast_to(row[None], stats.shape)


def unpack(pos, own, got, feats, n_dev):
    outs = (
        jax.ShapeDtypeStruct((B, HW), bf16),
        jax.ShapeDtypeStruct((HW, B + SC), bf16),
        jax.ShapeDtypeStruct((SC, C * N), bf16),
        jax.ShapeDtypeStruct((C * N, 128), bf16),
        jax.ShapeDtypeStruct((128, C * N), bf16),
        jax.ShapeDtypeStruct((8, HW), f32),
        jax.ShapeDtypeStruct((n_dev, 1, 128), f32),
    )
    return pl.pallas_call(
        unpack_kernel,
        out_shape=outs,
        in_specs=[smem(), vmem(), vmem(), vmem()],
        out_specs=tuple(vmem() for _ in outs),
        scratch_shapes=[
            pltpu.VMEM((2 * own.shape[0], 128), f32),
            pltpu.VMEM((ROWS_ALL, 128), f32),
            pltpu.VMEM((C * N, 128), f32),
        ],
        compiler_params=pltpu.CompilerParams(vmem_limit_bytes=VMEM_LIMIT),
        name="unpack",
    )(pos, own, got, feats)


def norm_scale(stats, sel):
    means, factors = [], []
    lane = lax.broadcasted_iota(jnp.int32, (1, 128), 1) % KINDS
    for o in range(sel.shape[0]):
        t = jnp.sum(stats * sel[o], axis=0, keepdims=True)
        mean = jnp.sum(jnp.where(lane == 0, t, 0.0), axis=1, keepdims=True)
        second = jnp.sum(jnp.where(lane == 1, t, 0.0), axis=1, keepdims=True)
        means.append(mean)
        factors.append(lax.rsqrt(second - mean * mean + norm_eps))
    return means, factors


def taps(vec, same_ref, m, nb):
    k0, k2 = vec[4:5, :], vec[6:7, :]
    out = []
    for h in range(2 * nb):
        lo = k0 * same_ref[m, h // 2] if h % 2 == 0 else k0
        hi = k2 if h % 2 == 0 else k2 * same_ref[m, h // 2 + 1]
        out.append((lo, hi))
    return out


def depth_kernel(
    same_ref, stats_ref, sel_ref, x_ref, xb_ref, xa_ref, w_in, vec, d_ref, out_stats, acc
):
    m = pl.program_id(0)
    frames = x_ref.shape[1]
    nb = frames // BLK
    means, factors = norm_scale(stats_ref[:, 0, :], sel_ref[0])
    g1, b1 = 1.0 + vec[0:1, :], vec[1:2, :]

    def normed(x, o):
        a = mm(x, w_in[...])
        u = a * sigmoid(a)
        scale = factors[o] * g1
        return (u * scale + (b1 - means[o] * scale)).astype(bf16).astype(f32)

    n1 = [normed(xb_ref[0], 0)]
    for h in range(2 * nb):
        n1.append(normed(x_ref[0, h * DIL : (h + 1) * DIL, :], 1 + h // 2))
    n1.append(normed(xa_ref[0], nb + 1))
    tap = taps(vec, same_ref, m, nb)
    k1, kb = vec[5:6, :], vec[7:8, :]
    lane = lax.broadcasted_iota(jnp.int32, (1, 128), 1)
    row = jnp.where(m == 0, jnp.zeros((1, 128), f32), acc[...])
    for b in range(nb):
        first, second = 0.0, 0.0
        for h in (2 * b, 2 * b + 1):
            d = tap[h][0] * n1[h] + k1 * n1[h + 1] + tap[h][1] * n1[h + 2] + kb
            d_ref[0, h * DIL : (h + 1) * DIL, :] = d
            v = d * sigmoid(d)
            first = first + jnp.sum(v, axis=0, keepdims=True)
            second = second + jnp.sum(v * v, axis=0, keepdims=True)
        at = (m * nb + b) * KINDS
        row = jnp.where(lane == at, jnp.sum(first, axis=1, keepdims=True), row)
        row = jnp.where(lane == at + 1, jnp.sum(second, axis=1, keepdims=True), row)
    acc[...] = row
    out_stats[...] = jnp.broadcast_to(row[None], out_stats.shape)


def per_micro(shape):
    rest = tuple(shape[1:])
    zeros = (0,) * len(rest)
    return pl.BlockSpec((1,) + rest, lambda m: (m,) + zeros)


def whole(shape):
    zeros = (0,) * len(shape)
    return pl.BlockSpec(tuple(shape), lambda m: zeros)


def depth(same, stats, sel, feats, before, after, w_in, vec):
    micro, frames, _ = feats.shape
    return pl.pallas_call(
        depth_kernel,
        grid=(micro,),
        out_shape=(
            jax.ShapeDtypeStruct((micro, frames, HW), f32),
            jax.ShapeDtypeStruct(stats.shape, f32),
        ),
        in_specs=[
            smem(),
            whole(stats.shape),
            per_micro(sel.shape),
            per_micro(feats.shape),
            per_micro(before.shape),
            per_micro(after.shape),
            whole(w_in.shape),
            whole(vec.shape),
        ],
        out_specs=(per_micro((micro, frames, HW)), whole(stats.shape)),
        scratch_shapes=[pltpu.VMEM((1, 128), f32)],
        compiler_params=pltpu.CompilerParams(vmem_limit_bytes=VMEM_LIMIT),
        name="depth",
    )(same, stats, sel, feats, before, after, w_in, vec)


def head_kernel(
    same_ref,
    stats_ref,
    sel_ref,
    d_ref,
    x_ref,
    enc_ref,
    dy_ref,
    dw_ref,
    w_rs,
    w_mask,
    w_dec,
    w_dect,
    vec,
    block_ref,
    waves_ref,
    dn2_ref,
    out_stats,
    g_rs,
    g_mask,
    g_dec,
    g_vec,
    acc,
):
    m = pl.program_id(0)
    frames = d_ref.shape[1]
    nb = frames // BLK

    @pl.when(m == 0)
    def _():
        g_rs[...] = jnp.zeros_like(g_rs)
        g_mask[...] = jnp.zeros_like(g_mask)
        g_dec[...] = jnp.zeros_like(g_dec)
        g_vec[...] = jnp.zeros_like(g_vec)
        acc[...] = jnp.zeros_like(acc)

    means, factors = norm_scale(stats_ref[:, 0, :], sel_ref[0])
    g1, g2, b1, b2 = 1.0 + vec[0:1, :], 1.0 + vec[2:3, :], vec[1:2, :], vec[3:4, :]
    k1, kb = vec[5:6, :], vec[7:8, :]
    tap = taps(vec, same_ref, m, nb)
    lane = lax.broadcasted_iota(jnp.int32, (1, 128), 1)
    row = acc[...]
    for b in range(nb):
        rows = slice(b * BLK, (b + 1) * BLK)
        mean, factor = means[1 + b], factors[1 + b]
        scale = factor * g2
        shift = b2 - mean * scale
        d = d_ref[0, rows, :]
        v = d * sigmoid(d)
        n2 = (v * scale + shift).astype(bf16)
        ys = mm(n2, w_rs[...])
        block_ref[0, rows, :] = (x_ref[0, rows, :].astype(f32) + ys[:, 0:B]).astype(bf16)
        s = ys[:, B : B + SC]
        sg = sigmoid(s)
        z = (s * sg).astype(bf16)
        slope = sg * (1.0 + s * (1.0 - sg))
        dw = dw_ref[0, rows, :]
        enc = enc_ref[0, rows, :].astype(f32)
        dz = jnp.zeros((BLK, SC), f32)
        wave = jnp.zeros((BLK, 128), f32)
        for c in range(C):
            cols = slice(c * N, (c + 1) * N)
            p = sigmoid(mm(z, w_mask[:, cols]))
            pe = p * enc
            e = pe.astype(bf16)
            wave = wave + mm(e, w_dec[cols, :])
            dq = (mm(dw, w_dect[0 : C * L, cols]) * (pe - pe * p)).astype(bf16)
            dz = dz + mm_t(dq, w_mask[:, cols])
            g_dec[:, cols] += mm_rows(dw, e)
            g_mask[:, cols] += mm_rows(z, dq)
        waves_ref[0, rows, :] = wave[:, 0 : C * L].astype(bf16)
        ds = (dz * slope).astype(bf16)
        dys = jnp.concatenate([dy_ref[0, rows, :], ds], axis=1)
        dn2 = mm_t(dys, w_rs[...])
        g_rs[...] += mm_rows(dys, n2)
        dn2_ref[0, rows, :] = dn2
        sum_d = jnp.sum(dn2, axis=0, keepdims=True)
        sum_dv = jnp.sum(dn2 * v, axis=0, keepdims=True)
        gain = (sum_dv - mean * sum_d) * factor
        g_vec[2:3, :] += gain
        g_vec[3:4, :] += sum_d
        vals = [sum_d * g2, gain * g2]
        six = [jnp.zeros((1, HW), f32)] * 6
        for h in (0, 1):
            hr = slice(b * BLK + h * DIL, b * BLK + (h + 1) * DIL)
            dh = d_ref[0, hr, :]
            sig = sigmoid(dh)
            vh = dh * sig
            sd = sig + vh * (1.0 - sig)
            a = dn2_ref[0, hr, :] * sd
            cv = vh * sd
            a0 = jnp.sum(a, axis=0, keepdims=True)
            a1 = jnp.sum(a * dh, axis=0, keepdims=True)
            s0 = jnp.sum(sd, axis=0, keepdims=True)
            s1 = jnp.sum(sd * dh, axis=0, keepdims=True)
            c0 = jnp.sum(cv, axis=0, keepdims=True)
            c1 = jnp.sum(cv * dh, axis=0, keepdims=True)
            lo, hi = tap[2 * b + h]
            kappa = k1 + lo + hi
            vw = g1 * kappa
            delta = kb + b1 * kappa
            a0, a1 = a0 * scale, a1 * scale
            s0, s1 = s0 * factor, s1 * factor
            c0, c1 = c0 * factor * factor - mean * factor * s0, c1 * factor * factor - mean * factor * s1
            new = [vw * a0, vw * s0, vw * c0, a1 - delta * a0, s1 - delta * s0, c1 - delta * c0]
            six = [p0 + p1 for p0, p1 in zip(six, new)]
        for k, val in enumerate(vals + six):
            at = (m * nb + b) * KINDS + k
            row = jnp.where(lane == at, jnp.sum(val, axis=1, keepdims=True), row)
    acc[...] = row
    out_stats[...] = jnp.broadcast_to(row[None], out_stats.shape)


def head(same, stats, sel, d, feats, enc, dy, dw, w_rs, w_mask, w_dec, w_dect, vec):
    micro, frames, _ = feats.shape
    outs = (
        (feats.shape, bf16, True),
        ((micro, frames, C * L), bf16, True),
        (d.shape, f32, True),
        (stats.shape, f32, False),
        ((B + SC, HW), f32, False),
        ((SC, C * N), f32, False),
        ((C * L, C * N), f32, False),
        ((8, HW), f32, False),
    )
    return pl.pallas_call(
        head_kernel,
        grid=(micro,),
        out_shape=tuple(jax.ShapeDtypeStruct(s, t) for s, t, _ in outs),
        in_specs=[
            smem(),
            whole(stats.shape),
            per_micro(sel.shape),
            per_micro(d.shape),
            per_micro(feats.shape),
            per_micro(enc.shape),
            per_micro(dy.shape),
            per_micro(dw.shape),
            whole(w_rs.shape),
            whole(w_mask.shape),
            whole(w_dec.shape),
            whole(w_dect.shape),
            whole(vec.shape),
        ],
        out_specs=tuple(per_micro(s) if each else whole(s) for s, _, each in outs),
        scratch_shapes=[pltpu.VMEM((1, 128), f32)],
        compiler_params=pltpu.CompilerParams(vmem_limit_bytes=VMEM_LIMIT),
        name="head",
    )(same, stats, sel, d, feats, enc, dy, dw, w_rs, w_mask, w_dec, w_dect, vec)


def back_means(stats, sel):
    lane = lax.broadcasted_iota(jnp.int32, (1, 128), 1) % KINDS
    t = jnp.sum(stats * sel, axis=0, keepdims=True)
    v = [jnp.sum(jnp.where(lane == k, t, 0.0), axis=1, keepdims=True) for k in range(KINDS)]
    p2, q2 = v[0], v[1]
    return p2, q2, v[2] - p2 * v[3] - q2 * v[4], v[5] - p2 * v[6] - q2 * v[7]


def depth_grad(d, dn2, mean, factor, g2, p2, q2):
    sig = sigmoid(d)
    v = d * sig
    sd = sig + v * (1.0 - sig)
    scale = factor * g2
    slope = factor * factor * q2
    shift = factor * p2 - slope * mean
    return (sd * (dn2 * scale - v * slope - shift)).astype(bf16)


def edge_kernel(stats2_ref, stats3_ref, sel_ref, d_ref, dn2_ref, vec, lo_ref, hi_ref):
    frames = d_ref.shape[1]
    nb = frames // BLK
    means, factors = norm_scale(stats2_ref[:, 0, :], sel_ref[0])
    g2 = 1.0 + vec[2:3, :]
    for ref, b, start in ((lo_ref, 0, 0), (hi_ref, nb - 1, frames - DIL)):
        p2, q2, _, _ = back_means(stats3_ref[:, 0, :], sel_ref[0, 1 + b])
        rows = slice(start, start + DIL)
        ref[0] = depth_grad(
            d_ref[0, rows, :], dn2_ref[0, rows, :], means[1 + b], factors[1 + b], g2, p2, q2
        )


def edges(stats2, stats3, sel, d, dn2, vec):
    micro, frames, _ = d.shape
    return pl.pallas_call(
        edge_kernel,
        grid=(micro,),
        out_shape=(jax.ShapeDtypeStruct((micro, DIL, HW), bf16),) * 2,
        in_specs=[
            whole(stats2.shape),
            whole(stats3.shape),
            per_micro(sel.shape),
            per_micro(d.shape),
            per_micro(dn2.shape),
            whole(vec.shape),
        ],
        out_specs=(per_micro((micro, DIL, HW)),) * 2,
        compiler_params=pltpu.CompilerParams(vmem_limit_bytes=VMEM_LIMIT),
        name="edges",
    )(stats2, stats3, sel, d, dn2, vec)


def input_kernel(
    same_ref,
    stats1_ref,
    stats2_ref,
    stats3_ref,
    sel_ref,
    d_ref,
    dn2_ref,
    lo_ref,
    hi_ref,
    x_ref,
    dy_ref,
    w_in,
    vec,
    feats_ref,
    g_in,
    g_vec,
):
    m = pl.program_id(0)
    frames = d_ref.shape[1]
    nb = frames // BLK

    @pl.when(m == 0)
    def _():
        g_in[...] = jnp.zeros_like(g_in)
        g_vec[...] = jnp.zeros_like(g_vec)

    sel = sel_ref[0]
    mean1, factor1 = norm_scale(stats1_ref[:, 0, :], sel)
    mean2, factor2 = norm_scale(stats2_ref[:, 0, :], sel)
    g1, g2, b1 = 1.0 + vec[0:1, :], 1.0 + vec[2:3, :], vec[1:2, :]
    k0, k1, k2 = vec[4:5, :], vec[5:6, :], vec[6:7, :]
    back = [back_means(stats3_ref[:, 0, :], sel[1 + b]) for b in range(nb)]
    dd = [lo_ref[0].astype(f32)]
    for h in range(2 * nb):
        rows = slice(h * DIL, (h + 1) * DIL)
        b = h // 2
        dd.append(
            depth_grad(
                d_ref[0, rows, :], dn2_ref[0, rows, :], mean2[1 + b], factor2[1 + b], g2, back[b][0], back[b][1]
            ).astype(f32)
        )
    dd.append(hi_ref[0].astype(f32))
    zero = jnp.zeros((1, HW), f32)
    t0, t1, t2, tb, gg, gb = zero, zero, zero, zero, zero, zero
    for h in range(2 * nb):
        b = h // 2
        rows = slice(h * DIL, (h + 1) * DIL)
        x = x_ref[0, rows, :]
        a = mm(x, w_in[...])
        sig = sigmoid(a)
        u = a * sig
        mean, factor = mean1[1 + b], factor1[1 + b]
        scale = factor * g1
        n1 = (u * scale + (b1 - mean * scale)).astype(bf16).astype(f32)
        lo = same_ref[m, b] if h % 2 == 0 else 1.0
        hi = 1.0 if h % 2 == 0 else same_ref[m, b + 1]
        here, prev, nxt = dd[h + 1], dd[h], dd[h + 2]
        t0 = t0 + jnp.sum(nxt * n1, axis=0, keepdims=True) * hi
        t1 = t1 + jnp.sum(here * n1, axis=0, keepdims=True)
        t2 = t2 + jnp.sum(prev * n1, axis=0, keepdims=True) * lo
        tb = tb + jnp.sum(here, axis=0, keepdims=True)
        dn1 = k1 * here + (k0 * hi) * nxt + (k2 * lo) * prev
        h1 = (u - mean) * factor
        gg = gg + jnp.sum(dn1 * h1, axis=0, keepdims=True)
        gb = gb + jnp.sum(dn1, axis=0, keepdims=True)
        du = factor * (dn1 * g1 - back[b][2] - h1 * back[b][3])
        da = (du * (sig + u * (1.0 - sig))).astype(bf16)
        g_in[...] += mm_rows(x, da)
        feats_ref[0, rows, :] = (dy_ref[0, rows, :].astype(f32) + mm_t(da, w_in[...])).astype(bf16)
    for r, val in ((0, gg), (1, gb), (4, t0), (5, t1), (6, t2), (7, tb)):
        g_vec[r : r + 1, :] += val


def input_grad(same, stats1, stats2, stats3, sel, d, dn2, lo, hi, feats, dy, w_in, vec):
    micro, frames, _ = d.shape
    return pl.pallas_call(
        input_kernel,
        grid=(micro,),
        out_shape=(
            jax.ShapeDtypeStruct(feats.shape, bf16),
            jax.ShapeDtypeStruct((B, HW), f32),
            jax.ShapeDtypeStruct((8, HW), f32),
        ),
        in_specs=[
            smem(),
            whole(stats1.shape),
            whole(stats2.shape),
            whole(stats3.shape),
            per_micro(sel.shape),
            per_micro(d.shape),
            per_micro(dn2.shape),
            per_micro(lo.shape),
            per_micro(hi.shape),
            per_micro(feats.shape),
            per_micro(dy.shape),
            whole(w_in.shape),
            whole(vec.shape),
        ],
        out_specs=(per_micro(feats.shape), whole((B, HW)), whole((8, HW))),
        compiler_params=pltpu.CompilerParams(vmem_limit_bytes=VMEM_LIMIT),
        name="input_grad",
    )(same, stats1, stats2, stats3, sel, d, dn2, lo, hi, feats, dy, w_in, vec)


def pack_kernel(pos_ref, g_in, g_rs, g_mask, g_dec, vec_a, vec_b, keep_ref, send_ref, t, out, wd):
    for k in range(4):
        cols = slice(128 * k, 128 * k + 128)
        t[pl.ds(R_IN + k, 128, stride=4), :] = g_in[:, cols]
        for c in range(C):
            t[pl.ds(R_MASK + 512 * c + k, 128, stride=4), :] = g_mask[
                :, 512 * c + 128 * k : 512 * c + 128 * k + 128
            ]
        t[pl.ds(R_VEC + k, 8, stride=4), :] = vec_a[:, cols] + vec_b[:, cols]
    t[R_RES : R_RES + 512, :] = g_rs[0:128, :].T
    t[R_SKIP : R_SKIP + 512, :] = g_rs[128:256, :].T
    wd[...] = jnp.concatenate([g_dec[...], jnp.zeros((128 - C * L, C * N), f32)], axis=0).T
    part = lax.broadcasted_iota(jnp.int32, (64, 128), 1) // L
    for c in range(C):
        rows = jnp.zeros((64, 128), f32)
        for s in range(8):
            piece = pltpu.roll(wd[pl.ds(512 * c + s, 64, stride=8), :], (L * (s - c)) % 128, 1)
            rows = jnp.where(part == s, piece, rows)
        t[R_DEC + 64 * c : R_DEC + 64 * c + 64, :] = rows
    out[...] = jnp.zeros_like(out)
    for i in range(NCH):
        start = pl.multiple_of(pos_ref[i] * 8, 8)
        out[pl.ds(start, 8), :] = t[8 * i : 8 * i + 8, :]
    half = keep_ref.shape[0]
    keep_ref[...] = out[0:half, :]
    send_ref[...] = out[half : 2 * half, :].astype(bf16)


def pack(pos, g_in, g_rs, g_mask, g_dec, vec_a, vec_b, rows):
    return pl.pallas_call(
        pack_kernel,
        out_shape=(
            jax.ShapeDtypeStruct((rows // 2, 128), f32),
            jax.ShapeDtypeStruct((rows // 2, 128), bf16),
        ),
        in_specs=[smem()] + [vmem()] * 6,
        out_specs=(vmem(), vmem()),
        scratch_shapes=[
            pltpu.VMEM((ROWS_ALL, 128), f32),
            pltpu.VMEM((rows, 128), f32),
            pltpu.VMEM((C * N, 128), f32),
        ],
        compiler_params=pltpu.CompilerParams(vmem_limit_bytes=VMEM_LIMIT),
        name="pack",
    )(pos, g_in, g_rs, g_mask, g_dec, vec_a, vec_b)


def fold_kernel(n_got, n_next, *refs):
    keep_ref, got = refs[0], refs[1 : 1 + n_got]
    outs = refs[1 + n_got :]
    total = keep_ref[...]
    for g in got:
        total = total + g[...].astype(f32)
    size = total.shape[0] // n_next
    outs[0][...] = total[0:size, :]
    for q in range(1, n_next):
        outs[q][...] = total[q * size : (q + 1) * size, :].astype(bf16)


def fold(keep, got, n_next):
    size = keep.shape[0] // n_next
    outs = [jax.ShapeDtypeStruct((size, 128), f32)]
    outs += [jax.ShapeDtypeStruct((size, 128), bf16)] * (n_next - 1)
    return pl.pallas_call(
        functools.partial(fold_kernel, len(got), n_next),
        out_shape=tuple(outs),
        in_specs=[vmem()] * (1 + len(got)),
        out_specs=tuple(vmem() for _ in outs),
        name="fold",
    )(keep, *got)


def adam_kernel(n_got, count_ref, *refs):
    keep_ref, got = refs[0], refs[1 : 1 + n_got]
    master_ref, one_ref, two_ref, new_master, new_one, new_two, buf = refs[1 + n_got :]
    total = keep_ref[...]
    for g in got:
        total = total + g[...].astype(f32)
    buf[...] = total
    slots = master_ref.shape[0]
    used = lax.broadcasted_iota(jnp.int32, (slots, 128), 0) < count_ref[0]
    for j in range(8):
        cols = slice(128 * j, 128 * j + 128)
        grad = buf[pl.ds(j, slots, stride=8), :]
        master = master_ref[:, cols]
        one = beta_one * one_ref[:, cols] + (1.0 - beta_one) * grad
        two = beta_two * two_ref[:, cols] + (1.0 - beta_two) * grad * grad
        unbias_one = one / (1.0 - beta_one**STEP)
        unbias_two = two / (1.0 - beta_two**STEP)
        new = master - learn_rate * (
            unbias_one / (jnp.sqrt(unbias_two) + adam_eps) + weight_decay * master
        )
        new_master[:, cols] = jnp.where(used, new, 0.0)
        new_one[:, cols] = jnp.where(used, one, 0.0)
        new_two[:, cols] = jnp.where(used, two, 0.0)


def adam(count, keep, got, master, one, two):
    out = jax.ShapeDtypeStruct(master.shape, f32)
    return pl.pallas_call(
        functools.partial(adam_kernel, len(got)),
        out_shape=(out, out, out),
        in_specs=[smem()] + [vmem()] * (4 + len(got)),
        out_specs=(vmem(), vmem(), vmem()),
        scratch_shapes=[pltpu.VMEM(keep.shape, f32)],
        name="adam",
    )(count, keep, *got, master, one, two)


def local(n_tm, n_src, feats, encoded, seg_lengths, owners, master, moment_one, moment_two, out_cot, wave_cot):
    n_dev = n_tm * n_src
    me = lax.axis_index(AXES)
    core = lax.axis_index("src")
    micro, frames, _ = feats.shape
    nb = frames // BLK
    slots = master.shape[0]

    tiles = to_tiles(master)
    own, got = gather_tiles(tiles, n_dev)

    up = [(i, i + 1) for i in range(n_dev - 1)]
    down = [(i + 1, i) for i in range(n_dev - 1)]
    before = lax.ppermute(feats[:, frames - DIL :, :], AXES, up)
    after = lax.ppermute(feats[:, :DIL, :], AXES, down)

    pair = [(2 * i + j, 2 * i + 1 - j) for i in range(n_tm) for j in range(2)]
    dw_keep = lax.dynamic_slice_in_dim(wave_cot[:, 0], core * frames, frames, axis=1)
    dw_send = lax.dynamic_slice_in_dim(wave_cot[:, 0], (1 - core) * frames, frames, axis=1)
    dw_got = lax.ppermute(dw_send, AXES, pair)
    first_core = core == 0
    dw = jnp.concatenate(
        [jnp.where(first_core, dw_keep, dw_got), jnp.where(first_core, dw_got, dw_keep)], axis=2
    )

    owner_ids = owners[:, 0]
    order = jnp.arange(NCH, dtype=jnp.int32)
    earlier = (owner_ids[:, None] == owner_ids[None, :]) & (order[None, :] < order[:, None])
    rank = jnp.sum(earlier.astype(jnp.int32), axis=1)
    pos = relative_block(owner_ids, me, n_dev) * slots + rank
    count = jnp.sum((owner_ids == me).astype(jnp.int32)).reshape(1)

    seg_order = jnp.arange(SEGS)
    bounds = jnp.sum(
        jnp.where(seg_order[:, None] >= seg_order[None, :], seg_lengths[:, None, :], 0), axis=2
    )
    def segment(block):
        return jnp.sum((block[..., None] * BLK >= bounds[:, None, None, :]).astype(jnp.int32), axis=-1)
    lane = jnp.arange(128)
    all_blocks = jnp.arange(n_dev)[:, None] * nb + (lane[None, :] // KINDS) % nb
    seg_all = segment(all_blocks[None])
    near = me * nb - 1 + jnp.arange(nb + 2)
    seg_near = segment(near[None, :, None])[:, :, 0]
    seg_near = jnp.where((near >= 0) & (near < n_dev * nb), seg_near, -1)
    lengths = jnp.sum(
        jnp.where(seg_near[:, :, None] == seg_order[None, None, :], seg_lengths[:, None, :], 0), axis=2
    )
    inverse = 1.0 / (jnp.maximum(lengths, 1).astype(f32) * HW)
    lane_micro = lane // (KINDS * nb)
    sel = jnp.where(
        (seg_all[:, None] == seg_near[:, :, None, None])
        & (lane_micro[None, None, None, :] == jnp.arange(micro)[:, None, None, None]),
        inverse[:, :, None, None],
        0.0,
    )
    same = (seg_near[:, 1:] == seg_near[:, :-1]).astype(f32)

    w_in, w_rs, w_mask, w_dec, w_dect, vec, stats = unpack(pos, own, got, feats, n_dev)
    stats1 = share_sums(stats, n_dev)
    d, stats = depth(same, stats1, sel, feats, before, after, w_in, vec)
    stats2 = share_sums(stats, n_dev)
    block_out, waves2, dn2, stats, g_rs, g_mask, g_dec, vec_a = head(
        same, stats2, sel, d, feats, encoded, out_cot, dw, w_rs, w_mask, w_dec, w_dect, vec
    )
    stats3 = share_sums(stats, n_dev)

    mine = jnp.where(first_core, waves2[:, :, :L], waves2[:, :, L:])
    other = jnp.where(first_core, waves2[:, :, L:], waves2[:, :, :L])
    theirs = lax.ppermute(other, AXES, pair)
    waves = jnp.concatenate(
        [jnp.where(first_core, mine, theirs), jnp.where(first_core, theirs, mine)], axis=1
    )[:, None]

    low, high = edges(stats2, stats3, sel, d, dn2, vec)
    prev_dd = lax.ppermute(high, AXES, up)
    next_dd = lax.ppermute(low, AXES, down)
    feats_grad, g_in, vec_b = input_grad(
        same, stats1, stats2, stats3, sel, d, dn2, prev_dd, next_dd, feats, out_cot, w_in, vec
    )

    keep, send = pack(pos, g_in, g_rs, g_mask, g_dec, vec_a, vec_b, n_dev * slots * 8)
    received = [swap(send, 1, n_dev)]
    for bits in reversed(stages(n_dev)[:-1]):
        n_next = 1 << len(bits)
        keep, *sends = fold(keep, received, n_next)
        received = [swap(s, spread(bits, k + 1), n_dev) for k, s in enumerate(sends)]
    new_master, new_one, new_two = adam(count, keep, received, master, moment_one, moment_two)
    return block_out, feats_grad, waves, new_master, new_one, new_two


def solution(mesh):
    n_tm, n_src = mesh.shape["tm"], mesh.shape["src"]
    return jax.shard_map(
        functools.partial(local, n_tm, n_src),
        mesh=mesh,
        in_specs=(
            P(None, AXES, None),
            P(None, AXES, None),
            P(),
            P(),
            P(AXES, None),
            P(AXES, None),
            P(AXES, None),
            P(None, AXES, None),
            P(None, "src", "tm", None),
        ),
        out_specs=(
            P(None, AXES, None),
            P(None, AXES, None),
            P(None, "src", "tm", None),
            P(AXES, None),
            P(AXES, None),
            P(AXES, None),
        ),
        check_vma=False,
    )
```

```python
import functools

import jax
import jax.numpy as jnp
from jax import lax
from jax.experimental import pallas as pl
from jax.experimental.pallas import tpu as pltpu
from jax.sharding import PartitionSpec as P

N = 512
L = 16
B = 128
SC = 128
HW = 512
C = 2
DIL = 128
ROW = 1024
SEGS = 8
MICRO = 4
STEP = 10
NCH = 340
BLK = 256
KINDS = 8
CHUNK = 16

norm_eps = 1e-05
adam_eps = 1e-08
beta_one = 0.9
beta_two = 0.999
learn_rate = 0.2
weight_decay = 0.01

AXES = ("tm", "src")
f32 = jnp.float32
bf16 = jnp.bfloat16
MIB = 1024 * 1024
DEPTH_MIB = HEAD_MIB = INPUT_MIB = 52

R_IN, R_RES, R_SKIP, R_MASK, R_DEC, R_VEC = 0, 512, 1024, 1536, 2560, 2688
ROWS_ALL = 2720


def mm(a, b):
    return lax.dot_general(a, b, (((1,), (0,)), ((), ())), preferred_element_type=f32)


def mm_t(a, b):
    return lax.dot_general(a, b, (((1,), (1,)), ((), ())), preferred_element_type=f32)


def mm_rows(a, b):
    return lax.dot_general(a, b, (((0,), (0,)), ((), ())), preferred_element_type=f32)


def sigmoid(v):
    return 0.5 * jnp.tanh(0.5 * v) + 0.5


def vmem():
    return pl.BlockSpec(memory_space=pltpu.VMEM)


def smem():
    return pl.BlockSpec(memory_space=pltpu.SMEM)


def stages(n_dev):
    bits = n_dev.bit_length() - 1
    groups = []
    hi = bits - 1
    while hi >= 1:
        lo = max(1, hi - 1)
        groups.append(tuple(range(lo, hi + 1)))
        hi = lo - 1
    groups.append((0,))
    return groups


def spread(bits, k):
    return sum(((k >> j) & 1) << b for j, b in enumerate(bits))


def swap(value, mask, n_dev):
    return lax.ppermute(value, AXES, [(i, i ^ mask) for i in range(n_dev)])


def gather_tiles(tiles, n_dev, *late):
    parts = [tiles]
    for bits in stages(n_dev)[:-1]:
        z = parts[0] if len(parts) == 1 else jnp.concatenate(parts, axis=0)
        parts = [z] + [swap(z, spread(bits, k), n_dev) for k in range(1, 1 << len(bits))]
    parts, late = lax.optimization_barrier((parts, late))
    return parts + [swap(z, 1, n_dev) for z in parts], late


def relative_block(owner, me, n_dev):
    q = owner ^ me
    index = jnp.zeros_like(q)
    size = 1
    for bits in stages(n_dev):
        digit = sum(((q >> b) & 1) << j for j, b in enumerate(bits))
        index = index + digit * size
        size = size << len(bits)
    return index


def share_sums(rows, n_dev):
    return lax.all_to_all(rows, AXES, 0, 0, tiled=True)


def tile_kernel(m_ref, out_ref, buf):
    slots = m_ref.shape[0]
    for j in range(8):
        buf[pl.ds(j, slots, stride=8), :] = m_ref[:, 128 * j : 128 * j + 128]
    out_ref[...] = buf[...].astype(bf16)


def to_tiles(master):
    slots = master.shape[0]
    return pl.pallas_call(
        tile_kernel,
        out_shape=jax.ShapeDtypeStruct((slots * 8, 128), bf16),
        in_specs=[vmem()],
        out_specs=vmem(),
        scratch_shapes=[pltpu.VMEM((slots * 8, 128), f32)],
        compiler_params=pltpu.CompilerParams(vmem_limit_bytes=4 * MIB),
        name="to_tiles",
    )(master)


def stat_rows(values, shape):
    lane = lax.broadcasted_iota(jnp.int32, shape, 1)
    row = jnp.zeros(shape, f32)
    for where, v in values.items():
        row = jnp.where(lane == where, v, row)
    return row


def unpack_kernel(n_parts, pos_ref, x_ref, *refs):
    parts, refs = refs[:n_parts], refs[n_parts:]
    w_in, w_rs, w_mask, w_dect, vec, stats, g, t, wd = refs
    size = parts[0].shape[0]
    for k, part in enumerate(parts):
        g[k * size : (k + 1) * size, :] = part[...].astype(f32)
    for i in range(NCH):
        start = pl.multiple_of(pos_ref[i] * 8, 8)
        t[8 * i : 8 * i + 8, :] = g[pl.ds(start, 8), :]
    for k in range(4):
        cols = slice(128 * k, 128 * k + 128)
        w_in[:, cols] = t[pl.ds(R_IN + k, 128, stride=4), :].astype(bf16)
        for c in range(C):
            w_mask[:, 512 * c + 128 * k : 512 * c + 128 * k + 128] = t[
                pl.ds(R_MASK + 512 * c + k, 128, stride=4), :
            ].astype(bf16)
        vec[:, cols] = t[pl.ds(R_VEC + k, 8, stride=4), :]
    w_rs[:, 0:128] = t[R_RES : R_RES + 512, :].astype(bf16)
    w_rs[:, 128:256] = t[R_SKIP : R_SKIP + 512, :].astype(bf16)
    part = lax.broadcasted_iota(jnp.int32, (64, 128), 1) // L
    for s in range(8):
        for c in range(C):
            rows = t[R_DEC + 64 * c : R_DEC + 64 * c + 64, :]
            rows = pltpu.roll(rows, (-L * s) % 128, 1)
            wd[pl.ds(512 * c + s, 64, stride=8), :] = jnp.where(part == 0, rows, 0.0)
    w_dect[...] = wd[...].T[0:L, :].astype(bf16)
    micro, frames, _ = x_ref.shape
    nb = frames // BLK
    sums = {}
    for m in range(micro):
        for b in range(nb):
            a = mm(x_ref[m, b * BLK : (b + 1) * BLK, :], w_in[...])
            u = a * sigmoid(a)
            first = jnp.sum(jnp.sum(u, axis=0, keepdims=True), axis=1, keepdims=True)
            second = jnp.sum(jnp.sum(u * u, axis=0, keepdims=True), axis=1, keepdims=True)
            sums[(m * nb + b) * KINDS] = first
            sums[(m * nb + b) * KINDS + 1] = second
    row = stat_rows(sums, (1, 128))
    stats[...] = jnp.broadcast_to(row[None], stats.shape)


def unpack(pos, parts, feats, n_dev):
    outs = (
        jax.ShapeDtypeStruct((B, HW), bf16),
        jax.ShapeDtypeStruct((HW, B + SC), bf16),
        jax.ShapeDtypeStruct((SC, C * N), bf16),
        jax.ShapeDtypeStruct((L, C * N), bf16),
        jax.ShapeDtypeStruct((8, HW), f32),
        jax.ShapeDtypeStruct((n_dev, 1, 128), f32),
    )
    return pl.pallas_call(
        functools.partial(unpack_kernel, len(parts)),
        out_shape=outs,
        in_specs=[smem()] + [vmem()] * (1 + len(parts)),
        out_specs=tuple(vmem() for _ in outs),
        scratch_shapes=[
            pltpu.VMEM((len(parts) * parts[0].shape[0], 128), f32),
            pltpu.VMEM((ROWS_ALL, 128), f32),
            pltpu.VMEM((C * N, 128), f32),
        ],
        compiler_params=pltpu.CompilerParams(vmem_limit_bytes=16 * MIB),
        name="unpack",
    )(pos, feats, *parts)


class Segments:
    def __init__(self, seg_ref, me_ref, m, nb, n_dev):
        bounds, total = [], 0
        for k in range(SEGS):
            total = total + seg_ref[m, k]
            bounds.append(total)
        shape = (n_dev, 128)
        lane = lax.broadcasted_iota(jnp.int32, shape, 1)
        start = (lax.broadcasted_iota(jnp.int32, shape, 0) * nb + (lane // KINDS) % nb) * BLK
        ids = jnp.where(lane // (KINDS * nb) == m, 0, SEGS + 1)
        for bound in bounds:
            ids = ids + (start >= bound).astype(jnp.int32)
        self.ids = ids
        self.here, self.inverse = [], []
        for o in range(-1, nb + 1):
            at = (me_ref[0] * nb + o) * BLK
            here, length = jnp.where(at < 0, -1, 0), 0
            for bound in bounds:
                here = here + jnp.where(at >= bound, 1, 0)
            for k in range(SEGS):
                length = length + jnp.where(here == k, seg_ref[m, k], 0)
            self.here.append(here)
            count = jnp.full((1, 1), jnp.maximum(length, 1), jnp.int32).astype(f32) * HW
            self.inverse.append(1.0 / count)
        self.same = [
            jnp.where(p == q, 1.0, 0.0).astype(f32) for p, q in zip(self.here[:-1], self.here[1:])
        ]

    def means(self, stats, kinds):
        lane = lax.broadcasted_iota(jnp.int32, (1, 128), 1) % KINDS
        rows = [
            jnp.sum(jnp.where(self.ids == here, stats, 0.0), axis=0, keepdims=True) * inverse
            for here, inverse in zip(self.here, self.inverse)
        ]
        t = jnp.concatenate(rows, axis=0)
        cols = [jnp.sum(jnp.where(lane == k, t, 0.0), axis=1, keepdims=True) for k in range(kinds)]
        return [[c[o : o + 1, :] for o in range(len(rows))] for c in cols]

    def norm(self, stats):
        mean, second = self.means(stats, 2)
        return mean, [lax.rsqrt(q - p * p + norm_eps) for p, q in zip(mean, second)]

    def taps(self, vec, h):
        k0, k2 = vec[4:5, :], vec[6:7, :]
        lo = k0 * self.same[h // 2 - 1] if h % 2 == 0 else k0
        hi = k2 if h % 2 == 0 else k2 * self.same[h // 2]
        return lo, hi


def depth_kernel(
    me_ref, seg_ref, stats_ref, x_ref, near_ref, far_ref, w_in, vec, d_ref, edge_ref, out_stats, acc
):
    m = pl.program_id(0)
    frames = x_ref.shape[1]
    nb = frames // BLK
    seg = Segments(seg_ref, me_ref, m, nb, stats_ref.shape[0])
    means, factors = seg.norm(stats_ref[:, 0, :])
    g1, b1 = 1.0 + vec[0:1, :], vec[1:2, :]

    def normed(x, o):
        a = mm(x, w_in[...])
        u = a * sigmoid(a)
        scale = factors[o] * g1
        return (u * scale + (b1 - means[o] * scale)).astype(bf16).astype(f32)

    even = me_ref[0] % 2 == 0
    n1 = []
    for h in range(2 * nb + 4):
        if h < 2:
            rows = slice(h * DIL, (h + 1) * DIL)
            x = jnp.where(even, far_ref[0, rows, :], near_ref[0, rows, :])
        elif h < 2 * nb + 2:
            x = x_ref[0, (h - 2) * DIL : (h - 1) * DIL, :]
        else:
            rows = slice((h - 2 * nb - 2) * DIL, (h - 2 * nb - 1) * DIL)
            x = jnp.where(even, near_ref[0, rows, :], far_ref[0, rows, :])
        n1.append(normed(x, h // 2))
    k1, kb = vec[5:6, :], vec[7:8, :]

    def conv(h):
        lo, hi = seg.taps(vec, h)
        return lo * n1[h - 1] + k1 * n1[h] + hi * n1[h + 1] + kb

    edge_ref[0, 0:DIL, :] = conv(1)
    edge_ref[0, DIL : 2 * DIL, :] = conv(2 * nb + 2)
    lane = lax.broadcasted_iota(jnp.int32, (1, 128), 1)
    row = jnp.where(m == 0, jnp.zeros((1, 128), f32), acc[...])
    for b in range(nb):
        first, second = 0.0, 0.0
        for h in (2 * b, 2 * b + 1):
            d = conv(h + 2)
            d_ref[0, h * DIL : (h + 1) * DIL, :] = d
            v = d * sigmoid(d)
            first = first + jnp.sum(v, axis=0, keepdims=True)
            second = second + jnp.sum(v * v, axis=0, keepdims=True)
        at = (m * nb + b) * KINDS
        row = jnp.where(lane == at, jnp.sum(first, axis=1, keepdims=True), row)
        row = jnp.where(lane == at + 1, jnp.sum(second, axis=1, keepdims=True), row)
    acc[...] = row
    out_stats[...] = jnp.broadcast_to(row[None], out_stats.shape)


def per_micro(shape):
    rest = tuple(shape[1:])
    zeros = (0,) * len(rest)
    return pl.BlockSpec((1,) + rest, lambda m: (m,) + zeros)


def whole(shape):
    zeros = (0,) * len(shape)
    return pl.BlockSpec(tuple(shape), lambda m: zeros)


def depth(me, lengths, stats, feats, near, far, w_in, vec):
    micro, frames, _ = feats.shape
    return pl.pallas_call(
        depth_kernel,
        grid=(micro,),
        out_shape=(
            jax.ShapeDtypeStruct((micro, frames, HW), f32),
            jax.ShapeDtypeStruct((micro, 2 * DIL, HW), f32),
            jax.ShapeDtypeStruct(stats.shape, f32),
        ),
        in_specs=[
            smem(),
            smem(),
            whole(stats.shape),
            per_micro(feats.shape),
            pl.BlockSpec((1, BLK, B), lambda m: (m, 0, 0)),
            pl.BlockSpec((1, BLK, B), lambda m: (m, 0, 0)),
            whole(w_in.shape),
            whole(vec.shape),
        ],
        out_specs=(
            per_micro((micro, frames, HW)),
            per_micro((micro, 2 * DIL, HW)),
            whole(stats.shape),
        ),
        scratch_shapes=[pltpu.VMEM((1, 128), f32)],
        compiler_params=pltpu.CompilerParams(vmem_limit_bytes=DEPTH_MIB * MIB),
        name="depth",
    )(me, lengths, stats, feats, near, far, w_in, vec)


def fold_rows(v):
    return functools.reduce(lambda p, q: p + q, [v[i : i + 8, :] for i in range(0, v.shape[0], 8)])


def head_kernel(
    me_ref,
    seg_ref,
    stats_ref,
    d_ref,
    x_ref,
    enc_ref,
    dy_ref,
    own_ref,
    other_ref,
    w_rs,
    w_mask,
    w_dect,
    vec,
    block_ref,
    wave_own_ref,
    wave_other_ref,
    ds_ref,
    out_stats,
    g_rs,
    g_mask,
    g_dec,
    g_vec,
    acc,
    n2_s,
    v_s,
    sd_s,
    q_s,
    gm_s,
    e_s,
    dq_s,
    dn2_s,
):
    m = pl.program_id(0)
    frames = d_ref.shape[1]
    nb = frames // BLK

    @pl.when(m == 0)
    def _():
        g_rs[...] = jnp.zeros_like(g_rs)
        g_mask[...] = jnp.zeros_like(g_mask)
        g_dec[...] = jnp.zeros_like(g_dec)
        g_vec[...] = jnp.zeros_like(g_vec)
        acc[...] = jnp.zeros_like(acc)

    core = me_ref[0] % 2
    seg = Segments(seg_ref, me_ref, m, nb, stats_ref.shape[0])
    means, factors = seg.norm(stats_ref[:, 0, :])
    g1, g2, b1, b2 = 1.0 + vec[0:1, :], 1.0 + vec[2:3, :], vec[1:2, :], vec[3:4, :]
    k1, kb = vec[5:6, :], vec[7:8, :]
    lane = lax.broadcasted_iota(jnp.int32, (1, 128), 1)
    scales = [factors[1 + b] * g2 for b in range(nb)]
    zero = jnp.zeros((8, HW), f32)

    sums = []
    for h in range(2 * nb):
        scale = scales[h // 2]
        shift = b2 - means[1 + h // 2] * scale
        s0 = s1 = c0 = c1 = zero
        for r in range(h * DIL, (h + 1) * DIL, CHUNK):
            rows = slice(r, r + CHUNK)
            d = d_ref[0, rows, :]
            sig = sigmoid(d)
            v = d * sig
            sd = sig + v * (1.0 - sig)
            n2_s[rows, :] = (v * scale + shift).astype(bf16)
            v_s[rows, :] = v
            sd_s[rows, :] = sd
            cv = v * sd
            s0 = s0 + fold_rows(sd)
            s1 = s1 + fold_rows(sd * d)
            c0 = c0 + fold_rows(cv)
            c1 = c1 + fold_rows(cv * d)
        sums.append((s0, s1, c0, c1))

    n2 = n2_s[...]
    ys = mm(n2, w_rs[...])
    block_ref[0] = (x_ref[0].astype(f32) + ys[:, 0:B]).astype(bf16)
    s = ys[:, B : B + SC]
    sg = sigmoid(s)
    z = (s * sg).astype(bf16)
    slope = sg * (1.0 + s * (1.0 - sg))
    dz = jnp.zeros((frames, SC), f32)
    for k, (c, dw_ref, wave_ref) in enumerate(
        ((core, own_ref, wave_own_ref), (1 - core, other_ref, wave_other_ref))
    ):
        cols = pl.ds(pl.multiple_of(c * N, N), N)
        dw = dw_ref[0]
        q_s[k] = mm(z, w_mask[:, cols])
        gm_s[k] = mm_rows(dw, w_dect[:, cols])
        for r in range(0, frames, CHUNK):
            rows = slice(r, r + CHUNK)
            p = sigmoid(q_s[k, rows, :])
            pe = p * enc_ref[0, rows, :].astype(f32)
            e_s[k, rows, :] = pe.astype(bf16)
            dq_s[k, rows, :] = (gm_s[k, rows, :] * (pe - pe * p)).astype(bf16)
        e = e_s[k]
        dq = dq_s[k]
        wave_ref[0] = mm_t(w_dect[:, cols], e).astype(bf16)
        dz = dz + mm_t(dq, w_mask[:, cols])
        g_dec[:, cols] += mm(dw, e)
        g_mask[:, cols] += mm_rows(z, dq)
    ds = (dz * slope).astype(bf16)
    ds_ref[0] = ds
    dys = jnp.concatenate([dy_ref[0], ds], axis=1)
    g_rs[...] += mm_rows(dys, n2)
    dn2_s[...] = mm_t(dys, w_rs[...])

    row = acc[...]
    for b in range(nb):
        mean, factor, scale = means[1 + b], factors[1 + b], scales[b]
        sum_d = sum_dv = zero
        six = [jnp.zeros((1, HW), f32)] * 6
        for h in (2 * b, 2 * b + 1):
            a0 = a1 = zero
            for r in range(h * DIL, (h + 1) * DIL, CHUNK):
                rows = slice(r, r + CHUNK)
                dn2 = dn2_s[rows, :]
                a = dn2 * sd_s[rows, :]
                sum_d = sum_d + fold_rows(dn2)
                sum_dv = sum_dv + fold_rows(dn2 * v_s[rows, :])
                a0 = a0 + fold_rows(a)
                a1 = a1 + fold_rows(a * d_ref[0, rows, :])
            a0, a1, s0, s1, c0, c1 = [
                jnp.sum(p, axis=0, keepdims=True) for p in (a0, a1) + sums[h]
            ]
            lo, hi = seg.taps(vec, h + 2)
            kappa = k1 + lo + hi
            vw = g1 * kappa
            delta = kb + b1 * kappa
            a0, a1 = a0 * scale, a1 * scale
            s0, s1 = s0 * factor, s1 * factor
            c0 = c0 * factor * factor - mean * factor * s0
            c1 = c1 * factor * factor - mean * factor * s1
            new = [vw * a0, vw * s0, vw * c0, a1 - delta * a0, s1 - delta * s0, c1 - delta * c0]
            six = [p0 + p1 for p0, p1 in zip(six, new)]
        sum_d = jnp.sum(sum_d, axis=0, keepdims=True)
        gain = (jnp.sum(sum_dv, axis=0, keepdims=True) - mean * sum_d) * factor
        g_vec[2:3, :] += gain
        g_vec[3:4, :] += sum_d
        for k, val in enumerate([sum_d * g2, gain * g2] + six):
            at = (m * nb + b) * KINDS + k
            row = jnp.where(lane == at, jnp.sum(val, axis=1, keepdims=True), row)
    acc[...] = row
    out_stats[...] = jnp.broadcast_to(row[None], out_stats.shape)


def head(me, lengths, stats, d, feats, enc, dy, own, other, w_rs, w_mask, w_dect, vec):
    micro, frames, _ = feats.shape
    outs = (
        (feats.shape, bf16, True),
        ((micro, L, frames), bf16, True),
        ((micro, L, frames), bf16, True),
        ((micro, frames, SC), bf16, True),
        (stats.shape, f32, False),
        ((B + SC, HW), f32, False),
        ((SC, C * N), f32, False),
        ((L, C * N), f32, False),
        ((8, HW), f32, False),
    )

    def each(shape):
        zeros = (0,) * (len(shape) - 1)
        return pl.BlockSpec((1,) + tuple(shape[1:]), lambda m, me_ref: (m,) + zeros)

    def once(shape):
        zeros = (0,) * len(shape)
        return pl.BlockSpec(tuple(shape), lambda m, me_ref: zeros)

    ours = pl.BlockSpec((1, L, frames), lambda m, me_ref: (m, 0, me_ref[0] % 2))
    return pl.pallas_call(
        head_kernel,
        grid_spec=pltpu.PrefetchScalarGridSpec(
            num_scalar_prefetch=1,
            grid=(micro,),
            in_specs=[
                smem(),
                once(stats.shape),
                each(d.shape),
                each(feats.shape),
                each(enc.shape),
                each(dy.shape),
                ours,
                ours,
                once(w_rs.shape),
                once(w_mask.shape),
                once(w_dect.shape),
                once(vec.shape),
            ],
            out_specs=tuple(each(s) if per else once(s) for s, _, per in outs),
            scratch_shapes=[
                pltpu.VMEM((1, 128), f32),
                pltpu.VMEM((frames, HW), bf16),
                pltpu.VMEM((frames, HW), f32),
                pltpu.VMEM((frames, HW), f32),
                pltpu.VMEM((C, frames, N), f32),
                pltpu.VMEM((C, frames, N), f32),
                pltpu.VMEM((C, frames, N), bf16),
                pltpu.VMEM((C, frames, N), bf16),
                pltpu.VMEM((frames, HW), f32),
            ],
        ),
        out_shape=tuple(jax.ShapeDtypeStruct(s, t) for s, t, _ in outs),
        compiler_params=pltpu.CompilerParams(vmem_limit_bytes=HEAD_MIB * MIB),
        name="head",
    )(me, lengths, stats, d, feats, enc, dy, own, other, w_rs, w_mask, w_dect, vec)


def back_means(seg, stats):
    v = seg.means(stats, KINDS)
    p2, q2 = v[0], v[1]
    p1 = [a - p * b - q * c for a, p, b, q, c in zip(v[2], p2, v[3], q2, v[4])]
    q1 = [a - p * b - q * c for a, p, b, q, c in zip(v[5], p2, v[6], q2, v[7])]
    return p2, q2, p1, q1


def depth_grad(d, dn2, mean, factor, g2, p2, q2):
    sig = sigmoid(d)
    v = d * sig
    sd = sig + v * (1.0 - sig)
    scale = factor * g2
    slope = factor * factor * q2
    shift = factor * p2 - slope * mean
    return (sd * (dn2 * scale - v * slope - shift)).astype(bf16)


def input_kernel(
    me_ref,
    seg_ref,
    stats1_ref,
    stats2_ref,
    stats3_ref,
    d_ref,
    edge_ref,
    x_ref,
    dy_ref,
    dy_near,
    dy_far,
    ds_ref,
    ds_near,
    ds_far,
    w_in,
    w_rs,
    vec,
    feats_ref,
    g_in,
    g_vec,
):
    m = pl.program_id(0)
    frames = d_ref.shape[1]
    nb = frames // BLK

    @pl.when(m == 0)
    def _():
        g_in[...] = jnp.zeros_like(g_in)
        g_vec[...] = jnp.zeros_like(g_vec)

    seg = Segments(seg_ref, me_ref, m, nb, stats1_ref.shape[0])
    mean1, factor1 = seg.norm(stats1_ref[:, 0, :])
    mean2, factor2 = seg.norm(stats2_ref[:, 0, :])
    p2, q2, p1, q1 = back_means(seg, stats3_ref[:, 0, :])
    g1, g2, b1 = 1.0 + vec[0:1, :], 1.0 + vec[2:3, :], vec[1:2, :]
    k0, k1, k2 = vec[4:5, :], vec[5:6, :], vec[6:7, :]
    even = me_ref[0] % 2 == 0
    dd = []
    for h in range(1, 2 * nb + 3):
        o = h // 2
        if h == 1:
            d = edge_ref[0, 0:DIL, :]
            dy = jnp.where(even, dy_far[0], dy_near[0])
            ds = jnp.where(even, ds_far[0], ds_near[0])
        elif h == 2 * nb + 2:
            d = edge_ref[0, DIL : 2 * DIL, :]
            dy = jnp.where(even, dy_near[0], dy_far[0])
            ds = jnp.where(even, ds_near[0], ds_far[0])
        else:
            rows = slice((h - 2) * DIL, (h - 1) * DIL)
            d, dy, ds = d_ref[0, rows, :], dy_ref[0, rows, :], ds_ref[0, rows, :]
        dn2 = mm_t(jnp.concatenate([dy, ds], axis=1), w_rs[...])
        dd.append(depth_grad(d, dn2, mean2[o], factor2[o], g2, p2[o], q2[o]).astype(f32))
    zero = jnp.zeros((1, HW), f32)
    t0, t1, t2, tb, gg, gb = zero, zero, zero, zero, zero, zero
    for h in range(2 * nb):
        o = h // 2 + 1
        rows = slice(h * DIL, (h + 1) * DIL)
        x = x_ref[0, rows, :]
        a = mm(x, w_in[...])
        sig = sigmoid(a)
        u = a * sig
        mean, factor = mean1[o], factor1[o]
        scale = factor * g1
        n1 = (u * scale + (b1 - mean * scale)).astype(bf16).astype(f32)
        lo = seg.same[o - 1] if h % 2 == 0 else 1.0
        hi = 1.0 if h % 2 == 0 else seg.same[o]
        here, prev, nxt = dd[h + 1], dd[h], dd[h + 2]
        t0 = t0 + jnp.sum(nxt * n1, axis=0, keepdims=True) * hi
        t1 = t1 + jnp.sum(here * n1, axis=0, keepdims=True)
        t2 = t2 + jnp.sum(prev * n1, axis=0, keepdims=True) * lo
        tb = tb + jnp.sum(here, axis=0, keepdims=True)
        dn1 = k1 * here + (k0 * hi) * nxt + (k2 * lo) * prev
        h1 = (u - mean) * factor
        gg = gg + jnp.sum(dn1 * h1, axis=0, keepdims=True)
        gb = gb + jnp.sum(dn1, axis=0, keepdims=True)
        du = factor * (dn1 * g1 - p1[o] - h1 * q1[o])
        da = (du * (sig + u * (1.0 - sig))).astype(bf16)
        g_in[...] += mm_rows(x, da)
        feats_ref[0, rows, :] = (dy_ref[0, rows, :].astype(f32) + mm_t(da, w_in[...])).astype(bf16)
    for r, val in ((0, gg), (1, gb), (4, t0), (5, t1), (6, t2), (7, tb)):
        g_vec[r : r + 1, :] += val


def input_grad(me, lengths, stats, d, edge, feats, dy, near, far, ds, ds_near, ds_far, w_in, w_rs, vec):
    micro, frames, _ = d.shape
    halo = pl.BlockSpec((1, DIL, B), lambda m: (m, BLK // DIL, 0))
    return pl.pallas_call(
        input_kernel,
        grid=(micro,),
        out_shape=(
            jax.ShapeDtypeStruct(feats.shape, bf16),
            jax.ShapeDtypeStruct((B, HW), f32),
            jax.ShapeDtypeStruct((8, HW), f32),
        ),
        in_specs=[smem(), smem()]
        + [whole(s.shape) for s in stats]
        + [per_micro(v.shape) for v in (d, edge, feats, dy)]
        + [halo, halo]
        + [per_micro(v.shape) for v in (ds, ds_near, ds_far)]
        + [whole(w.shape) for w in (w_in, w_rs, vec)],
        out_specs=(per_micro(feats.shape), whole((B, HW)), whole((8, HW))),
        compiler_params=pltpu.CompilerParams(vmem_limit_bytes=INPUT_MIB * MIB),
        name="input_grad",
    )(me, lengths, *stats, d, edge, feats, dy, near, far, ds, ds_near, ds_far, w_in, w_rs, vec)


def pack_kernel(pos_ref, g_in, g_rs, g_mask, g_dec, vec_a, vec_b, keep_ref, send_ref, t, out, wd):
    for k in range(4):
        cols = slice(128 * k, 128 * k + 128)
        t[pl.ds(R_IN + k, 128, stride=4), :] = g_in[:, cols]
        for c in range(C):
            t[pl.ds(R_MASK + 512 * c + k, 128, stride=4), :] = g_mask[
                :, 512 * c + 128 * k : 512 * c + 128 * k + 128
            ]
        t[pl.ds(R_VEC + k, 8, stride=4), :] = vec_a[:, cols] + vec_b[:, cols]
    t[R_RES : R_RES + 512, :] = g_rs[0:128, :].T
    t[R_SKIP : R_SKIP + 512, :] = g_rs[128:256, :].T
    wd[...] = jnp.concatenate([g_dec[...], jnp.zeros((128 - L, C * N), f32)], axis=0).T
    part = lax.broadcasted_iota(jnp.int32, (64, 128), 1) // L
    for c in range(C):
        rows = jnp.zeros((64, 128), f32)
        for s in range(8):
            piece = pltpu.roll(wd[pl.ds(512 * c + s, 64, stride=8), :], L * s, 1)
            rows = jnp.where(part == s, piece, rows)
        t[R_DEC + 64 * c : R_DEC + 64 * c + 64, :] = rows
    out[...] = jnp.zeros_like(out)
    for i in range(NCH):
        start = pl.multiple_of(pos_ref[i] * 8, 8)
        out[pl.ds(start, 8), :] = t[8 * i : 8 * i + 8, :]
    half = keep_ref.shape[0]
    keep_ref[...] = out[0:half, :]
    send_ref[...] = out[half : 2 * half, :].astype(bf16)


def pack(pos, g_in, g_rs, g_mask, g_dec, vec_a, vec_b, rows):
    return pl.pallas_call(
        pack_kernel,
        out_shape=(
            jax.ShapeDtypeStruct((rows // 2, 128), f32),
            jax.ShapeDtypeStruct((rows // 2, 128), bf16),
        ),
        in_specs=[smem()] + [vmem()] * 6,
        out_specs=(vmem(), vmem()),
        scratch_shapes=[
            pltpu.VMEM((ROWS_ALL, 128), f32),
            pltpu.VMEM((rows, 128), f32),
            pltpu.VMEM((C * N, 128), f32),
        ],
        compiler_params=pltpu.CompilerParams(vmem_limit_bytes=16 * MIB),
        name="pack",
    )(pos, g_in, g_rs, g_mask, g_dec, vec_a, vec_b)


def fold_kernel(n_got, n_next, *refs):
    keep_ref, got = refs[0], refs[1 : 1 + n_got]
    outs = refs[1 + n_got :]
    total = keep_ref[...]
    for g in got:
        total = total + g[...].astype(f32)
    size = total.shape[0] // n_next
    outs[0][...] = total[0:size, :]
    for q in range(1, n_next):
        outs[q][...] = total[q * size : (q + 1) * size, :].astype(bf16)


def fold(keep, got, n_next):
    size = keep.shape[0] // n_next
    outs = [jax.ShapeDtypeStruct((size, 128), f32)]
    outs += [jax.ShapeDtypeStruct((size, 128), bf16)] * (n_next - 1)
    return pl.pallas_call(
        functools.partial(fold_kernel, len(got), n_next),
        out_shape=tuple(outs),
        in_specs=[vmem()] * (1 + len(got)),
        out_specs=tuple(vmem() for _ in outs),
        compiler_params=pltpu.CompilerParams(vmem_limit_bytes=8 * MIB),
        name="fold",
    )(keep, *got)


def adam_kernel(n_got, count_ref, *refs):
    keep_ref, got = refs[0], refs[1 : 1 + n_got]
    master_ref, one_ref, two_ref, new_master, new_one, new_two, buf = refs[1 + n_got :]
    total = keep_ref[...]
    for g in got:
        total = total + g[...].astype(f32)
    buf[...] = total
    slots = master_ref.shape[0]
    used = lax.broadcasted_iota(jnp.int32, (slots, 128), 0) < count_ref[0]
    for j in range(8):
        cols = slice(128 * j, 128 * j + 128)
        grad = buf[pl.ds(j, slots, stride=8), :]
        master = master_ref[:, cols]
        one = beta_one * one_ref[:, cols] + (1.0 - beta_one) * grad
        two = beta_two * two_ref[:, cols] + (1.0 - beta_two) * grad * grad
        unbias_one = one / (1.0 - beta_one**STEP)
        unbias_two = two / (1.0 - beta_two**STEP)
        new = master - learn_rate * (
            unbias_one / (jnp.sqrt(unbias_two) + adam_eps) + weight_decay * master
        )
        new_master[:, cols] = jnp.where(used, new, 0.0)
        new_one[:, cols] = jnp.where(used, one, 0.0)
        new_two[:, cols] = jnp.where(used, two, 0.0)


def adam(count, keep, got, master, one, two):
    out = jax.ShapeDtypeStruct(master.shape, f32)
    return pl.pallas_call(
        functools.partial(adam_kernel, len(got)),
        out_shape=(out, out, out),
        in_specs=[smem()] + [vmem()] * (4 + len(got)),
        out_specs=(vmem(), vmem(), vmem()),
        scratch_shapes=[pltpu.VMEM(keep.shape, f32)],
        compiler_params=pltpu.CompilerParams(vmem_limit_bytes=4 * MIB),
        name="adam",
    )(count, keep, *got, master, one, two)


def local(n_tm, n_src, feats, encoded, seg_lengths, owners, master, moment_one, moment_two, out_cot, wave_cot):
    n_dev = n_tm * n_src
    me = lax.axis_index(AXES)
    core = lax.axis_index("src")
    micro, frames, _ = feats.shape
    nb = frames // BLK
    slots = master.shape[0]


    across = [(i, i + 1) for i in range(1, n_dev - 1, 2)]
    across = across + [(j, i) for i, j in across]

    def ends(at_end, *arrays):
        size = [jnp.where(at_end, v.shape[1] - w, 0) for v, w in arrays]
        rows = [lax.dynamic_slice_in_dim(v, at, w, axis=1) for (v, w), at in zip(arrays, size)]
        return rows[0] if len(rows) == 1 else jnp.concatenate(rows, axis=1)

    cot = jnp.transpose(wave_cot[:, 0], (0, 2, 1))
    halo = (feats, BLK), (out_cot, DIL)
    parts, (near, far, cot_other) = gather_tiles(
        to_tiles(master), n_dev, ends(core == 0, *halo), ends(core == 1, *halo), cot
    )
    near = swap(near, 1, n_dev)
    far = lax.ppermute(far, AXES, across)
    cot_other = swap(cot_other, 1, n_dev)

    owner_ids = owners[:, 0]
    order = jnp.arange(NCH, dtype=jnp.int32)
    earlier = (owner_ids[:, None] == owner_ids[None, :]) & (order[None, :] < order[:, None])
    rank = jnp.sum(earlier.astype(jnp.int32), axis=1)
    pos = relative_block(owner_ids, me, n_dev) * slots + rank
    count = jnp.sum((owner_ids == me).astype(jnp.int32)).reshape(1)
    here = me.astype(jnp.int32).reshape(1)

    w_in, w_rs, w_mask, w_dect, vec, stats = unpack(pos, parts, feats, n_dev)
    stats1 = share_sums(stats, n_dev)
    d, edge, stats = depth(here, seg_lengths, stats1, feats, near, far, w_in, vec)
    stats2 = share_sums(stats, n_dev)
    block_out, wave_own, wave_other, ds, stats, g_rs, g_mask, g_dec, vec_a = head(
        here, seg_lengths, stats2, d, feats, encoded, out_cot, cot, cot_other, w_rs, w_mask, w_dect, vec
    )
    stats3 = share_sums(stats, n_dev)
    ds_near = swap(ends(core == 0, (ds, DIL)), 1, n_dev)
    ds_far = lax.ppermute(ends(core == 1, (ds, DIL)), AXES, across)

    wave_got = swap(wave_other, 1, n_dev)
    waves = jnp.concatenate(
        [jnp.where(core == 0, wave_own, wave_got), jnp.where(core == 0, wave_got, wave_own)], axis=2
    )
    waves = jnp.transpose(waves, (0, 2, 1))[:, None]

    feats_grad, g_in, vec_b = input_grad(
        here, seg_lengths, (stats1, stats2, stats3), d, edge, feats, out_cot, near, far, ds, ds_near, ds_far, w_in, w_rs, vec
    )

    keep, send = pack(pos, g_in, g_rs, g_mask, g_dec, vec_a, vec_b, n_dev * slots * 8)
    received = [swap(send, 1, n_dev)]
    for bits in reversed(stages(n_dev)[:-1]):
        n_next = 1 << len(bits)
        keep, *sends = fold(keep, received, n_next)
        received = [swap(s, spread(bits, k + 1), n_dev) for k, s in enumerate(sends)]
    new_master, new_one, new_two = adam(count, keep, received, master, moment_one, moment_two)
    return block_out, feats_grad, waves, new_master, new_one, new_two


def solution(mesh):
    n_tm, n_src = mesh.shape["tm"], mesh.shape["src"]
    return jax.shard_map(
        functools.partial(local, n_tm, n_src),
        mesh=mesh,
        in_specs=(
            P(None, AXES, None),
            P(None, AXES, None),
            P(),
            P(),
            P(AXES, None),
            P(AXES, None),
            P(AXES, None),
            P(None, AXES, None),
            P(None, "src", "tm", None),
        ),
        out_specs=(
            P(None, AXES, None),
            P(None, AXES, None),
            P(None, "src", "tm", None),
            P(AXES, None),
            P(AXES, None),
            P(AXES, None),
        ),
        check_vma=False,
    )
```

```python
import functools

import jax
import jax.numpy as jnp
from jax import lax
from jax.experimental import pallas as pl
from jax.experimental.pallas import tpu as pltpu
from jax.sharding import PartitionSpec as P

N = 512
L = 16
B = 128
SC = 128
HW = 512
C = 2
DIL = 128
ROW = 1024
SEGS = 8
MICRO = 4
STEP = 10
NCH = 340
BLK = 256
KINDS = 8
CHUNK = 16
LANES, ROWS = 256, 16
HALF_W = 256

norm_eps = 1e-05
adam_eps = 1e-08
beta_one = 0.9
beta_two = 0.999
learn_rate = 0.2
weight_decay = 0.01

AXES = ("tm", "src")
f32 = jnp.float32
bf16 = jnp.bfloat16
MIB = 1024 * 1024
DEPTH_MIB = HEAD_MIB = INPUT_MIB = 20

R_IN, R_RES, R_SKIP, R_MASK, R_DEC, R_VEC = 0, 512, 1024, 1536, 2560, 2688
ROWS_ALL = 2720


def mm(a, b):
    return lax.dot_general(a, b, (((1,), (0,)), ((), ())), preferred_element_type=f32)


def mm_t(a, b):
    return lax.dot_general(a, b, (((1,), (1,)), ((), ())), preferred_element_type=f32)


def mm_rows(a, b):
    return lax.dot_general(a, b, (((0,), (0,)), ((), ())), preferred_element_type=f32)


def sigmoid(v):
    return 0.5 * jnp.tanh(0.5 * v) + 0.5


def fold_rows(v):
    return functools.reduce(lambda p, q: p + q, [v[i : i + 8, :] for i in range(0, v.shape[0], 8)])


def slope_parts(half, t):
    w = half * t
    return half + w, (1.0 + t) + (half - w * t)


def weave(first, second):
    steps = [((i + 0.5) / len(first), 0, i) for i in range(len(first))]
    steps += [((i + 0.5) / len(second), 1, i) for i in range(len(second))]
    for _, which, i in sorted(steps):
        (first, second)[which][i]()


def run(steps):
    for step in steps:
        step()


def tiles_of(halves):
    return [(h, slice(c, c + LANES)) for h in halves for c in range(0, HW, LANES)]


def loop(count, body, carry):
    def pair(i, carry):
        return body(2 * i + 1, 1, body(2 * i, 0, carry))

    return lax.fori_loop(0, count // 2, pair, carry)


def row_sum(v):
    return jnp.sum(v, axis=0, keepdims=True)


def vmem():
    return pl.BlockSpec(memory_space=pltpu.VMEM)


def smem():
    return pl.BlockSpec(memory_space=pltpu.SMEM)


def stages(n_dev):
    bits = n_dev.bit_length() - 1
    groups = []
    hi = bits - 1
    while hi >= 1:
        lo = max(1, hi - 1)
        groups.append(tuple(range(lo, hi + 1)))
        hi = lo - 1
    groups.append((0,))
    return groups


def spread(bits, k):
    return sum(((k >> j) & 1) << b for j, b in enumerate(bits))


def swap(value, mask, n_dev):
    return lax.ppermute(value, AXES, [(i, i ^ mask) for i in range(n_dev)])


def gather_tiles(tiles, n_dev, early, late):
    parts = [tiles]
    for k, bits in enumerate(stages(n_dev)[:-1]):
        if k == 1:
            parts, early = lax.optimization_barrier((parts, early))
        z = parts[0] if len(parts) == 1 else jnp.concatenate(parts, axis=0)
        parts = [z] + [swap(z, spread(bits, q), n_dev) for q in range(1, 1 << len(bits))]
    parts, late = lax.optimization_barrier((parts, late))
    return parts + [swap(z, 1, n_dev) for z in parts], early, late


def relative_block(owner, me, n_dev):
    q = owner ^ me
    index = jnp.zeros_like(q)
    size = 1
    for bits in stages(n_dev):
        digit = sum(((q >> b) & 1) << j for j, b in enumerate(bits))
        index = index + digit * size
        size = size << len(bits)
    return index


def share_sums(rows, n_dev):
    return lax.all_to_all(rows, AXES, 0, 0, tiled=True)


def tile_kernel(m_ref, out_ref, buf):
    slots = m_ref.shape[0]
    for j in range(8):
        buf[pl.ds(j, slots, stride=8), :] = m_ref[:, 128 * j : 128 * j + 128]
    out_ref[...] = buf[...].astype(bf16)


def to_tiles(master):
    slots = master.shape[0]
    return pl.pallas_call(
        tile_kernel,
        out_shape=jax.ShapeDtypeStruct((slots * 8, 128), bf16),
        in_specs=[vmem()],
        out_specs=vmem(),
        scratch_shapes=[pltpu.VMEM((slots * 8, 128), f32)],
        compiler_params=pltpu.CompilerParams(vmem_limit_bytes=4 * MIB),
        name="to_tiles",
    )(master)


def stat_rows(values, shape):
    lane = lax.broadcasted_iota(jnp.int32, shape, 1)
    row = jnp.zeros(shape, f32)
    for where, v in values.items():
        row = jnp.where(lane == where, v, row)
    return row


def unpack_kernel(n_parts, pos_ref, x_ref, *refs):
    parts, refs = refs[:n_parts], refs[n_parts:]
    w_in, w_rs, w_mask, w_dect, vec, stats, g, t, wd = refs
    size = parts[0].shape[0]
    for k, part in enumerate(parts):
        g[k * size : (k + 1) * size, :] = part[...].astype(f32)
    for i in range(NCH):
        start = pl.multiple_of(pos_ref[i] * 8, 8)
        t[8 * i : 8 * i + 8, :] = g[pl.ds(start, 8), :]
    for k in range(4):
        cols = slice(128 * k, 128 * k + 128)
        w_in[:, cols] = (0.5 * t[pl.ds(R_IN + k, 128, stride=4), :]).astype(bf16)
        for c in range(C):
            w_mask[:, 512 * c + 128 * k : 512 * c + 128 * k + 128] = (
                0.5 * t[pl.ds(R_MASK + 512 * c + k, 128, stride=4), :]
            ).astype(bf16)
        vec[:, cols] = t[pl.ds(R_VEC + k, 8, stride=4), :]
    w_rs[:, 0:128] = t[R_RES : R_RES + 512, :].astype(bf16)
    w_rs[:, 128:256] = t[R_SKIP : R_SKIP + 512, :].astype(bf16)
    part = lax.broadcasted_iota(jnp.int32, (64, 128), 1) // L
    for s in range(8):
        for c in range(C):
            rows = t[R_DEC + 64 * c : R_DEC + 64 * c + 64, :]
            rows = pltpu.roll(rows, (-L * s) % 128, 1)
            wd[pl.ds(512 * c + s, 64, stride=8), :] = jnp.where(part == 0, rows, 0.0)
    w_dect[...] = (0.5 * wd[...].T[0:L, :]).astype(bf16)
    micro, frames, _ = x_ref.shape
    nb = frames // BLK
    sums = {}
    for m in range(micro):
        for b in range(nb):
            half = mm(x_ref[m, b * BLK : (b + 1) * BLK, :], w_in[...])
            u = half + half * jnp.tanh(half)
            first = jnp.sum(jnp.sum(u, axis=0, keepdims=True), axis=1, keepdims=True)
            second = jnp.sum(jnp.sum(u * u, axis=0, keepdims=True), axis=1, keepdims=True)
            sums[(m * nb + b) * KINDS] = first
            sums[(m * nb + b) * KINDS + 1] = second
    row = stat_rows(sums, (1, 128))
    stats[...] = jnp.broadcast_to(row[None], stats.shape)


def unpack(pos, parts, feats, n_dev):
    outs = (
        jax.ShapeDtypeStruct((B, HW), bf16),
        jax.ShapeDtypeStruct((HW, B + SC), bf16),
        jax.ShapeDtypeStruct((SC, C * N), bf16),
        jax.ShapeDtypeStruct((L, C * N), bf16),
        jax.ShapeDtypeStruct((8, HW), f32),
        jax.ShapeDtypeStruct((n_dev, 1, 128), f32),
    )
    return pl.pallas_call(
        functools.partial(unpack_kernel, len(parts)),
        out_shape=outs,
        in_specs=[smem()] + [vmem()] * (1 + len(parts)),
        out_specs=tuple(vmem() for _ in outs),
        scratch_shapes=[
            pltpu.VMEM((len(parts) * parts[0].shape[0], 128), f32),
            pltpu.VMEM((ROWS_ALL, 128), f32),
            pltpu.VMEM((C * N, 128), f32),
        ],
        compiler_params=pltpu.CompilerParams(vmem_limit_bytes=16 * MIB),
        name="unpack",
    )(pos, feats, *parts)


class Segments:
    def __init__(self, seg_ref, me_ref, micro, nb, n_dev):
        self.seg_ref, self.micro, self.nb, self.n_dev = seg_ref, micro, nb, n_dev
        self.bounds, self.here, self.same = [], [], []
        for m in range(micro):
            bounds, total = [], 0
            for k in range(SEGS):
                total = total + seg_ref[m, k]
                bounds.append(total)
            here = []
            for o in range(-1, nb + 1):
                at = (me_ref[0] * nb + o) * BLK
                here.append(functools.reduce(lambda p, q: p + q, [jnp.where(at >= k, 1, 0) for k in bounds]))
            start, end = me_ref[0] * nb, me_ref[0] * nb + nb
            same = [jnp.where(p == q, 1.0, 0.0).astype(f32) for p, q in zip(here[:-1], here[1:])]
            same[0] = jnp.where(start > 0, same[0], 0.0)
            same[-1] = jnp.where(end < n_dev * nb, same[-1], 0.0)
            self.bounds.append(bounds)
            self.here.append([jnp.minimum(h, SEGS - 1) for h in here])
            self.same.append(same)
        lane = lax.broadcasted_iota(jnp.int32, (1, 128), 1)
        self.lane_micro = lane // (KINDS * nb)
        start = lax.broadcasted_iota(jnp.int32, (n_dev, 128), 0) * nb
        start = (start + (lax.broadcasted_iota(jnp.int32, (n_dev, 128), 1) // KINDS) % nb) * BLK
        self.ids = jnp.zeros((n_dev, 128), jnp.int32)
        for k in range(SEGS - 1):
            bound = self.by_micro([b[k] for b in self.bounds])
            self.ids = self.ids + jnp.where(start >= bound, 1, 0)
        lengths = self.rows([self.by_micro([seg_ref[m, k] for m in range(micro)]) for k in range(SEGS)])
        self.inverse = 1.0 / (lengths.astype(f32) * HW)

    def by_micro(self, values):
        out = jnp.full((1, 128), values[0], jnp.int32)
        for m in range(1, self.micro):
            out = jnp.where(self.lane_micro == m, values[m], out)
        return out

    def rows(self, values):
        at = lax.broadcasted_iota(jnp.int32, (SEGS, 128), 0)
        out = jnp.broadcast_to(values[0], (SEGS, 128))
        for k in range(1, SEGS):
            out = jnp.where(at == k, values[k], out)
        return out

    def means(self, stats):
        sums = self.rows(
            [row_sum(fold_rows(jnp.where(self.ids == k, stats, 0.0))) for k in range(SEGS)]
        )
        total = sums
        for b in range(1, self.nb):
            total = total + pltpu.roll(sums, 128 - b * KINDS, 1)
        return total * self.inverse

    def norm(self, stats):
        mean = self.means(stats)
        factor = lax.rsqrt(pltpu.roll(mean, 127, 1) - mean * mean + norm_eps)
        return mean, factor

    def pick(self, ref, m, o):
        at = m * self.nb * KINDS
        return ref[pl.ds(self.here[m][o], 1), :][:, at : at + 1]

    def taps(self, vec, m, h):
        k0, k2 = vec[4:5, :], vec[6:7, :]
        lo = k0 * self.same[m][h // 2 - 1] if h % 2 == 0 else k0
        hi = k2 if h % 2 == 0 else k2 * self.same[m][h // 2]
        return lo, hi


def depth_kernel(
    me_ref, seg_ref, stats_ref, x_ref, near_ref, far_ref, w_in, vec, d_ref, edge_ref, out_stats, tab, par, a_s, n_s
):
    micro, frames, _ = x_ref.shape
    nb = frames // BLK
    even = me_ref[0] % 2 == 0
    g1, b1 = 1.0 + vec[0:1, :], vec[1:2, :]
    lane = lax.broadcasted_iota(jnp.int32, (1, 128), 1)

    def project(m, slot):
        def side(at, first):
            near, far = near_ref[m, 0:BLK, :], far_ref[m, 0:BLK, :]
            a_s[slot, at : at + BLK, :] = mm(jnp.where(even == first, far, near), w_in[...])

        def main(c):
            cols = slice(c, c + HALF_W)
            a_s[slot, BLK : BLK + frames, cols] = mm(x_ref[m], w_in[:, cols])

        steps = [functools.partial(main, c) for c in range(0, HW, HALF_W)]
        return steps + [
            functools.partial(side, 0, True),
            functools.partial(side, BLK + frames, False),
        ]

    def body(m, slot, row):
        def normed(h, cols):
            o = h // 2
            scale, shift = par[m, 0, o : o + 1, cols], par[m, 1, o : o + 1, cols]
            for r in range(h * DIL, (h + 1) * DIL, ROWS):
                half = a_s[slot, r : r + ROWS, cols]
                u = half + half * jnp.tanh(half)
                n_s[r : r + ROWS, cols] = (u * scale + shift).astype(bf16).astype(f32)

        totals = {b: [0.0, 0.0] for b in range(nb)}

        def conv(h, cols):
            lo, hi = par[m, 2, h : h + 1, cols], par[m, 3, h : h + 1, cols]
            k1, kb = 0.5 * vec[5:6, cols], 0.5 * vec[7:8, cols]
            first = second = jnp.zeros((8, LANES), f32)
            for r in range(0, DIL, ROWS):
                at = h * DIL + r
                half = (
                    lo * n_s[at - DIL : at - DIL + ROWS, cols]
                    + k1 * n_s[at : at + ROWS, cols]
                    + hi * n_s[at + DIL : at + DIL + ROWS, cols]
                    + kb
                )
                if h == 1:
                    edge_ref[m, r : r + ROWS, cols] = half
                elif h == 2 * nb + 2:
                    edge_ref[m, DIL + r : DIL + r + ROWS, cols] = half
                else:
                    d_ref[m, at - BLK : at - BLK + ROWS, cols] = half
                    v = half + half * jnp.tanh(half)
                    first = first + fold_rows(v)
                    second = second + fold_rows(v * v)
            if 2 <= h < 2 * nb + 2:
                total = totals[h // 2 - 1]
                total[0] = total[0] + first
                total[1] = total[1] + second

        work = [functools.partial(normed, *t) for t in tiles_of(range(2 * nb + 4))]
        work += [functools.partial(conv, *t) for t in tiles_of(range(1, 2 * nb + 3))]
        weave(project(jnp.minimum(m + 1, micro - 1), 1 - slot), work)
        for b, total in totals.items():
            for k, val in enumerate(total):
                val = jnp.sum(row_sum(val), axis=1, keepdims=True)
                row = jnp.where(lane == (m * nb + b) * KINDS + k, val, row)
        return row

    seg = Segments(seg_ref, me_ref, micro, nb, stats_ref.shape[0])
    tab[0], tab[1] = seg.norm(stats_ref[:, 0, :])
    for m in range(micro):
        for o in range(nb + 2):
            scale = seg.pick(tab.at[1], m, o) * g1
            par[m, 0, o : o + 1, :] = scale
            par[m, 1, o : o + 1, :] = b1 - seg.pick(tab.at[0], m, o) * scale
        for h in range(1, 2 * nb + 3):
            lo, hi = seg.taps(vec, m, h)
            par[m, 2, h : h + 1, :] = 0.5 * lo
            par[m, 3, h : h + 1, :] = 0.5 * hi
    for step in project(0, 0):
        step()
    row = loop(micro, body, jnp.zeros((1, 128), f32))
    out_stats[...] = jnp.broadcast_to(row[None], out_stats.shape)


def depth(me, lengths, stats, feats, near, far, w_in, vec):
    micro, frames, _ = feats.shape
    return pl.pallas_call(
        depth_kernel,
        out_shape=(
            jax.ShapeDtypeStruct((micro, frames, HW), f32),
            jax.ShapeDtypeStruct((micro, 2 * DIL, HW), f32),
            jax.ShapeDtypeStruct(stats.shape, f32),
        ),
        in_specs=[smem(), smem()] + [vmem()] * 6,
        out_specs=(vmem(),) * 3,
        scratch_shapes=[
            pltpu.VMEM((2, SEGS, 128), f32),
            pltpu.VMEM((micro, 4, 8, HW), f32),
            pltpu.VMEM((2, frames + 2 * BLK, HW), f32),
            pltpu.VMEM((frames + 2 * BLK, HW), f32),
        ],
        compiler_params=pltpu.CompilerParams(vmem_limit_bytes=DEPTH_MIB * MIB),
        name="depth",
    )(me, lengths, stats, feats, near, far, w_in, vec)


def head_kernel(
    me_ref,
    seg_ref,
    stats_ref,
    d_ref,
    x_ref,
    enc_ref,
    dy_ref,
    own_ref,
    other_ref,
    w_rs,
    w_mask,
    w_dect,
    vec,
    block_ref,
    wave_own_ref,
    wave_other_ref,
    ds_ref,
    out_stats,
    g_rs,
    g_mask,
    g_dec,
    g_vec,
    tab,
    par,
    sums,
    ends,
    n2_s,
    v_s,
    sd_s,
    z_s,
    slope_s,
    dys_s,
    q_s,
    gm_s,
    e_s,
    dq_s,
    dz_s,
    dn2_s,
    dw_s,
    wave_s,
):
    micro, frames, _ = d_ref.shape
    nb = frames // BLK
    halves = 2 * nb
    for ref in (g_rs, g_mask, g_dec, g_vec):
        ref[...] = jnp.zeros_like(ref)
    core = me_ref[0] % 2
    ours = pl.ds(pl.multiple_of(core * frames, BLK), frames)
    lane = lax.broadcasted_iota(jnp.int32, (1, 128), 1)
    seg = Segments(seg_ref, me_ref, micro, nb, stats_ref.shape[0])
    tab[0], tab[1] = seg.norm(stats_ref[:, 0, :])
    for m in range(micro):
        means = [seg.pick(tab.at[0], m, o) for o in range(nb + 1)]
        factors = [seg.pick(tab.at[1], m, o) for o in range(nb + 1)]
        for h in range(halves):
            o = 1 + h // 2
            scale = factors[o] * (1.0 + vec[2:3, :])
            lo, hi = seg.taps(vec, m, h + 2)
            rows = (
                scale,
                vec[3:4, :] - means[o] * scale,
                jnp.broadcast_to(means[o], (1, HW)),
                jnp.broadcast_to(factors[o], (1, HW)),
                vec[5:6, :] + lo + hi,
            )
            for k, v in enumerate(rows):
                par[m, k, h : h + 1, :] = v

    def norm_steps(m, slot):
        def step(h, cols):
            scale, shift = par[m, 0, h : h + 1, cols], par[m, 1, h : h + 1, cols]
            s0 = s1 = c0 = c1 = jnp.zeros((8, LANES), f32)
            for r in range(h * DIL, (h + 1) * DIL, ROWS):
                rows = slice(r, r + ROWS)
                half = d_ref[m, rows, cols]
                v, sd = slope_parts(half, jnp.tanh(half))
                n2_s[slot, rows, cols] = (v * scale + shift).astype(bf16)
                v_s[slot, rows, cols] = v
                sd_s[slot, rows, cols] = sd
                cv = v * sd
                s0 = s0 + fold_rows(sd)
                s1 = s1 + fold_rows(sd * half)
                c0 = c0 + fold_rows(cv)
                c1 = c1 + fold_rows(cv * half)
            for k, v in enumerate((s0, s1, c0, c1)):
                sums[slot, k, h : h + 1, cols] = row_sum(v)

        return [functools.partial(step, *t) for t in tiles_of(range(halves))]

    def end_steps(m, slot):
        def step(h, cols):
            sum_d = sum_dv = a0 = a1 = jnp.zeros((8, LANES), f32)
            for r in range(h * DIL, (h + 1) * DIL, ROWS):
                rows = slice(r, r + ROWS)
                dn2 = dn2_s[rows, cols]
                a = dn2 * sd_s[slot, rows, cols]
                sum_d = sum_d + fold_rows(dn2)
                sum_dv = sum_dv + fold_rows(dn2 * v_s[slot, rows, cols])
                a0 = a0 + fold_rows(a)
                a1 = a1 + fold_rows(a * d_ref[m, rows, cols])
            for k, v in enumerate((sum_d, sum_dv, a0, a1)):
                ends[k, h : h + 1, cols] = row_sum(v)

        return [functools.partial(step, *t) for t in tiles_of(range(halves))]

    def end_row(m, at, slot, row, valid):
        scale, _, mean, factor, kappa = [par[m, k, 0:halves, :] for k in range(5)]
        s0, s1, c0, c1 = [sums[slot, k, 0:halves, :] for k in range(4)]
        sum_d, sum_dv, a0, a1 = [ends[k, 0:halves, :] for k in range(4)]
        g1, g2 = 1.0 + vec[0:1, :], 1.0 + vec[2:3, :]
        gain = (sum_dv - mean * sum_d) * factor
        g_vec[2:3, :] += jnp.where(valid, row_sum(gain), 0.0)
        g_vec[3:4, :] += jnp.where(valid, row_sum(sum_d), 0.0)
        vw = g1 * kappa
        delta = vec[7:8, :] + vec[1:2, :] * kappa
        a0, a1 = 0.5 * a0 * scale, a1 * scale
        s0, s1 = 0.5 * s0 * factor, s1 * factor
        c0 = 0.5 * c0 * factor * factor - mean * factor * s0
        c1 = c1 * factor * factor - mean * factor * s1
        vals = (
            sum_d * g2,
            gain * g2,
            vw * a0,
            vw * s0,
            vw * c0,
            a1 - delta * a0,
            s1 - delta * s0,
            c1 - delta * c0,
        )
        for k, val in enumerate(vals):
            val = jnp.sum(val, axis=1, keepdims=True)
            for b in range(nb):
                two = val[2 * b : 2 * b + 1, :] + val[2 * b + 1 : 2 * b + 2, :]
                row = jnp.where(lane == at + b * KINDS + k, two, row)
        return row

    def body(m, slot, row):
        later, before = min(m + 1, micro - 1), max(m - 1, 0)
        own, other = own_ref[m, :, ours], other_ref[m, :, ours]
        dw_s[slot, 0] = jnp.where(core == 0, own, other)
        dw_s[slot, 1] = jnp.where(core == 0, other, own)
        ahead = norm_steps(later, 1 - slot)

        def skip():
            rows = slice(0, frames)
            ys = mm(n2_s[slot, rows, :], w_rs[...])
            block_ref[m, rows, :] = (x_ref[m, rows, :].astype(f32) + ys[:, 0:B]).astype(bf16)
            half = 0.5 * ys[:, B : B + SC]
            z, slope = slope_parts(half, jnp.tanh(half))
            z_s[rows, :] = z.astype(bf16)
            slope_s[rows, :] = slope

        def logits(k, c):
            cols = slice(k * N + c, k * N + c + HALF_W)
            q_s[k, :, c : c + HALF_W] = mm(z_s[...], w_mask[:, cols])

        def back(k, c):
            cols = slice(k * N + c, k * N + c + HALF_W)
            gm_s[k, :, c : c + HALF_W] = mm_rows(dw_s[slot, k], w_dect[:, cols])

        def masked(k, h, cols):
            for r in range(h * DIL, (h + 1) * DIL, ROWS):
                rows = slice(r, r + ROWS)
                t = jnp.tanh(q_s[k, rows, cols])
                pe = (0.5 * t + 0.5) * enc_ref[m, rows, cols].astype(f32)
                e_s[k, rows, cols] = pe.astype(bf16)
                dq_s[k, rows, cols] = (gm_s[k, rows, cols] * (pe * (1.0 - t))).astype(bf16)

        def wave(k):
            cols = slice(k * N, (k + 1) * N)
            wave_s[k] = (2.0 * mm_t(w_dect[:, cols], e_s[k])).astype(bf16)

        def gated(k):
            cols = slice(k * N, (k + 1) * N)
            rows = slice(0, frames)
            part = mm_t(dq_s[k, rows, :], w_mask[:, cols])
            dz_s[rows, :] = part if k == 0 else dz_s[rows, :] + part

        def dec_grad(k):
            cols = slice(k * N, (k + 1) * N)
            g_dec[:, cols] += mm(dw_s[slot, k], e_s[k])

        def mask_grad(k, c):
            cols = slice(k * N + c, k * N + c + HALF_W)
            g_mask[:, cols] += mm_rows(z_s[...], dq_s[k, :, c : c + HALF_W])

        def norm_back(c):
            dn2_s[:, c : c + HALF_W] = mm_t(dys_s[...], w_rs[c : c + HALF_W, :])

        def out_grad(c):
            g_rs[:, c : c + HALF_W] += mm_rows(dys_s[...], n2_s[slot, :, c : c + HALF_W])

        part = functools.partial
        wide = range(0, HW, HALF_W)
        third = len(ahead) // 3

        def ups(k):
            return [part(logits, k, c) for c in wide] + [part(back, k, c) for c in wide]

        def elementwise(k):
            return [part(masked, k, *t) for t in tiles_of(range(halves))]

        def downs(k):
            return (
                [part(gated, k)]
                + [part(mask_grad, k, c) for c in wide]
                + [part(wave, k), part(dec_grad, k)]
            )

        weave([skip], end_steps(before, 1 - slot))
        row = end_row(before, (m - 1) * nb * KINDS, 1 - slot, row, m > 0)
        weave(ups(0), ahead[:third])
        weave(ups(1), elementwise(0))
        weave(downs(0), elementwise(1))
        weave(downs(1), ahead[third : 2 * third])
        wave_own_ref[m] = jnp.where(core == 0, wave_s[0], wave_s[1])
        wave_other_ref[m] = jnp.where(core == 0, wave_s[1], wave_s[0])
        ds = (dz_s[...] * slope_s[...]).astype(bf16)
        ds_ref[m] = ds
        dys_s[:, 0:B] = dy_ref[m]
        dys_s[:, B : B + SC] = ds
        weave([part(norm_back, c) for c in wide] + [part(out_grad, c) for c in wide], ahead[2 * third :])
        return row

    for step in norm_steps(0, 0):
        step()
    row = jnp.zeros((1, 128), f32)
    for m in range(micro):
        row = body(m, m % 2, row)
    last = micro - 1
    for step in end_steps(last, last % 2):
        step()
    row = end_row(last, last * nb * KINDS, last % 2, row, True)
    out_stats[...] = jnp.broadcast_to(row[None], out_stats.shape)


def head(me, lengths, stats, d, feats, enc, dy, own, other, w_rs, w_mask, w_dect, vec):
    micro, frames, _ = feats.shape
    outs = (
        (feats.shape, bf16),
        ((micro, L, frames), bf16),
        ((micro, L, frames), bf16),
        ((micro, frames, SC), bf16),
        (stats.shape, f32),
        ((B + SC, HW), f32),
        ((SC, C * N), f32),
        ((L, C * N), f32),
        ((8, HW), f32),
    )
    return pl.pallas_call(
        head_kernel,
        in_specs=[smem(), smem()] + [vmem()] * 11,
        out_specs=(vmem(),) * len(outs),
        scratch_shapes=[
            pltpu.VMEM((2, SEGS, 128), f32),
            pltpu.VMEM((micro, 5, 8, HW), f32),
            pltpu.VMEM((2, 4, 8, HW), f32),
            pltpu.VMEM((4, 8, HW), f32),
            pltpu.VMEM((2, frames, HW), bf16),
            pltpu.VMEM((2, frames, HW), f32),
            pltpu.VMEM((2, frames, HW), f32),
            pltpu.VMEM((frames, SC), bf16),
            pltpu.VMEM((frames, SC), f32),
            pltpu.VMEM((frames, B + SC), bf16),
            pltpu.VMEM((C, frames, N), f32),
            pltpu.VMEM((C, frames, N), f32),
            pltpu.VMEM((C, frames, N), bf16),
            pltpu.VMEM((C, frames, N), bf16),
            pltpu.VMEM((frames, SC), f32),
            pltpu.VMEM((frames, HW), f32),
            pltpu.VMEM((2, C, L, frames), bf16),
            pltpu.VMEM((C, L, frames), bf16),
        ],
        out_shape=tuple(jax.ShapeDtypeStruct(s, t) for s, t in outs),
        compiler_params=pltpu.CompilerParams(vmem_limit_bytes=HEAD_MIB * MIB),
        name="head",
    )(me, lengths, stats, d, feats, enc, dy, own, other, w_rs, w_mask, w_dect, vec)


def back_means(seg, stats):
    v = seg.means(stats)
    w = [v] + [pltpu.roll(v, 128 - k, 1) for k in range(1, KINDS)]
    p2, q2 = w[0], w[1]
    return p2, q2, w[2] - p2 * w[3] - q2 * w[4], w[5] - p2 * w[6] - q2 * w[7]


def input_kernel(
    me_ref,
    seg_ref,
    stats1_ref,
    stats2_ref,
    stats3_ref,
    d_ref,
    edge_ref,
    x_ref,
    dy_ref,
    dy_near,
    dy_far,
    ds_ref,
    ds_near,
    ds_far,
    w_in,
    w_rs,
    vec,
    feats_ref,
    g_in,
    g_vec,
    tab,
    par2,
    par1,
    col_s,
    dn2_s,
    dd_s,
    a_s,
    da_s,
):
    micro, frames, _ = d_ref.shape
    nb = frames // BLK
    halves = 2 * nb
    part = functools.partial
    for ref in (g_in, g_vec):
        ref[...] = jnp.zeros_like(ref)
    even = me_ref[0] % 2 == 0
    halo = slice(BLK, BLK + DIL)
    g1, g2 = 1.0 + vec[0:1, :], 1.0 + vec[2:3, :]
    seg = Segments(seg_ref, me_ref, micro, nb, stats1_ref.shape[0])
    tables = seg.norm(stats1_ref[:, 0, :]) + seg.norm(stats2_ref[:, 0, :])
    for k, table in enumerate(tables + back_means(seg, stats3_ref[:, 0, :])):
        tab[k] = table
    for m in range(micro):
        mean1, factor1, mean2, factor2, p2, q2, p1, q1 = [
            [seg.pick(tab.at[k], m, o) for o in range(nb + 2)] for k in range(8)
        ]
        for o in range(nb + 2):
            slope = 0.5 * factor2[o] * factor2[o] * q2[o]
            shift = 0.5 * factor2[o] * p2[o] - slope * mean2[o]
            rows = ((0.5 * factor2[o]) * g2, slope, shift)
            for k, v in enumerate(rows):
                par2[m, k, o : o + 1, :] = jnp.broadcast_to(v, (1, HW))
        for b in range(nb):
            o = b + 1
            scale = factor1[o] * g1
            slope = 0.5 * factor1[o] * factor1[o] * q1[o]
            rows = (
                scale,
                vec[1:2, :] - mean1[o] * scale,
                slope,
                0.5 * factor1[o] * p1[o] - slope * mean1[o],
                mean1[o],
                factor1[o],
                vec[4:5, :] * seg.same[m][o],
                vec[6:7, :] * seg.same[m][o - 1],
                seg.same[m][o],
                seg.same[m][o - 1],
            )
            for k, v in enumerate(rows):
                par1[m, k, b : b + 1, :] = jnp.broadcast_to(v, (1, HW))

    def project(m, slot):
        def side(at, first):
            near = jnp.concatenate([dy_near[m, halo, :], ds_near[m]], axis=1)
            far = jnp.concatenate([dy_far[m, halo, :], ds_far[m]], axis=1)
            dn2_s[at : at + DIL, :] = mm_t(jnp.where(even == first, far, near), w_rs[...])

        def main(c):
            dys = jnp.concatenate([dy_ref[m], ds_ref[m]], axis=1)
            dn2_s[DIL : DIL + frames, c : c + HALF_W] = mm_t(dys, w_rs[c : c + HALF_W, :])

        def hidden(c):
            a_s[slot, :, c : c + HALF_W] = mm(x_ref[m], w_in[:, c : c + HALF_W])

        wide = range(0, HW, HALF_W)
        return (
            [part(main, c) for c in wide]
            + [part(side, 0, True), part(side, DIL + frames, False)]
            + [part(hidden, c) for c in wide]
        )

    def depth_steps(m):
        def step(h, cols):
            o = (h + 1) // 2
            scale, slope, shift = [par2[m, k, o : o + 1, cols] for k in range(3)]
            total = jnp.zeros((8, LANES), f32)
            for r in range(0, DIL, ROWS):
                at = h * DIL + r
                if h == 0:
                    half = edge_ref[m, r : r + ROWS, cols]
                elif h == halves + 1:
                    half = edge_ref[m, DIL + r : DIL + r + ROWS, cols]
                else:
                    half = d_ref[m, at - DIL : at - DIL + ROWS, cols]
                v, sd = slope_parts(half, jnp.tanh(half))
                rows = slice(at, at + ROWS)
                dd = (sd * (dn2_s[rows, cols] * scale - v * slope - shift)).astype(bf16).astype(f32)
                dd_s[rows, cols] = dd
                total = total + fold_rows(dd)
            col_s[h : h + 1, cols] = row_sum(total)

        return [part(step, *t) for t in tiles_of(range(halves + 2))]

    def hidden_steps(m, slot):
        def step(h, cols):
            b = h // 2
            scale, shift, slope, base, mean, factor, k0, k2, hi, lo = [
                par1[m, k, b : b + 1, cols] for k in range(10)
            ]
            k1 = vec[5:6, cols]
            if h % 2 == 0:
                k0, hi = vec[4:5, cols], 1.0
            else:
                k2, lo = vec[6:7, cols], 1.0
            half_scale = 0.5 * scale
            s0 = s1 = s2 = jnp.zeros((8, LANES), f32)
            for r in range(h * DIL, (h + 1) * DIL, ROWS):
                prev, here, nxt = [dd_s[r + q * DIL : r + q * DIL + ROWS, cols] for q in range(3)]
                half = a_s[slot, r : r + ROWS, cols]
                u, su = slope_parts(half, jnp.tanh(half))
                n1 = (u * scale + shift).astype(bf16).astype(f32)
                s0 = s0 + fold_rows(nxt * n1)
                s1 = s1 + fold_rows(here * n1)
                s2 = s2 + fold_rows(prev * n1)
                dn1 = k1 * here + k0 * nxt + k2 * prev
                du = dn1 * half_scale - u * slope - base
                da_s[r : r + ROWS, cols] = (du * su).astype(bf16)
            s0, s1, s2 = [row_sum(v) for v in (s0, s1, s2)]
            prev, here, nxt = [col_s[h + q : h + q + 1, cols] for q in range(3)]
            dn1 = k1 * here + k0 * nxt + k2 * prev
            dn1_u = (k1 * s1 + k0 * s0 + k2 * s2 - shift * dn1) / scale
            rows = (
                (0, (dn1_u - mean * dn1) * factor),
                (1, dn1),
                (4, s0 * hi),
                (5, s1),
                (6, s2 * lo),
                (7, here),
            )
            for k, v in rows:
                g_vec[k : k + 1, cols] += v

        return [part(step, *t) for t in tiles_of(range(halves))]

    def last_steps(m):
        def weight(c):
            g_in[:, c : c + HALF_W] += mm_rows(x_ref[m], da_s[:, c : c + HALF_W])

        def feats(r):
            rows = slice(r, r + BLK)
            grad = dy_ref[m, rows, :].astype(f32) + 2.0 * mm_t(da_s[rows, :], w_in[...])
            feats_ref[m, rows, :] = grad.astype(bf16)

        return [part(weight, c) for c in range(0, HW, HALF_W)] + [
            part(feats, r) for r in range(0, frames, BLK)
        ]

    def body(m, slot, carry):
        run(project(m, 0) + depth_steps(m) + hidden_steps(m, 0) + last_steps(m))
        return carry

    lax.fori_loop(0, micro, lambda m, c: body(m, 0, c), 0)


def input_grad(me, lengths, stats, d, edge, feats, dy, near, far, ds, ds_near, ds_far, w_in, w_rs, vec):
    micro, frames, _ = d.shape
    return pl.pallas_call(
        input_kernel,
        out_shape=(
            jax.ShapeDtypeStruct(feats.shape, bf16),
            jax.ShapeDtypeStruct((B, HW), f32),
            jax.ShapeDtypeStruct((8, HW), f32),
        ),
        in_specs=[smem(), smem()] + [vmem()] * 15,
        out_specs=(vmem(),) * 3,
        scratch_shapes=[
            pltpu.VMEM((8, SEGS, 128), f32),
            pltpu.VMEM((micro, 3, 8, HW), f32),
            pltpu.VMEM((micro, 10, 8, HW), f32),
            pltpu.VMEM((8, HW), f32),
            pltpu.VMEM((frames + 2 * DIL, HW), f32),
            pltpu.VMEM((frames + 2 * DIL, HW), f32),
            pltpu.VMEM((2, frames, HW), f32),
            pltpu.VMEM((frames, HW), bf16),
        ],
        compiler_params=pltpu.CompilerParams(vmem_limit_bytes=INPUT_MIB * MIB),
        name="input_grad",
    )(me, lengths, *stats, d, edge, feats, dy, near, far, ds, ds_near, ds_far, w_in, w_rs, vec)


def pack_kernel(pos_ref, g_in, g_rs, g_mask, g_dec, vec_a, vec_b, keep_ref, send_ref, t, out, wd):
    for k in range(4):
        cols = slice(128 * k, 128 * k + 128)
        t[pl.ds(R_IN + k, 128, stride=4), :] = g_in[:, cols]
        for c in range(C):
            t[pl.ds(R_MASK + 512 * c + k, 128, stride=4), :] = g_mask[
                :, 512 * c + 128 * k : 512 * c + 128 * k + 128
            ]
        t[pl.ds(R_VEC + k, 8, stride=4), :] = vec_a[:, cols] + vec_b[:, cols]
    t[R_RES : R_RES + 512, :] = g_rs[0:128, :].T
    t[R_SKIP : R_SKIP + 512, :] = g_rs[128:256, :].T
    wd[...] = jnp.concatenate([g_dec[...], jnp.zeros((128 - L, C * N), f32)], axis=0).T
    part = lax.broadcasted_iota(jnp.int32, (64, 128), 1) // L
    for c in range(C):
        rows = jnp.zeros((64, 128), f32)
        for s in range(8):
            piece = pltpu.roll(wd[pl.ds(512 * c + s, 64, stride=8), :], L * s, 1)
            rows = jnp.where(part == s, piece, rows)
        t[R_DEC + 64 * c : R_DEC + 64 * c + 64, :] = rows
    out[...] = jnp.zeros_like(out)
    for i in range(NCH):
        start = pl.multiple_of(pos_ref[i] * 8, 8)
        out[pl.ds(start, 8), :] = t[8 * i : 8 * i + 8, :]
    half = keep_ref.shape[0]
    keep_ref[...] = out[0:half, :]
    send_ref[...] = out[half : 2 * half, :].astype(bf16)


def pack(pos, g_in, g_rs, g_mask, g_dec, vec_a, vec_b, rows):
    return pl.pallas_call(
        pack_kernel,
        out_shape=(
            jax.ShapeDtypeStruct((rows // 2, 128), f32),
            jax.ShapeDtypeStruct((rows // 2, 128), bf16),
        ),
        in_specs=[smem()] + [vmem()] * 6,
        out_specs=(vmem(), vmem()),
        scratch_shapes=[
            pltpu.VMEM((ROWS_ALL, 128), f32),
            pltpu.VMEM((rows, 128), f32),
            pltpu.VMEM((C * N, 128), f32),
        ],
        compiler_params=pltpu.CompilerParams(vmem_limit_bytes=16 * MIB),
        name="pack",
    )(pos, g_in, g_rs, g_mask, g_dec, vec_a, vec_b)


def fold_kernel(n_got, n_next, *refs):
    keep_ref, got = refs[0], refs[1 : 1 + n_got]
    outs = refs[1 + n_got :]
    total = keep_ref[...]
    for g in got:
        total = total + g[...].astype(f32)
    size = total.shape[0] // n_next
    outs[0][...] = total[0:size, :]
    for q in range(1, n_next):
        outs[q][...] = total[q * size : (q + 1) * size, :].astype(bf16)


def fold(keep, got, n_next):
    size = keep.shape[0] // n_next
    outs = [jax.ShapeDtypeStruct((size, 128), f32)]
    outs += [jax.ShapeDtypeStruct((size, 128), bf16)] * (n_next - 1)
    return pl.pallas_call(
        functools.partial(fold_kernel, len(got), n_next),
        out_shape=tuple(outs),
        in_specs=[vmem()] * (1 + len(got)),
        out_specs=tuple(vmem() for _ in outs),
        compiler_params=pltpu.CompilerParams(vmem_limit_bytes=8 * MIB),
        name="fold",
    )(keep, *got)


def adam_kernel(n_got, count_ref, *refs):
    keep_ref, got = refs[0], refs[1 : 1 + n_got]
    master_ref, one_ref, two_ref, new_master, new_one, new_two, buf = refs[1 + n_got :]
    total = keep_ref[...]
    for g in got:
        total = total + g[...].astype(f32)
    buf[...] = total
    slots = master_ref.shape[0]
    used = lax.broadcasted_iota(jnp.int32, (slots, 128), 0) < count_ref[0]
    for j in range(8):
        cols = slice(128 * j, 128 * j + 128)
        grad = buf[pl.ds(j, slots, stride=8), :]
        master = master_ref[:, cols]
        one = beta_one * one_ref[:, cols] + (1.0 - beta_one) * grad
        two = beta_two * two_ref[:, cols] + (1.0 - beta_two) * grad * grad
        unbias_one = one / (1.0 - beta_one**STEP)
        unbias_two = two / (1.0 - beta_two**STEP)
        new = master - learn_rate * (
            unbias_one / (jnp.sqrt(unbias_two) + adam_eps) + weight_decay * master
        )
        new_master[:, cols] = jnp.where(used, new, 0.0)
        new_one[:, cols] = jnp.where(used, one, 0.0)
        new_two[:, cols] = jnp.where(used, two, 0.0)


def adam(count, keep, got, master, one, two):
    out = jax.ShapeDtypeStruct(master.shape, f32)
    return pl.pallas_call(
        functools.partial(adam_kernel, len(got)),
        out_shape=(out, out, out),
        in_specs=[smem()] + [vmem()] * (4 + len(got)),
        out_specs=(vmem(), vmem(), vmem()),
        scratch_shapes=[pltpu.VMEM(keep.shape, f32)],
        compiler_params=pltpu.CompilerParams(vmem_limit_bytes=4 * MIB),
        name="adam",
    )(count, keep, *got, master, one, two)


def local(n_tm, n_src, feats, encoded, seg_lengths, owners, master, moment_one, moment_two, out_cot, wave_cot):
    n_dev = n_tm * n_src
    me = lax.axis_index(AXES)
    core = lax.axis_index("src")
    micro, frames, _ = feats.shape
    nb = frames // BLK
    slots = master.shape[0]


    across = [(i, i + 1) for i in range(1, n_dev - 1, 2)]
    across = across + [(j, i) for i, j in across]

    def ends(at_end, *arrays):
        size = [jnp.where(at_end, v.shape[1] - w, 0) for v, w in arrays]
        rows = [lax.dynamic_slice_in_dim(v, at, w, axis=1) for (v, w), at in zip(arrays, size)]
        return rows[0] if len(rows) == 1 else jnp.concatenate(rows, axis=1)

    owner_ids = owners[:, 0]
    order = jnp.arange(NCH, dtype=jnp.int32)
    earlier = (owner_ids[:, None] == owner_ids[None, :]) & (order[None, :] < order[:, None])
    rank = jnp.sum(earlier.astype(jnp.int32), axis=1)
    pos = relative_block(owner_ids, me, n_dev) * slots + rank
    count = jnp.sum((owner_ids == me).astype(jnp.int32)).reshape(1)
    here = me.astype(jnp.int32).reshape(1)

    cot = jnp.transpose(wave_cot[:, 0], (0, 2, 1))
    halo = (feats, BLK), (out_cot, DIL)
    sides = ends(core == 0, *halo), ends(core == 1, *halo)
    parts, (pos, here, count), (near, far, cot_other) = gather_tiles(
        to_tiles(master), n_dev, (pos, here, count), (*sides, cot)
    )
    near = swap(near, 1, n_dev)
    far = lax.ppermute(far, AXES, across)
    cot_other = swap(cot_other, 1, n_dev)

    w_in, w_rs, w_mask, w_dect, vec, stats = unpack(pos, parts, feats, n_dev)
    stats1 = share_sums(stats, n_dev)
    stats1, near, far, cot_other = lax.optimization_barrier((stats1, near, far, cot_other))
    d, edge, stats = depth(here, seg_lengths, stats1, feats, near, far, w_in, vec)
    stats2 = share_sums(stats, n_dev)
    block_out, wave_own, wave_other, ds, stats, g_rs, g_mask, g_dec, vec_a = head(
        here, seg_lengths, stats2, d, feats, encoded, out_cot, cot, cot_other, w_rs, w_mask, w_dect, vec
    )
    stats3 = share_sums(stats, n_dev)
    ds_near = swap(ends(core == 0, (ds, DIL)), 1, n_dev)
    ds_far = lax.ppermute(ends(core == 1, (ds, DIL)), AXES, across)

    wave_got = swap(wave_other, 1, n_dev)
    waves = jnp.concatenate(
        [jnp.where(core == 0, wave_own, wave_got), jnp.where(core == 0, wave_got, wave_own)], axis=2
    )
    waves = jnp.transpose(waves, (0, 2, 1))[:, None]

    feats_grad, g_in, vec_b = input_grad(
        here, seg_lengths, (stats1, stats2, stats3), d, edge, feats, out_cot, near, far, ds, ds_near, ds_far, w_in, w_rs, vec
    )

    keep, send = pack(pos, g_in, g_rs, g_mask, g_dec, vec_a, vec_b, n_dev * slots * 8)
    received = [swap(send, 1, n_dev)]
    for bits in reversed(stages(n_dev)[:-1]):
        n_next = 1 << len(bits)
        keep, *sends = fold(keep, received, n_next)
        received = [swap(s, spread(bits, k + 1), n_dev) for k, s in enumerate(sends)]
    new_master, new_one, new_two = adam(count, keep, received, master, moment_one, moment_two)
    return block_out, feats_grad, waves, new_master, new_one, new_two


def solution(mesh):
    n_tm, n_src = mesh.shape["tm"], mesh.shape["src"]
    return jax.shard_map(
        functools.partial(local, n_tm, n_src),
        mesh=mesh,
        in_specs=(
            P(None, AXES, None),
            P(None, AXES, None),
            P(),
            P(),
            P(AXES, None),
            P(AXES, None),
            P(AXES, None),
            P(None, AXES, None),
            P(None, "src", "tm", None),
        ),
        out_specs=(
            P(None, AXES, None),
            P(None, AXES, None),
            P(None, "src", "tm", None),
            P(AXES, None),
            P(AXES, None),
            P(AXES, None),
        ),
        check_vma=False,
    )
```

```python
import functools

import jax
import jax.numpy as jnp
from jax import lax
from jax.experimental import pallas as pl
from jax.experimental.pallas import tpu as pltpu
from jax.sharding import PartitionSpec as P

N = 512
L = 16
B = 128
SC = 128
HW = 512
C = 2
DIL = 128
ROW = 1024
SEGS = 8
MICRO = 4
STEP = 10
NCH = 340
BLK = 256
KINDS = 8
CHUNK = 16
LANES, ROWS = 256, 16
HALF_W = 256

norm_eps = 1e-05
adam_eps = 1e-08
beta_one = 0.9
beta_two = 0.999
learn_rate = 0.2
weight_decay = 0.01

AXES = ("tm", "src")
f32 = jnp.float32
bf16 = jnp.bfloat16
MIB = 1024 * 1024
DEPTH_MIB = HEAD_MIB = INPUT_MIB = 20

R_IN, R_RES, R_SKIP, R_MASK, R_DEC, R_VEC = 0, 512, 1024, 1536, 2560, 2688
ROWS_ALL = 2720


def mm(a, b):
    return lax.dot_general(a, b, (((1,), (0,)), ((), ())), preferred_element_type=f32)


def mm_t(a, b):
    return lax.dot_general(a, b, (((1,), (1,)), ((), ())), preferred_element_type=f32)


def mm_rows(a, b):
    return lax.dot_general(a, b, (((0,), (0,)), ((), ())), preferred_element_type=f32)


def sigmoid(v):
    return 0.5 * jnp.tanh(0.5 * v) + 0.5


def fold_rows(v):
    return functools.reduce(lambda p, q: p + q, [v[i : i + 8, :] for i in range(0, v.shape[0], 8)])


def slope_parts(half, t):
    w = half * t
    return half + w, (1.0 + t) + (half - w * t)


def weave(first, second):
    steps = [((i + 0.5) / len(first), 0, i) for i in range(len(first))]
    steps += [((i + 0.5) / len(second), 1, i) for i in range(len(second))]
    for _, which, i in sorted(steps):
        (first, second)[which][i]()


def run(steps):
    for step in steps:
        step()


def tiles_of(halves):
    return [(h, slice(c, c + LANES)) for h in halves for c in range(0, HW, LANES)]


def loop(count, body, carry):
    def pair(i, carry):
        return body(2 * i + 1, 1, body(2 * i, 0, carry))

    return lax.fori_loop(0, count // 2, pair, carry)


def row_sum(v):
    return jnp.sum(v, axis=0, keepdims=True)


def vmem():
    return pl.BlockSpec(memory_space=pltpu.VMEM)


def smem():
    return pl.BlockSpec(memory_space=pltpu.SMEM)


def stages(n_dev):
    bits = n_dev.bit_length() - 1
    groups = []
    hi = bits - 1
    while hi >= 1:
        lo = max(1, hi - 1)
        groups.append(tuple(range(lo, hi + 1)))
        hi = lo - 1
    groups.append((0,))
    return groups


def spread(bits, k):
    return sum(((k >> j) & 1) << b for j, b in enumerate(bits))


def swap(value, mask, n_dev):
    return lax.ppermute(value, AXES, [(i, i ^ mask) for i in range(n_dev)])


def gather_tiles(tiles, n_dev, early, rows, sides):
    parts = [tiles]
    for k, bits in enumerate(stages(n_dev)[:-1]):
        if k == 1:
            parts, early, rows = lax.optimization_barrier((parts, early, rows))
        z = parts[0] if len(parts) == 1 else jnp.concatenate(parts, axis=0)
        parts = [z] + [swap(z, spread(bits, q), n_dev) for q in range(1, 1 << len(bits))]
    parts, late = lax.optimization_barrier((parts, sides(*rows)))
    return parts + [swap(z, 1, n_dev) for z in parts], early, late


def relative_block(owner, me, n_dev):
    q = owner ^ me
    index = jnp.zeros_like(q)
    size = 1
    for bits in stages(n_dev):
        digit = sum(((q >> b) & 1) << j for j, b in enumerate(bits))
        index = index + digit * size
        size = size << len(bits)
    return index


def share_sums(rows, n_dev):
    return lax.all_to_all(rows, AXES, 0, 0, tiled=True)


def tile_kernel(m_ref, out_ref, buf):
    slots = m_ref.shape[0]
    for j in range(8):
        buf[pl.ds(j, slots, stride=8), :] = m_ref[:, 128 * j : 128 * j + 128]
    out_ref[...] = buf[...].astype(bf16)


def to_tiles(master):
    slots = master.shape[0]
    return pl.pallas_call(
        tile_kernel,
        out_shape=jax.ShapeDtypeStruct((slots * 8, 128), bf16),
        in_specs=[vmem()],
        out_specs=vmem(),
        scratch_shapes=[pltpu.VMEM((slots * 8, 128), f32)],
        compiler_params=pltpu.CompilerParams(vmem_limit_bytes=4 * MIB),
        name="to_tiles",
    )(master)


def stat_rows(values, shape):
    lane = lax.broadcasted_iota(jnp.int32, shape, 1)
    row = jnp.zeros(shape, f32)
    for where, v in values.items():
        row = jnp.where(lane == where, v, row)
    return row


def unpack_kernel(n_parts, pos_ref, x_ref, *refs):
    parts, refs = refs[:n_parts], refs[n_parts:]
    w_in, w_rs, w_mask, w_dect, vec, stats, g, t, wd = refs
    size = parts[0].shape[0]
    for k, part in enumerate(parts):
        g[k * size : (k + 1) * size, :] = part[...].astype(f32)
    for i in range(NCH):
        start = pl.multiple_of(pos_ref[i] * 8, 8)
        t[8 * i : 8 * i + 8, :] = g[pl.ds(start, 8), :]
    for k in range(4):
        cols = slice(128 * k, 128 * k + 128)
        w_in[:, cols] = (0.5 * t[pl.ds(R_IN + k, 128, stride=4), :]).astype(bf16)
        for c in range(C):
            w_mask[:, 512 * c + 128 * k : 512 * c + 128 * k + 128] = (
                0.5 * t[pl.ds(R_MASK + 512 * c + k, 128, stride=4), :]
            ).astype(bf16)
        vec[:, cols] = t[pl.ds(R_VEC + k, 8, stride=4), :]
    w_rs[:, 0:128] = t[R_RES : R_RES + 512, :].astype(bf16)
    w_rs[:, 128:256] = t[R_SKIP : R_SKIP + 512, :].astype(bf16)
    part = lax.broadcasted_iota(jnp.int32, (64, 128), 1) // L
    for s in range(8):
        for c in range(C):
            rows = t[R_DEC + 64 * c : R_DEC + 64 * c + 64, :]
            rows = pltpu.roll(rows, (-L * s) % 128, 1)
            wd[pl.ds(512 * c + s, 64, stride=8), :] = jnp.where(part == 0, rows, 0.0)
    w_dect[...] = (0.5 * wd[...].T[0:L, :]).astype(bf16)
    micro, frames, _ = x_ref.shape
    nb = frames // BLK
    sums = {}
    for m in range(micro):
        for b in range(nb):
            half = mm(x_ref[m, b * BLK : (b + 1) * BLK, :], w_in[...])
            u = half + half * jnp.tanh(half)
            first = jnp.sum(jnp.sum(u, axis=0, keepdims=True), axis=1, keepdims=True)
            second = jnp.sum(jnp.sum(u * u, axis=0, keepdims=True), axis=1, keepdims=True)
            sums[(m * nb + b) * KINDS] = first
            sums[(m * nb + b) * KINDS + 1] = second
    row = stat_rows(sums, (1, 128))
    stats[...] = jnp.broadcast_to(row[None], stats.shape)


def unpack(pos, parts, feats, n_dev):
    outs = (
        jax.ShapeDtypeStruct((B, HW), bf16),
        jax.ShapeDtypeStruct((HW, B + SC), bf16),
        jax.ShapeDtypeStruct((SC, C * N), bf16),
        jax.ShapeDtypeStruct((L, C * N), bf16),
        jax.ShapeDtypeStruct((8, HW), f32),
        jax.ShapeDtypeStruct((n_dev, 1, 128), f32),
    )
    return pl.pallas_call(
        functools.partial(unpack_kernel, len(parts)),
        out_shape=outs,
        in_specs=[smem()] + [vmem()] * (1 + len(parts)),
        out_specs=tuple(vmem() for _ in outs),
        scratch_shapes=[
            pltpu.VMEM((len(parts) * parts[0].shape[0], 128), f32),
            pltpu.VMEM((ROWS_ALL, 128), f32),
            pltpu.VMEM((C * N, 128), f32),
        ],
        compiler_params=pltpu.CompilerParams(vmem_limit_bytes=16 * MIB),
        name="unpack",
    )(pos, feats, *parts)


class Segments:
    def __init__(self, seg_ref, me_ref, micro, nb, n_dev):
        self.seg_ref, self.micro, self.nb, self.n_dev = seg_ref, micro, nb, n_dev
        self.bounds, self.here, self.same = [], [], []
        for m in range(micro):
            bounds, total = [], 0
            for k in range(SEGS):
                total = total + seg_ref[m, k]
                bounds.append(total)
            here = []
            for o in range(-1, nb + 1):
                at = (me_ref[0] * nb + o) * BLK
                here.append(functools.reduce(lambda p, q: p + q, [jnp.where(at >= k, 1, 0) for k in bounds]))
            start, end = me_ref[0] * nb, me_ref[0] * nb + nb
            same = [jnp.where(p == q, 1.0, 0.0).astype(f32) for p, q in zip(here[:-1], here[1:])]
            same[0] = jnp.where(start > 0, same[0], 0.0)
            same[-1] = jnp.where(end < n_dev * nb, same[-1], 0.0)
            self.bounds.append(bounds)
            self.here.append([jnp.minimum(h, SEGS - 1) for h in here])
            self.same.append(same)
        lane = lax.broadcasted_iota(jnp.int32, (1, 128), 1)
        self.lane_micro = lane // (KINDS * nb)
        start = lax.broadcasted_iota(jnp.int32, (n_dev, 128), 0) * nb
        start = (start + (lax.broadcasted_iota(jnp.int32, (n_dev, 128), 1) // KINDS) % nb) * BLK
        self.ids = jnp.zeros((n_dev, 128), jnp.int32)
        for k in range(SEGS - 1):
            bound = self.by_micro([b[k] for b in self.bounds])
            self.ids = self.ids + jnp.where(start >= bound, 1, 0)
        lengths = self.rows([self.by_micro([seg_ref[m, k] for m in range(micro)]) for k in range(SEGS)])
        self.inverse = 1.0 / (lengths.astype(f32) * HW)

    def by_micro(self, values):
        out = jnp.full((1, 128), values[0], jnp.int32)
        for m in range(1, self.micro):
            out = jnp.where(self.lane_micro == m, values[m], out)
        return out

    def rows(self, values):
        at = lax.broadcasted_iota(jnp.int32, (SEGS, 128), 0)
        out = jnp.broadcast_to(values[0], (SEGS, 128))
        for k in range(1, SEGS):
            out = jnp.where(at == k, values[k], out)
        return out

    def means(self, stats):
        sums = self.rows(
            [row_sum(fold_rows(jnp.where(self.ids == k, stats, 0.0))) for k in range(SEGS)]
        )
        total = sums
        for b in range(1, self.nb):
            total = total + pltpu.roll(sums, 128 - b * KINDS, 1)
        return total * self.inverse

    def norm(self, stats):
        mean = self.means(stats)
        factor = lax.rsqrt(pltpu.roll(mean, 127, 1) - mean * mean + norm_eps)
        return mean, factor

    def pick(self, ref, m, o):
        at = m * self.nb * KINDS
        return ref[pl.ds(self.here[m][o], 1), :][:, at : at + 1]

    def taps(self, vec, m, h):
        k0, k2 = vec[4:5, :], vec[6:7, :]
        lo = k0 * self.same[m][h // 2 - 1] if h % 2 == 0 else k0
        hi = k2 if h % 2 == 0 else k2 * self.same[m][h // 2]
        return lo, hi


def depth_kernel(
    me_ref, seg_ref, stats_ref, x_ref, near_ref, far_ref, w_in, vec, d_ref, edge_ref, out_stats, tab, par, a_s, n_s
):
    micro, frames, _ = x_ref.shape
    nb = frames // BLK
    even = me_ref[0] % 2 == 0
    g1, b1 = 1.0 + vec[0:1, :], vec[1:2, :]
    lane = lax.broadcasted_iota(jnp.int32, (1, 128), 1)

    def project(m, slot):
        def side(at, first):
            near, far = near_ref[m, 0:BLK, :], far_ref[m, 0:BLK, :]
            a_s[slot, at : at + BLK, :] = mm(jnp.where(even == first, far, near), w_in[...])

        def main(c):
            cols = slice(c, c + HALF_W)
            a_s[slot, BLK : BLK + frames, cols] = mm(x_ref[m], w_in[:, cols])

        steps = [functools.partial(main, c) for c in range(0, HW, HALF_W)]
        return steps + [
            functools.partial(side, 0, True),
            functools.partial(side, BLK + frames, False),
        ]

    def body(m, slot, row):
        def normed(h, cols):
            o = h // 2
            scale, shift = par[m, 0, o : o + 1, cols], par[m, 1, o : o + 1, cols]
            for r in range(h * DIL, (h + 1) * DIL, ROWS):
                half = a_s[slot, r : r + ROWS, cols]
                u = half + half * jnp.tanh(half)
                n_s[r : r + ROWS, cols] = (u * scale + shift).astype(bf16).astype(f32)

        totals = {b: [0.0, 0.0] for b in range(nb)}

        def conv(h, cols):
            lo, hi = par[m, 2, h : h + 1, cols], par[m, 3, h : h + 1, cols]
            k1, kb = 0.5 * vec[5:6, cols], 0.5 * vec[7:8, cols]
            first = second = jnp.zeros((8, LANES), f32)
            for r in range(0, DIL, ROWS):
                at = h * DIL + r
                half = (
                    lo * n_s[at - DIL : at - DIL + ROWS, cols]
                    + k1 * n_s[at : at + ROWS, cols]
                    + hi * n_s[at + DIL : at + DIL + ROWS, cols]
                    + kb
                )
                if h == 1:
                    edge_ref[m, r : r + ROWS, cols] = half
                elif h == 2 * nb + 2:
                    edge_ref[m, DIL + r : DIL + r + ROWS, cols] = half
                else:
                    d_ref[m, at - BLK : at - BLK + ROWS, cols] = half
                    v = half + half * jnp.tanh(half)
                    first = first + fold_rows(v)
                    second = second + fold_rows(v * v)
            if 2 <= h < 2 * nb + 2:
                total = totals[h // 2 - 1]
                total[0] = total[0] + first
                total[1] = total[1] + second

        work = [functools.partial(normed, *t) for t in tiles_of(range(2 * nb + 4))]
        work += [functools.partial(conv, *t) for t in tiles_of(range(1, 2 * nb + 3))]
        weave(project(jnp.minimum(m + 1, micro - 1), 1 - slot), work)
        for b, total in totals.items():
            for k, val in enumerate(total):
                val = jnp.sum(row_sum(val), axis=1, keepdims=True)
                row = jnp.where(lane == (m * nb + b) * KINDS + k, val, row)
        return row

    seg = Segments(seg_ref, me_ref, micro, nb, stats_ref.shape[0])
    tab[0], tab[1] = seg.norm(stats_ref[:, 0, :])
    for m in range(micro):
        for o in range(nb + 2):
            scale = seg.pick(tab.at[1], m, o) * g1
            par[m, 0, o : o + 1, :] = scale
            par[m, 1, o : o + 1, :] = b1 - seg.pick(tab.at[0], m, o) * scale
        for h in range(1, 2 * nb + 3):
            lo, hi = seg.taps(vec, m, h)
            par[m, 2, h : h + 1, :] = 0.5 * lo
            par[m, 3, h : h + 1, :] = 0.5 * hi
    for step in project(0, 0):
        step()
    row = loop(micro, body, jnp.zeros((1, 128), f32))
    out_stats[...] = jnp.broadcast_to(row[None], out_stats.shape)


def depth(me, lengths, stats, feats, near, far, w_in, vec):
    micro, frames, _ = feats.shape
    return pl.pallas_call(
        depth_kernel,
        out_shape=(
            jax.ShapeDtypeStruct((micro, frames, HW), f32),
            jax.ShapeDtypeStruct((micro, 2 * DIL, HW), f32),
            jax.ShapeDtypeStruct(stats.shape, f32),
        ),
        in_specs=[smem(), smem()] + [vmem()] * 6,
        out_specs=(vmem(),) * 3,
        scratch_shapes=[
            pltpu.VMEM((2, SEGS, 128), f32),
            pltpu.VMEM((micro, 4, 8, HW), f32),
            pltpu.VMEM((2, frames + 2 * BLK, HW), f32),
            pltpu.VMEM((frames + 2 * BLK, HW), f32),
        ],
        compiler_params=pltpu.CompilerParams(vmem_limit_bytes=DEPTH_MIB * MIB),
        name="depth",
    )(me, lengths, stats, feats, near, far, w_in, vec)


def head_kernel(
    me_ref,
    seg_ref,
    stats_ref,
    d_ref,
    x_ref,
    enc_ref,
    dy_ref,
    own_ref,
    other_ref,
    w_rs,
    w_mask,
    w_dect,
    vec,
    block_ref,
    wave_own_ref,
    wave_other_ref,
    ds_ref,
    out_stats,
    g_rs,
    g_mask,
    g_dec,
    g_vec,
    tab,
    par,
    sums,
    ends,
    n2_s,
    v_s,
    sd_s,
    z_s,
    slope_s,
    dys_s,
    q_s,
    gm_s,
    e_s,
    dq_s,
    dz_s,
    dn2_s,
    dw_s,
    wave_s,
    block_s,
    sems,
):
    micro, frames, _ = d_ref.shape
    nb = frames // BLK
    halves = 2 * nb
    for ref in (g_rs, g_mask, g_dec, g_vec):
        ref[...] = jnp.zeros_like(ref)
    core = me_ref[0] % 2
    ours = pl.ds(pl.multiple_of(core * frames, BLK), frames)
    lane = lax.broadcasted_iota(jnp.int32, (1, 128), 1)
    seg = Segments(seg_ref, me_ref, micro, nb, stats_ref.shape[0])
    tab[0], tab[1] = seg.norm(stats_ref[:, 0, :])
    for m in range(micro):
        means = [seg.pick(tab.at[0], m, o) for o in range(nb + 1)]
        factors = [seg.pick(tab.at[1], m, o) for o in range(nb + 1)]
        for h in range(halves):
            o = 1 + h // 2
            scale = factors[o] * (1.0 + vec[2:3, :])
            lo, hi = seg.taps(vec, m, h + 2)
            rows = (
                scale,
                vec[3:4, :] - means[o] * scale,
                jnp.broadcast_to(means[o], (1, HW)),
                jnp.broadcast_to(factors[o], (1, HW)),
                vec[5:6, :] + lo + hi,
            )
            for k, v in enumerate(rows):
                par[m, k, h : h + 1, :] = v

    def leave(m):
        return pltpu.make_async_copy(block_s.at[m], block_ref.at[m], sems.at[m])

    def norm_steps(m, slot):
        def step(h, cols):
            scale, shift = par[m, 0, h : h + 1, cols], par[m, 1, h : h + 1, cols]
            s0 = s1 = c0 = c1 = jnp.zeros((8, LANES), f32)
            for r in range(h * DIL, (h + 1) * DIL, ROWS):
                rows = slice(r, r + ROWS)
                half = d_ref[m, rows, cols]
                v, sd = slope_parts(half, jnp.tanh(half))
                n2_s[slot, rows, cols] = (v * scale + shift).astype(bf16)
                v_s[slot, rows, cols] = v
                sd_s[slot, rows, cols] = sd
                cv = v * sd
                s0 = s0 + fold_rows(sd)
                s1 = s1 + fold_rows(sd * half)
                c0 = c0 + fold_rows(cv)
                c1 = c1 + fold_rows(cv * half)
            for k, v in enumerate((s0, s1, c0, c1)):
                sums[slot, k, h : h + 1, cols] = row_sum(v)

        return [functools.partial(step, *t) for t in tiles_of(range(halves))]

    def end_steps(m, slot):
        def step(h, cols):
            sum_d = sum_dv = a0 = a1 = jnp.zeros((8, LANES), f32)
            for r in range(h * DIL, (h + 1) * DIL, ROWS):
                rows = slice(r, r + ROWS)
                dn2 = dn2_s[rows, cols]
                a = dn2 * sd_s[slot, rows, cols]
                sum_d = sum_d + fold_rows(dn2)
                sum_dv = sum_dv + fold_rows(dn2 * v_s[slot, rows, cols])
                a0 = a0 + fold_rows(a)
                a1 = a1 + fold_rows(a * d_ref[m, rows, cols])
            for k, v in enumerate((sum_d, sum_dv, a0, a1)):
                ends[k, h : h + 1, cols] = row_sum(v)

        return [functools.partial(step, *t) for t in tiles_of(range(halves))]

    def end_row(m, at, slot, row, valid):
        scale, _, mean, factor, kappa = [par[m, k, 0:halves, :] for k in range(5)]
        s0, s1, c0, c1 = [sums[slot, k, 0:halves, :] for k in range(4)]
        sum_d, sum_dv, a0, a1 = [ends[k, 0:halves, :] for k in range(4)]
        g1, g2 = 1.0 + vec[0:1, :], 1.0 + vec[2:3, :]
        gain = (sum_dv - mean * sum_d) * factor
        g_vec[2:3, :] += jnp.where(valid, row_sum(gain), 0.0)
        g_vec[3:4, :] += jnp.where(valid, row_sum(sum_d), 0.0)
        vw = g1 * kappa
        delta = vec[7:8, :] + vec[1:2, :] * kappa
        a0, a1 = 0.5 * a0 * scale, a1 * scale
        s0, s1 = 0.5 * s0 * factor, s1 * factor
        c0 = 0.5 * c0 * factor * factor - mean * factor * s0
        c1 = c1 * factor * factor - mean * factor * s1
        vals = (
            sum_d * g2,
            gain * g2,
            vw * a0,
            vw * s0,
            vw * c0,
            a1 - delta * a0,
            s1 - delta * s0,
            c1 - delta * c0,
        )
        for k, val in enumerate(vals):
            val = jnp.sum(val, axis=1, keepdims=True)
            for b in range(nb):
                two = val[2 * b : 2 * b + 1, :] + val[2 * b + 1 : 2 * b + 2, :]
                row = jnp.where(lane == at + b * KINDS + k, two, row)
        return row

    def body(m, slot, row):
        later, before = min(m + 1, micro - 1), max(m - 1, 0)
        own, other = own_ref[m, :, ours], other_ref[m, :, ours]
        dw_s[slot, 0] = jnp.where(core == 0, own, other)
        dw_s[slot, 1] = jnp.where(core == 0, other, own)
        ahead = norm_steps(later, 1 - slot)

        def skip():
            rows = slice(0, frames)
            ys = mm(n2_s[slot, rows, :], w_rs[...])
            block_s[m, rows, :] = (x_ref[m, rows, :].astype(f32) + ys[:, 0:B]).astype(bf16)
            half = 0.5 * ys[:, B : B + SC]
            z, slope = slope_parts(half, jnp.tanh(half))
            leave(m).start()
            z_s[rows, :] = z.astype(bf16)
            slope_s[rows, :] = slope

        def logits(k, c):
            cols = slice(k * N + c, k * N + c + HALF_W)
            q_s[k, :, c : c + HALF_W] = mm(z_s[...], w_mask[:, cols])

        def back(k, c):
            cols = slice(k * N + c, k * N + c + HALF_W)
            gm_s[k, :, c : c + HALF_W] = mm_rows(dw_s[slot, k], w_dect[:, cols])

        def masked(k, h, cols):
            for r in range(h * DIL, (h + 1) * DIL, ROWS):
                rows = slice(r, r + ROWS)
                t = jnp.tanh(q_s[k, rows, cols])
                pe = (0.5 * t + 0.5) * enc_ref[m, rows, cols].astype(f32)
                e_s[k, rows, cols] = pe.astype(bf16)
                dq_s[k, rows, cols] = (gm_s[k, rows, cols] * (pe * (1.0 - t))).astype(bf16)

        def wave(k):
            cols = slice(k * N, (k + 1) * N)
            wave_s[k] = (2.0 * mm_t(w_dect[:, cols], e_s[k])).astype(bf16)

        def gated(k):
            cols = slice(k * N, (k + 1) * N)
            rows = slice(0, frames)
            part = mm_t(dq_s[k, rows, :], w_mask[:, cols])
            dz_s[rows, :] = part if k == 0 else dz_s[rows, :] + part

        def dec_grad(k):
            cols = slice(k * N, (k + 1) * N)
            g_dec[:, cols] += mm(dw_s[slot, k], e_s[k])

        def mask_grad(k, c):
            cols = slice(k * N + c, k * N + c + HALF_W)
            g_mask[:, cols] += mm_rows(z_s[...], dq_s[k, :, c : c + HALF_W])

        def norm_back(c):
            dn2_s[:, c : c + HALF_W] = mm_t(dys_s[...], w_rs[c : c + HALF_W, :])

        def out_grad(c):
            g_rs[:, c : c + HALF_W] += mm_rows(dys_s[...], n2_s[slot, :, c : c + HALF_W])

        part = functools.partial
        wide = range(0, HW, HALF_W)
        third = len(ahead) // 3

        def ups(k):
            return [part(logits, k, c) for c in wide] + [part(back, k, c) for c in wide]

        def elementwise(k):
            return [part(masked, k, *t) for t in tiles_of(range(halves))]

        def downs(k):
            return (
                [part(gated, k)]
                + [part(mask_grad, k, c) for c in wide]
                + [part(wave, k), part(dec_grad, k)]
            )

        weave([skip], end_steps(before, 1 - slot))
        row = end_row(before, (m - 1) * nb * KINDS, 1 - slot, row, m > 0)
        weave(ups(0), ahead[:third])
        weave(ups(1), elementwise(0))
        weave(downs(0), elementwise(1))
        weave(downs(1), ahead[third : 2 * third])
        wave_own_ref[m] = jnp.where(core == 0, wave_s[0], wave_s[1])
        wave_other_ref[m] = jnp.where(core == 0, wave_s[1], wave_s[0])
        ds = (dz_s[...] * slope_s[...]).astype(bf16)
        ds_ref[m] = ds
        dys_s[:, 0:B] = dy_ref[m]
        dys_s[:, B : B + SC] = ds
        weave([part(norm_back, c) for c in wide] + [part(out_grad, c) for c in wide], ahead[2 * third :])
        return row

    for step in norm_steps(0, 0):
        step()
    row = jnp.zeros((1, 128), f32)
    for m in range(micro):
        row = body(m, m % 2, row)
    last = micro - 1
    for step in end_steps(last, last % 2):
        step()
    row = end_row(last, last * nb * KINDS, last % 2, row, True)
    for m in range(micro):
        leave(m).wait()
    out_stats[...] = jnp.broadcast_to(row[None], out_stats.shape)


def head(me, lengths, stats, d, feats, enc, dy, own, other, w_rs, w_mask, w_dect, vec):
    micro, frames, _ = feats.shape
    outs = (
        (feats.shape, bf16),
        ((micro, L, frames), bf16),
        ((micro, L, frames), bf16),
        ((micro, frames, SC), bf16),
        (stats.shape, f32),
        ((B + SC, HW), f32),
        ((SC, C * N), f32),
        ((L, C * N), f32),
        ((8, HW), f32),
    )
    return pl.pallas_call(
        head_kernel,
        in_specs=[smem(), smem()] + [vmem()] * 11,
        out_specs=(pl.BlockSpec(memory_space=pl.ANY),) + (vmem(),) * (len(outs) - 1),
        scratch_shapes=[
            pltpu.VMEM((2, SEGS, 128), f32),
            pltpu.VMEM((micro, 5, 8, HW), f32),
            pltpu.VMEM((2, 4, 8, HW), f32),
            pltpu.VMEM((4, 8, HW), f32),
            pltpu.VMEM((2, frames, HW), bf16),
            pltpu.VMEM((2, frames, HW), f32),
            pltpu.VMEM((2, frames, HW), f32),
            pltpu.VMEM((frames, SC), bf16),
            pltpu.VMEM((frames, SC), f32),
            pltpu.VMEM((frames, B + SC), bf16),
            pltpu.VMEM((C, frames, N), f32),
            pltpu.VMEM((C, frames, N), f32),
            pltpu.VMEM((C, frames, N), bf16),
            pltpu.VMEM((C, frames, N), bf16),
            pltpu.VMEM((frames, SC), f32),
            pltpu.VMEM((frames, HW), f32),
            pltpu.VMEM((2, C, L, frames), bf16),
            pltpu.VMEM((C, L, frames), bf16),
            pltpu.VMEM(feats.shape, bf16),
            pltpu.SemaphoreType.DMA((micro,)),
        ],
        out_shape=tuple(jax.ShapeDtypeStruct(s, t) for s, t in outs),
        compiler_params=pltpu.CompilerParams(vmem_limit_bytes=HEAD_MIB * MIB),
        name="head",
    )(me, lengths, stats, d, feats, enc, dy, own, other, w_rs, w_mask, w_dect, vec)


def back_means(seg, stats):
    v = seg.means(stats)
    w = [v] + [pltpu.roll(v, 128 - k, 1) for k in range(1, KINDS)]
    p2, q2 = w[0], w[1]
    return p2, q2, w[2] - p2 * w[3] - q2 * w[4], w[5] - p2 * w[6] - q2 * w[7]


def input_kernel(
    me_ref,
    seg_ref,
    stats1_ref,
    stats2_ref,
    stats3_ref,
    d_ref,
    edge_ref,
    x_ref,
    dy_ref,
    dy_near,
    dy_far,
    ds_ref,
    ds_near,
    ds_far,
    w_in,
    w_rs,
    vec,
    feats_ref,
    g_in,
    g_vec,
    tab,
    par2,
    par1,
    col_s,
    dn2_s,
    dd_s,
    a_s,
    da_s,
    feats_s,
    sems,
):
    micro, frames, _ = d_ref.shape
    nb = frames // BLK
    halves = 2 * nb
    part = functools.partial
    for ref in (g_in, g_vec):
        ref[...] = jnp.zeros_like(ref)
    even = me_ref[0] % 2 == 0
    halo = slice(BLK, BLK + DIL)
    g1, g2 = 1.0 + vec[0:1, :], 1.0 + vec[2:3, :]
    seg = Segments(seg_ref, me_ref, micro, nb, stats1_ref.shape[0])
    tables = seg.norm(stats1_ref[:, 0, :]) + seg.norm(stats2_ref[:, 0, :])
    for k, table in enumerate(tables + back_means(seg, stats3_ref[:, 0, :])):
        tab[k] = table
    for m in range(micro):
        mean1, factor1, mean2, factor2, p2, q2, p1, q1 = [
            [seg.pick(tab.at[k], m, o) for o in range(nb + 2)] for k in range(8)
        ]
        for o in range(nb + 2):
            slope = 0.5 * factor2[o] * factor2[o] * q2[o]
            shift = 0.5 * factor2[o] * p2[o] - slope * mean2[o]
            rows = ((0.5 * factor2[o]) * g2, slope, shift)
            for k, v in enumerate(rows):
                par2[m, k, o : o + 1, :] = jnp.broadcast_to(v, (1, HW))
        for b in range(nb):
            o = b + 1
            scale = factor1[o] * g1
            slope = 0.5 * factor1[o] * factor1[o] * q1[o]
            rows = (
                scale,
                vec[1:2, :] - mean1[o] * scale,
                slope,
                0.5 * factor1[o] * p1[o] - slope * mean1[o],
                mean1[o],
                factor1[o],
                vec[4:5, :] * seg.same[m][o],
                vec[6:7, :] * seg.same[m][o - 1],
                seg.same[m][o],
                seg.same[m][o - 1],
            )
            for k, v in enumerate(rows):
                par1[m, k, b : b + 1, :] = jnp.broadcast_to(v, (1, HW))

    def project(m, slot):
        def side(at, first):
            near = jnp.concatenate([dy_near[m, halo, :], ds_near[m]], axis=1)
            far = jnp.concatenate([dy_far[m, halo, :], ds_far[m]], axis=1)
            dn2_s[at : at + DIL, :] = mm_t(jnp.where(even == first, far, near), w_rs[...])

        def main(c):
            dys = jnp.concatenate([dy_ref[m], ds_ref[m]], axis=1)
            dn2_s[DIL : DIL + frames, c : c + HALF_W] = mm_t(dys, w_rs[c : c + HALF_W, :])

        def hidden(c):
            a_s[slot, :, c : c + HALF_W] = mm(x_ref[m], w_in[:, c : c + HALF_W])

        wide = range(0, HW, HALF_W)
        return (
            [part(main, c) for c in wide]
            + [part(side, 0, True), part(side, DIL + frames, False)]
            + [part(hidden, c) for c in wide]
        )

    def depth_steps(m):
        def step(h, cols):
            o = (h + 1) // 2
            scale, slope, shift = [par2[m, k, o : o + 1, cols] for k in range(3)]
            total = jnp.zeros((8, LANES), f32)
            for r in range(0, DIL, ROWS):
                at = h * DIL + r
                if h == 0:
                    half = edge_ref[m, r : r + ROWS, cols]
                elif h == halves + 1:
                    half = edge_ref[m, DIL + r : DIL + r + ROWS, cols]
                else:
                    half = d_ref[m, at - DIL : at - DIL + ROWS, cols]
                v, sd = slope_parts(half, jnp.tanh(half))
                rows = slice(at, at + ROWS)
                dd = (sd * (dn2_s[rows, cols] * scale - v * slope - shift)).astype(bf16).astype(f32)
                dd_s[rows, cols] = dd
                total = total + fold_rows(dd)
            col_s[h : h + 1, cols] = row_sum(total)

        return [part(step, *t) for t in tiles_of(range(halves + 2))]

    def hidden_steps(m, slot):
        def step(h, cols):
            b = h // 2
            scale, shift, slope, base, mean, factor, k0, k2, hi, lo = [
                par1[m, k, b : b + 1, cols] for k in range(10)
            ]
            k1 = vec[5:6, cols]
            if h % 2 == 0:
                k0, hi = vec[4:5, cols], 1.0
            else:
                k2, lo = vec[6:7, cols], 1.0
            half_scale = 0.5 * scale
            s0 = s1 = s2 = jnp.zeros((8, LANES), f32)
            for r in range(h * DIL, (h + 1) * DIL, ROWS):
                prev, here, nxt = [dd_s[r + q * DIL : r + q * DIL + ROWS, cols] for q in range(3)]
                half = a_s[slot, r : r + ROWS, cols]
                u, su = slope_parts(half, jnp.tanh(half))
                n1 = (u * scale + shift).astype(bf16).astype(f32)
                s0 = s0 + fold_rows(nxt * n1)
                s1 = s1 + fold_rows(here * n1)
                s2 = s2 + fold_rows(prev * n1)
                dn1 = k1 * here + k0 * nxt + k2 * prev
                du = dn1 * half_scale - u * slope - base
                da_s[r : r + ROWS, cols] = (du * su).astype(bf16)
            s0, s1, s2 = [row_sum(v) for v in (s0, s1, s2)]
            prev, here, nxt = [col_s[h + q : h + q + 1, cols] for q in range(3)]
            dn1 = k1 * here + k0 * nxt + k2 * prev
            dn1_u = (k1 * s1 + k0 * s0 + k2 * s2 - shift * dn1) / scale
            rows = (
                (0, (dn1_u - mean * dn1) * factor),
                (1, dn1),
                (4, s0 * hi),
                (5, s1),
                (6, s2 * lo),
                (7, here),
            )
            for k, v in rows:
                g_vec[k : k + 1, cols] += v

        return [part(step, *t) for t in tiles_of(range(halves))]

    def last_steps(m):
        def weight(c):
            g_in[:, c : c + HALF_W] += mm_rows(x_ref[m], da_s[:, c : c + HALF_W])

        def feats(r):
            rows = slice(r, r + BLK)
            grad = dy_ref[m, rows, :].astype(f32) + 2.0 * mm_t(da_s[rows, :], w_in[...])
            feats_s[m, rows, :] = grad.astype(bf16)

        return [part(weight, c) for c in range(0, HW, HALF_W)] + [
            part(feats, r) for r in range(0, frames, BLK)
        ]

    def leave(m):
        return pltpu.make_async_copy(feats_s.at[m], feats_ref.at[m], sems.at[m])

    def body(m, slot, carry):
        run(project(m, 0) + depth_steps(m) + hidden_steps(m, 0) + last_steps(m))
        leave(m).start()
        return carry

    lax.fori_loop(0, micro, lambda m, c: body(m, 0, c), 0)
    for m in range(micro):
        leave(m).wait()


def input_grad(me, lengths, stats, d, edge, feats, dy, near, far, ds, ds_near, ds_far, w_in, w_rs, vec):
    micro, frames, _ = d.shape
    return pl.pallas_call(
        input_kernel,
        out_shape=(
            jax.ShapeDtypeStruct(feats.shape, bf16),
            jax.ShapeDtypeStruct((B, HW), f32),
            jax.ShapeDtypeStruct((8, HW), f32),
        ),
        in_specs=[smem(), smem()] + [vmem()] * 15,
        out_specs=(pl.BlockSpec(memory_space=pl.ANY), vmem(), vmem()),
        scratch_shapes=[
            pltpu.VMEM((8, SEGS, 128), f32),
            pltpu.VMEM((micro, 3, 8, HW), f32),
            pltpu.VMEM((micro, 10, 8, HW), f32),
            pltpu.VMEM((8, HW), f32),
            pltpu.VMEM((frames + 2 * DIL, HW), f32),
            pltpu.VMEM((frames + 2 * DIL, HW), f32),
            pltpu.VMEM((2, frames, HW), f32),
            pltpu.VMEM((frames, HW), bf16),
            pltpu.VMEM(feats.shape, bf16),
            pltpu.SemaphoreType.DMA((micro,)),
        ],
        compiler_params=pltpu.CompilerParams(vmem_limit_bytes=INPUT_MIB * MIB),
        name="input_grad",
    )(me, lengths, *stats, d, edge, feats, dy, near, far, ds, ds_near, ds_far, w_in, w_rs, vec)


def pack_kernel(pos_ref, g_in, g_rs, g_mask, g_dec, vec_a, vec_b, keep_ref, send_ref, t, out, wd):
    for k in range(4):
        cols = slice(128 * k, 128 * k + 128)
        t[pl.ds(R_IN + k, 128, stride=4), :] = g_in[:, cols]
        for c in range(C):
            t[pl.ds(R_MASK + 512 * c + k, 128, stride=4), :] = g_mask[
                :, 512 * c + 128 * k : 512 * c + 128 * k + 128
            ]
        t[pl.ds(R_VEC + k, 8, stride=4), :] = vec_a[:, cols] + vec_b[:, cols]
    t[R_RES : R_RES + 512, :] = g_rs[0:128, :].T
    t[R_SKIP : R_SKIP + 512, :] = g_rs[128:256, :].T
    wd[...] = jnp.concatenate([g_dec[...], jnp.zeros((128 - L, C * N), f32)], axis=0).T
    part = lax.broadcasted_iota(jnp.int32, (64, 128), 1) // L
    for c in range(C):
        rows = jnp.zeros((64, 128), f32)
        for s in range(8):
            piece = pltpu.roll(wd[pl.ds(512 * c + s, 64, stride=8), :], L * s, 1)
            rows = jnp.where(part == s, piece, rows)
        t[R_DEC + 64 * c : R_DEC + 64 * c + 64, :] = rows
    out[...] = jnp.zeros_like(out)
    for i in range(NCH):
        start = pl.multiple_of(pos_ref[i] * 8, 8)
        out[pl.ds(start, 8), :] = t[8 * i : 8 * i + 8, :]
    half = keep_ref.shape[0]
    keep_ref[...] = out[0:half, :]
    send_ref[...] = out[half : 2 * half, :].astype(bf16)


def pack(pos, g_in, g_rs, g_mask, g_dec, vec_a, vec_b, rows):
    return pl.pallas_call(
        pack_kernel,
        out_shape=(
            jax.ShapeDtypeStruct((rows // 2, 128), f32),
            jax.ShapeDtypeStruct((rows // 2, 128), bf16),
        ),
        in_specs=[smem()] + [vmem()] * 6,
        out_specs=(vmem(), vmem()),
        scratch_shapes=[
            pltpu.VMEM((ROWS_ALL, 128), f32),
            pltpu.VMEM((rows, 128), f32),
            pltpu.VMEM((C * N, 128), f32),
        ],
        compiler_params=pltpu.CompilerParams(vmem_limit_bytes=16 * MIB),
        name="pack",
    )(pos, g_in, g_rs, g_mask, g_dec, vec_a, vec_b)


def fold_kernel(n_got, n_next, *refs):
    keep_ref, got = refs[0], refs[1 : 1 + n_got]
    outs = refs[1 + n_got :]
    total = keep_ref[...]
    for g in got:
        total = total + g[...].astype(f32)
    size = total.shape[0] // n_next
    outs[0][...] = total[0:size, :]
    for q in range(1, n_next):
        outs[q][...] = total[q * size : (q + 1) * size, :].astype(bf16)


def fold(keep, got, n_next):
    size = keep.shape[0] // n_next
    outs = [jax.ShapeDtypeStruct((size, 128), f32)]
    outs += [jax.ShapeDtypeStruct((size, 128), bf16)] * (n_next - 1)
    return pl.pallas_call(
        functools.partial(fold_kernel, len(got), n_next),
        out_shape=tuple(outs),
        in_specs=[vmem()] * (1 + len(got)),
        out_specs=tuple(vmem() for _ in outs),
        compiler_params=pltpu.CompilerParams(vmem_limit_bytes=8 * MIB),
        name="fold",
    )(keep, *got)


def adam_kernel(n_got, count_ref, *refs):
    keep_ref, got = refs[0], refs[1 : 1 + n_got]
    master_ref, one_ref, two_ref, new_master, new_one, new_two, buf = refs[1 + n_got :]
    total = keep_ref[...]
    for g in got:
        total = total + g[...].astype(f32)
    buf[...] = total
    slots = master_ref.shape[0]
    used = lax.broadcasted_iota(jnp.int32, (slots, 128), 0) < count_ref[0]
    for j in range(8):
        cols = slice(128 * j, 128 * j + 128)
        grad = buf[pl.ds(j, slots, stride=8), :]
        master = master_ref[:, cols]
        one = beta_one * one_ref[:, cols] + (1.0 - beta_one) * grad
        two = beta_two * two_ref[:, cols] + (1.0 - beta_two) * grad * grad
        unbias_one = one / (1.0 - beta_one**STEP)
        unbias_two = two / (1.0 - beta_two**STEP)
        new = master - learn_rate * (
            unbias_one / (jnp.sqrt(unbias_two) + adam_eps) + weight_decay * master
        )
        new_master[:, cols] = jnp.where(used, new, 0.0)
        new_one[:, cols] = jnp.where(used, one, 0.0)
        new_two[:, cols] = jnp.where(used, two, 0.0)


def adam(count, keep, got, master, one, two):
    out = jax.ShapeDtypeStruct(master.shape, f32)
    return pl.pallas_call(
        functools.partial(adam_kernel, len(got)),
        out_shape=(out, out, out),
        in_specs=[smem()] + [vmem()] * (4 + len(got)),
        out_specs=(vmem(), vmem(), vmem()),
        scratch_shapes=[pltpu.VMEM(keep.shape, f32)],
        compiler_params=pltpu.CompilerParams(vmem_limit_bytes=4 * MIB),
        name="adam",
    )(count, keep, *got, master, one, two)


def local(n_tm, n_src, feats, encoded, seg_lengths, owners, master, moment_one, moment_two, out_cot, wave_cot):
    n_dev = n_tm * n_src
    me = lax.axis_index(AXES)
    core = lax.axis_index("src")
    micro, frames, _ = feats.shape
    nb = frames // BLK
    slots = master.shape[0]


    across = [(i, i + 1) for i in range(1, n_dev - 1, 2)]
    across = across + [(j, i) for i, j in across]

    def ends(at_end, *arrays):
        size = [jnp.where(at_end, v.shape[1] - w, 0) for v, w in arrays]
        rows = [lax.dynamic_slice_in_dim(v, at, w, axis=1) for (v, w), at in zip(arrays, size)]
        return rows[0] if len(rows) == 1 else jnp.concatenate(rows, axis=1)

    owner_ids = owners[:, 0]
    order = jnp.arange(NCH, dtype=jnp.int32)
    earlier = (owner_ids[:, None] == owner_ids[None, :]) & (order[None, :] < order[:, None])
    rank = jnp.sum(earlier.astype(jnp.int32), axis=1)
    pos = relative_block(owner_ids, me, n_dev) * slots + rank
    count = jnp.sum((owner_ids == me).astype(jnp.int32)).reshape(1)
    here = me.astype(jnp.int32).reshape(1)

    cot = jnp.transpose(wave_cot[:, 0], (0, 2, 1))

    def sides(x, dy, other):
        halo = (x, BLK), (dy, DIL)
        return ends(core == 0, *halo), ends(core == 1, *halo), other

    parts, (pos, here, count), (near, far, cot_other) = gather_tiles(
        to_tiles(master), n_dev, (pos, here, count), (feats, out_cot, cot), sides
    )
    near = swap(near, 1, n_dev)
    far = lax.ppermute(far, AXES, across)
    cot_other = swap(cot_other, 1, n_dev)

    w_in, w_rs, w_mask, w_dect, vec, stats = unpack(pos, parts, feats, n_dev)
    stats1 = share_sums(stats, n_dev)
    stats1, near, far, cot_other = lax.optimization_barrier((stats1, near, far, cot_other))
    d, edge, stats = depth(here, seg_lengths, stats1, feats, near, far, w_in, vec)
    stats2 = share_sums(stats, n_dev)
    block_out, wave_own, wave_other, ds, stats, g_rs, g_mask, g_dec, vec_a = head(
        here, seg_lengths, stats2, d, feats, encoded, out_cot, cot, cot_other, w_rs, w_mask, w_dect, vec
    )
    stats3 = share_sums(stats, n_dev)
    ds_near = swap(ends(core == 0, (ds, DIL)), 1, n_dev)
    ds_far = lax.ppermute(ends(core == 1, (ds, DIL)), AXES, across)

    wave_got = swap(wave_other, 1, n_dev)
    waves = jnp.concatenate(
        [jnp.where(core == 0, wave_own, wave_got), jnp.where(core == 0, wave_got, wave_own)], axis=2
    )
    waves = jnp.transpose(waves, (0, 2, 1))[:, None]

    feats_grad, g_in, vec_b = input_grad(
        here, seg_lengths, (stats1, stats2, stats3), d, edge, feats, out_cot, near, far, ds, ds_near, ds_far, w_in, w_rs, vec
    )

    keep, send = pack(pos, g_in, g_rs, g_mask, g_dec, vec_a, vec_b, n_dev * slots * 8)
    received = [swap(send, 1, n_dev)]
    for bits in reversed(stages(n_dev)[:-1]):
        n_next = 1 << len(bits)
        keep, *sends = fold(keep, received, n_next)
        received = [swap(s, spread(bits, k + 1), n_dev) for k, s in enumerate(sends)]
    new_master, new_one, new_two = adam(count, keep, received, master, moment_one, moment_two)
    return block_out, feats_grad, waves, new_master, new_one, new_two


def solution(mesh):
    n_tm, n_src = mesh.shape["tm"], mesh.shape["src"]
    return jax.shard_map(
        functools.partial(local, n_tm, n_src),
        mesh=mesh,
        in_specs=(
            P(None, AXES, None),
            P(None, AXES, None),
            P(),
            P(),
            P(AXES, None),
            P(AXES, None),
            P(AXES, None),
            P(None, AXES, None),
            P(None, "src", "tm", None),
        ),
        out_specs=(
            P(None, AXES, None),
            P(None, AXES, None),
            P(None, "src", "tm", None),
            P(AXES, None),
            P(AXES, None),
            P(AXES, None),
        ),
        check_vma=False,
    )
```

```python
import functools

import jax
import jax.numpy as jnp
from jax import lax
from jax.experimental import pallas as pl
from jax.experimental.pallas import tpu as pltpu
from jax.sharding import PartitionSpec as P

N = 512
L = 16
B = 128
SC = 128
HW = 512
C = 2
DIL = 128
ROW = 1024
SEGS = 8
MICRO = 4
STEP = 10
NCH = 340
BLK = 256
KINDS = 8
CHUNK = 16
LANES, ROWS = 256, 16
HALF_W = 256

norm_eps = 1e-05
adam_eps = 1e-08
beta_one = 0.9
beta_two = 0.999
learn_rate = 0.2
weight_decay = 0.01

AXES = ("tm", "src")
f32 = jnp.float32
bf16 = jnp.bfloat16
MIB = 1024 * 1024
DEPTH_MIB = HEAD_MIB = INPUT_MIB = 20

R_IN, R_RES, R_SKIP, R_MASK, R_DEC, R_VEC = 0, 512, 1024, 1536, 2560, 2688
ROWS_ALL = 2720


def mm(a, b):
    return lax.dot_general(a, b, (((1,), (0,)), ((), ())), preferred_element_type=f32)


def mm_t(a, b):
    return lax.dot_general(a, b, (((1,), (1,)), ((), ())), preferred_element_type=f32)


def mm_rows(a, b):
    return lax.dot_general(a, b, (((0,), (0,)), ((), ())), preferred_element_type=f32)


def sigmoid(v):
    return 0.5 * jnp.tanh(0.5 * v) + 0.5


def fold_rows(v):
    return functools.reduce(lambda p, q: p + q, [v[i : i + 8, :] for i in range(0, v.shape[0], 8)])


def slope_parts(half, t):
    w = half * t
    return half + w, (1.0 + t) + (half - w * t)


def weave(first, second):
    steps = [((i + 0.5) / len(first), 0, i) for i in range(len(first))]
    steps += [((i + 0.5) / len(second), 1, i) for i in range(len(second))]
    for _, which, i in sorted(steps):
        (first, second)[which][i]()


def run(steps):
    for step in steps:
        step()


def tiles_of(halves):
    return [(h, slice(c, c + LANES)) for h in halves for c in range(0, HW, LANES)]


def loop(count, body, carry):
    def pair(i, carry):
        return body(2 * i + 1, 1, body(2 * i, 0, carry))

    return lax.fori_loop(0, count // 2, pair, carry)


def row_sum(v):
    return jnp.sum(v, axis=0, keepdims=True)


def vmem():
    return pl.BlockSpec(memory_space=pltpu.VMEM)


def smem():
    return pl.BlockSpec(memory_space=pltpu.SMEM)


def stages(n_dev):
    bits = n_dev.bit_length() - 1
    groups = []
    hi = bits - 1
    while hi >= 1:
        lo = max(1, hi - 1)
        groups.append(tuple(range(lo, hi + 1)))
        hi = lo - 1
    groups.append((0,))
    return groups


def spread(bits, k):
    return sum(((k >> j) & 1) << b for j, b in enumerate(bits))


def swap(value, mask, n_dev):
    return lax.ppermute(value, AXES, [(i, i ^ mask) for i in range(n_dev)])


def gather_tiles(tiles, n_dev, early, rows, sides):
    parts = [tiles]
    for k, bits in enumerate(stages(n_dev)[:-1]):
        if k == 1:
            parts, early, rows = lax.optimization_barrier((parts, early, rows))
        z = parts[0] if len(parts) == 1 else jnp.concatenate(parts, axis=0)
        parts = [z] + [swap(z, spread(bits, q), n_dev) for q in range(1, 1 << len(bits))]
    got, late = lax.optimization_barrier(([swap(z, 1, n_dev) for z in parts], sides(*rows)))
    return parts + got, early, late


def relative_block(owner, me, n_dev):
    q = owner ^ me
    index = jnp.zeros_like(q)
    size = 1
    for bits in stages(n_dev):
        digit = sum(((q >> b) & 1) << j for j, b in enumerate(bits))
        index = index + digit * size
        size = size << len(bits)
    return index


def share_sums(rows, n_dev):
    return lax.all_to_all(rows, AXES, 0, 0, tiled=True)


def tile_kernel(m_ref, out_ref, buf):
    slots = m_ref.shape[0]
    for j in range(8):
        buf[pl.ds(j, slots, stride=8), :] = m_ref[:, 128 * j : 128 * j + 128]
    out_ref[...] = buf[...].astype(bf16)


def to_tiles(master):
    slots = master.shape[0]
    return pl.pallas_call(
        tile_kernel,
        out_shape=jax.ShapeDtypeStruct((slots * 8, 128), bf16),
        in_specs=[vmem()],
        out_specs=vmem(),
        scratch_shapes=[pltpu.VMEM((slots * 8, 128), f32)],
        compiler_params=pltpu.CompilerParams(vmem_limit_bytes=4 * MIB),
        name="to_tiles",
    )(master)


def stat_rows(values, shape):
    lane = lax.broadcasted_iota(jnp.int32, shape, 1)
    row = jnp.zeros(shape, f32)
    for where, v in values.items():
        row = jnp.where(lane == where, v, row)
    return row


def unpack_kernel(n_parts, pos_ref, x_ref, *refs):
    parts, refs = refs[:n_parts], refs[n_parts:]
    w_in, w_rs, w_mask, w_dect, vec, stats, g, t, wd = refs
    size = parts[0].shape[0]
    for k, part in enumerate(parts):
        g[k * size : (k + 1) * size, :] = part[...].astype(f32)
    for i in range(NCH):
        start = pl.multiple_of(pos_ref[i] * 8, 8)
        t[8 * i : 8 * i + 8, :] = g[pl.ds(start, 8), :]
    for k in range(4):
        cols = slice(128 * k, 128 * k + 128)
        w_in[:, cols] = (0.5 * t[pl.ds(R_IN + k, 128, stride=4), :]).astype(bf16)
        for c in range(C):
            w_mask[:, 512 * c + 128 * k : 512 * c + 128 * k + 128] = (
                0.5 * t[pl.ds(R_MASK + 512 * c + k, 128, stride=4), :]
            ).astype(bf16)
        vec[:, cols] = t[pl.ds(R_VEC + k, 8, stride=4), :]
    w_rs[:, 0:128] = t[R_RES : R_RES + 512, :].astype(bf16)
    w_rs[:, 128:256] = t[R_SKIP : R_SKIP + 512, :].astype(bf16)
    part = lax.broadcasted_iota(jnp.int32, (64, 128), 1) // L
    for s in range(8):
        for c in range(C):
            rows = t[R_DEC + 64 * c : R_DEC + 64 * c + 64, :]
            rows = pltpu.roll(rows, (-L * s) % 128, 1)
            wd[pl.ds(512 * c + s, 64, stride=8), :] = jnp.where(part == 0, rows, 0.0)
    w_dect[...] = (0.5 * wd[...].T[0:L, :]).astype(bf16)
    micro, frames, _ = x_ref.shape
    nb = frames // BLK
    sums = {}
    for m in range(micro):
        for b in range(nb):
            half = mm(x_ref[m, b * BLK : (b + 1) * BLK, :], w_in[...])
            u = half + half * jnp.tanh(half)
            first = jnp.sum(jnp.sum(u, axis=0, keepdims=True), axis=1, keepdims=True)
            second = jnp.sum(jnp.sum(u * u, axis=0, keepdims=True), axis=1, keepdims=True)
            sums[(m * nb + b) * KINDS] = first
            sums[(m * nb + b) * KINDS + 1] = second
    row = stat_rows(sums, (1, 128))
    stats[...] = jnp.broadcast_to(row[None], stats.shape)


def unpack(pos, parts, feats, n_dev):
    outs = (
        jax.ShapeDtypeStruct((B, HW), bf16),
        jax.ShapeDtypeStruct((HW, B + SC), bf16),
        jax.ShapeDtypeStruct((SC, C * N), bf16),
        jax.ShapeDtypeStruct((L, C * N), bf16),
        jax.ShapeDtypeStruct((8, HW), f32),
        jax.ShapeDtypeStruct((n_dev, 1, 128), f32),
    )
    return pl.pallas_call(
        functools.partial(unpack_kernel, len(parts)),
        out_shape=outs,
        in_specs=[smem()] + [vmem()] * (1 + len(parts)),
        out_specs=tuple(vmem() for _ in outs),
        scratch_shapes=[
            pltpu.VMEM((len(parts) * parts[0].shape[0], 128), f32),
            pltpu.VMEM((ROWS_ALL, 128), f32),
            pltpu.VMEM((C * N, 128), f32),
        ],
        compiler_params=pltpu.CompilerParams(vmem_limit_bytes=16 * MIB),
        name="unpack",
    )(pos, feats, *parts)


class Segments:
    def __init__(self, seg_ref, me_ref, micro, nb, n_dev):
        self.seg_ref, self.micro, self.nb, self.n_dev = seg_ref, micro, nb, n_dev
        self.bounds, self.here, self.same = [], [], []
        for m in range(micro):
            bounds, total = [], 0
            for k in range(SEGS):
                total = total + seg_ref[m, k]
                bounds.append(total)
            here = []
            for o in range(-1, nb + 1):
                at = (me_ref[0] * nb + o) * BLK
                here.append(functools.reduce(lambda p, q: p + q, [jnp.where(at >= k, 1, 0) for k in bounds]))
            start, end = me_ref[0] * nb, me_ref[0] * nb + nb
            same = [jnp.where(p == q, 1.0, 0.0).astype(f32) for p, q in zip(here[:-1], here[1:])]
            same[0] = jnp.where(start > 0, same[0], 0.0)
            same[-1] = jnp.where(end < n_dev * nb, same[-1], 0.0)
            self.bounds.append(bounds)
            self.here.append([jnp.minimum(h, SEGS - 1) for h in here])
            self.same.append(same)
        lane = lax.broadcasted_iota(jnp.int32, (1, 128), 1)
        self.lane_micro = lane // (KINDS * nb)
        start = lax.broadcasted_iota(jnp.int32, (n_dev, 128), 0) * nb
        start = (start + (lax.broadcasted_iota(jnp.int32, (n_dev, 128), 1) // KINDS) % nb) * BLK
        self.ids = jnp.zeros((n_dev, 128), jnp.int32)
        for k in range(SEGS - 1):
            bound = self.by_micro([b[k] for b in self.bounds])
            self.ids = self.ids + jnp.where(start >= bound, 1, 0)
        lengths = self.rows([self.by_micro([seg_ref[m, k] for m in range(micro)]) for k in range(SEGS)])
        self.inverse = 1.0 / (lengths.astype(f32) * HW)

    def by_micro(self, values):
        out = jnp.full((1, 128), values[0], jnp.int32)
        for m in range(1, self.micro):
            out = jnp.where(self.lane_micro == m, values[m], out)
        return out

    def rows(self, values):
        at = lax.broadcasted_iota(jnp.int32, (SEGS, 128), 0)
        out = jnp.broadcast_to(values[0], (SEGS, 128))
        for k in range(1, SEGS):
            out = jnp.where(at == k, values[k], out)
        return out

    def means(self, stats):
        sums = self.rows(
            [row_sum(fold_rows(jnp.where(self.ids == k, stats, 0.0))) for k in range(SEGS)]
        )
        total = sums
        for b in range(1, self.nb):
            total = total + pltpu.roll(sums, 128 - b * KINDS, 1)
        return total * self.inverse

    def norm(self, stats):
        mean = self.means(stats)
        factor = lax.rsqrt(pltpu.roll(mean, 127, 1) - mean * mean + norm_eps)
        return mean, factor

    def pick(self, ref, m, o):
        at = m * self.nb * KINDS
        return ref[pl.ds(self.here[m][o], 1), :][:, at : at + 1]

    def taps(self, vec, m, h):
        k0, k2 = vec[4:5, :], vec[6:7, :]
        lo = k0 * self.same[m][h // 2 - 1] if h % 2 == 0 else k0
        hi = k2 if h % 2 == 0 else k2 * self.same[m][h // 2]
        return lo, hi


def depth_kernel(
    me_ref, seg_ref, stats_ref, x_ref, near_ref, far_ref, w_in, vec, d_ref, edge_ref, out_stats, tab, par, a_s, n_s
):
    micro, frames, _ = x_ref.shape
    nb = frames // BLK
    even = me_ref[0] % 2 == 0
    g1, b1 = 1.0 + vec[0:1, :], vec[1:2, :]
    lane = lax.broadcasted_iota(jnp.int32, (1, 128), 1)

    def project(m, slot):
        def side(at, first):
            near, far = near_ref[m, 0:BLK, :], far_ref[m, 0:BLK, :]
            a_s[slot, at : at + BLK, :] = mm(jnp.where(even == first, far, near), w_in[...])

        def main(c):
            cols = slice(c, c + HALF_W)
            a_s[slot, BLK : BLK + frames, cols] = mm(x_ref[m], w_in[:, cols])

        steps = [functools.partial(main, c) for c in range(0, HW, HALF_W)]
        return steps + [
            functools.partial(side, 0, True),
            functools.partial(side, BLK + frames, False),
        ]

    def body(m, slot, row):
        def normed(h, cols):
            o = h // 2
            scale, shift = par[m, 0, o : o + 1, cols], par[m, 1, o : o + 1, cols]
            for r in range(h * DIL, (h + 1) * DIL, ROWS):
                half = a_s[slot, r : r + ROWS, cols]
                u = half + half * jnp.tanh(half)
                n_s[r : r + ROWS, cols] = (u * scale + shift).astype(bf16).astype(f32)

        totals = {b: [0.0, 0.0] for b in range(nb)}

        def conv(h, cols):
            lo, hi = par[m, 2, h : h + 1, cols], par[m, 3, h : h + 1, cols]
            k1, kb = 0.5 * vec[5:6, cols], 0.5 * vec[7:8, cols]
            first = second = jnp.zeros((8, LANES), f32)
            for r in range(0, DIL, ROWS):
                at = h * DIL + r
                half = (
                    lo * n_s[at - DIL : at - DIL + ROWS, cols]
                    + k1 * n_s[at : at + ROWS, cols]
                    + hi * n_s[at + DIL : at + DIL + ROWS, cols]
                    + kb
                )
                if h == 1:
                    edge_ref[m, r : r + ROWS, cols] = half
                elif h == 2 * nb + 2:
                    edge_ref[m, DIL + r : DIL + r + ROWS, cols] = half
                else:
                    d_ref[m, at - BLK : at - BLK + ROWS, cols] = half
                    v = half + half * jnp.tanh(half)
                    first = first + fold_rows(v)
                    second = second + fold_rows(v * v)
            if 2 <= h < 2 * nb + 2:
                total = totals[h // 2 - 1]
                total[0] = total[0] + first
                total[1] = total[1] + second

        work = [functools.partial(normed, *t) for t in tiles_of(range(2 * nb + 4))]
        work += [functools.partial(conv, *t) for t in tiles_of(range(1, 2 * nb + 3))]
        weave(project(jnp.minimum(m + 1, micro - 1), 1 - slot), work)
        for b, total in totals.items():
            for k, val in enumerate(total):
                val = jnp.sum(row_sum(val), axis=1, keepdims=True)
                row = jnp.where(lane == (m * nb + b) * KINDS + k, val, row)
        return row

    seg = Segments(seg_ref, me_ref, micro, nb, stats_ref.shape[0])
    tab[0], tab[1] = seg.norm(stats_ref[:, 0, :])
    for m in range(micro):
        for o in range(nb + 2):
            scale = seg.pick(tab.at[1], m, o) * g1
            par[m, 0, o : o + 1, :] = scale
            par[m, 1, o : o + 1, :] = b1 - seg.pick(tab.at[0], m, o) * scale
        for h in range(1, 2 * nb + 3):
            lo, hi = seg.taps(vec, m, h)
            par[m, 2, h : h + 1, :] = 0.5 * lo
            par[m, 3, h : h + 1, :] = 0.5 * hi
    for step in project(0, 0):
        step()
    row = loop(micro, body, jnp.zeros((1, 128), f32))
    out_stats[...] = jnp.broadcast_to(row[None], out_stats.shape)


def depth(me, lengths, stats, feats, near, far, w_in, vec):
    micro, frames, _ = feats.shape
    return pl.pallas_call(
        depth_kernel,
        out_shape=(
            jax.ShapeDtypeStruct((micro, frames, HW), f32),
            jax.ShapeDtypeStruct((micro, 2 * DIL, HW), f32),
            jax.ShapeDtypeStruct(stats.shape, f32),
        ),
        in_specs=[smem(), smem()] + [vmem()] * 6,
        out_specs=(vmem(),) * 3,
        scratch_shapes=[
            pltpu.VMEM((2, SEGS, 128), f32),
            pltpu.VMEM((micro, 4, 8, HW), f32),
            pltpu.VMEM((2, frames + 2 * BLK, HW), f32),
            pltpu.VMEM((frames + 2 * BLK, HW), f32),
        ],
        compiler_params=pltpu.CompilerParams(vmem_limit_bytes=DEPTH_MIB * MIB),
        name="depth",
    )(me, lengths, stats, feats, near, far, w_in, vec)


def head_kernel(
    me_ref,
    seg_ref,
    stats_ref,
    d_ref,
    x_ref,
    enc_ref,
    dy_ref,
    own_ref,
    other_ref,
    w_rs,
    w_mask,
    w_dect,
    vec,
    block_ref,
    wave_own_ref,
    wave_other_ref,
    ds_ref,
    out_stats,
    g_rs,
    g_mask,
    g_dec,
    g_vec,
    tab,
    par,
    sums,
    ends,
    n2_s,
    v_s,
    sd_s,
    z_s,
    slope_s,
    dys_s,
    q_s,
    gm_s,
    e_s,
    dq_s,
    dz_s,
    dn2_s,
    dw_s,
    wave_s,
    block_s,
    sems,
):
    micro, frames, _ = d_ref.shape
    nb = frames // BLK
    halves = 2 * nb
    for ref in (g_rs, g_mask, g_dec, g_vec):
        ref[...] = jnp.zeros_like(ref)
    core = me_ref[0] % 2
    ours = pl.ds(pl.multiple_of(core * frames, BLK), frames)
    lane = lax.broadcasted_iota(jnp.int32, (1, 128), 1)
    seg = Segments(seg_ref, me_ref, micro, nb, stats_ref.shape[0])
    tab[0], tab[1] = seg.norm(stats_ref[:, 0, :])
    for m in range(micro):
        means = [seg.pick(tab.at[0], m, o) for o in range(nb + 1)]
        factors = [seg.pick(tab.at[1], m, o) for o in range(nb + 1)]
        for h in range(halves):
            o = 1 + h // 2
            scale = factors[o] * (1.0 + vec[2:3, :])
            lo, hi = seg.taps(vec, m, h + 2)
            rows = (
                scale,
                vec[3:4, :] - means[o] * scale,
                jnp.broadcast_to(means[o], (1, HW)),
                jnp.broadcast_to(factors[o], (1, HW)),
                vec[5:6, :] + lo + hi,
            )
            for k, v in enumerate(rows):
                par[m, k, h : h + 1, :] = v

    def leave(m):
        return pltpu.make_async_copy(block_s.at[m], block_ref.at[m], sems.at[m])

    def norm_steps(m, slot):
        def step(h, cols):
            scale, shift = par[m, 0, h : h + 1, cols], par[m, 1, h : h + 1, cols]
            s0 = s1 = c0 = c1 = jnp.zeros((8, LANES), f32)
            for r in range(h * DIL, (h + 1) * DIL, ROWS):
                rows = slice(r, r + ROWS)
                half = d_ref[m, rows, cols]
                v, sd = slope_parts(half, jnp.tanh(half))
                n2_s[slot, rows, cols] = (v * scale + shift).astype(bf16)
                v_s[slot, rows, cols] = v
                sd_s[slot, rows, cols] = sd
                cv = v * sd
                s0 = s0 + fold_rows(sd)
                s1 = s1 + fold_rows(sd * half)
                c0 = c0 + fold_rows(cv)
                c1 = c1 + fold_rows(cv * half)
            for k, v in enumerate((s0, s1, c0, c1)):
                sums[slot, k, h : h + 1, cols] = row_sum(v)

        return [functools.partial(step, *t) for t in tiles_of(range(halves))]

    def end_steps(m, slot):
        def step(h, cols):
            sum_d = sum_dv = a0 = a1 = jnp.zeros((8, LANES), f32)
            for r in range(h * DIL, (h + 1) * DIL, ROWS):
                rows = slice(r, r + ROWS)
                dn2 = dn2_s[rows, cols]
                a = dn2 * sd_s[slot, rows, cols]
                sum_d = sum_d + fold_rows(dn2)
                sum_dv = sum_dv + fold_rows(dn2 * v_s[slot, rows, cols])
                a0 = a0 + fold_rows(a)
                a1 = a1 + fold_rows(a * d_ref[m, rows, cols])
            for k, v in enumerate((sum_d, sum_dv, a0, a1)):
                ends[k, h : h + 1, cols] = row_sum(v)

        return [functools.partial(step, *t) for t in tiles_of(range(halves))]

    def end_row(m, at, slot, row, valid):
        scale, _, mean, factor, kappa = [par[m, k, 0:halves, :] for k in range(5)]
        s0, s1, c0, c1 = [sums[slot, k, 0:halves, :] for k in range(4)]
        sum_d, sum_dv, a0, a1 = [ends[k, 0:halves, :] for k in range(4)]
        g1, g2 = 1.0 + vec[0:1, :], 1.0 + vec[2:3, :]
        gain = (sum_dv - mean * sum_d) * factor
        g_vec[2:3, :] += jnp.where(valid, row_sum(gain), 0.0)
        g_vec[3:4, :] += jnp.where(valid, row_sum(sum_d), 0.0)
        vw = g1 * kappa
        delta = vec[7:8, :] + vec[1:2, :] * kappa
        a0, a1 = 0.5 * a0 * scale, a1 * scale
        s0, s1 = 0.5 * s0 * factor, s1 * factor
        c0 = 0.5 * c0 * factor * factor - mean * factor * s0
        c1 = c1 * factor * factor - mean * factor * s1
        vals = (
            sum_d * g2,
            gain * g2,
            vw * a0,
            vw * s0,
            vw * c0,
            a1 - delta * a0,
            s1 - delta * s0,
            c1 - delta * c0,
        )
        for k, val in enumerate(vals):
            val = jnp.sum(val, axis=1, keepdims=True)
            for b in range(nb):
                two = val[2 * b : 2 * b + 1, :] + val[2 * b + 1 : 2 * b + 2, :]
                row = jnp.where(lane == at + b * KINDS + k, two, row)
        return row

    def body(m, slot, row):
        later, before = min(m + 1, micro - 1), max(m - 1, 0)
        own, other = own_ref[m, :, ours], other_ref[m, :, ours]
        dw_s[slot, 0] = jnp.where(core == 0, own, other)
        dw_s[slot, 1] = jnp.where(core == 0, other, own)
        ahead = norm_steps(later, 1 - slot)

        def skip():
            rows = slice(0, frames)
            ys = mm(n2_s[slot, rows, :], w_rs[...])
            block_s[m, rows, :] = (x_ref[m, rows, :].astype(f32) + ys[:, 0:B]).astype(bf16)
            half = 0.5 * ys[:, B : B + SC]
            z, slope = slope_parts(half, jnp.tanh(half))
            leave(m).start()
            z_s[rows, :] = z.astype(bf16)
            slope_s[rows, :] = slope

        def logits(k, c):
            cols = slice(k * N + c, k * N + c + HALF_W)
            q_s[k, :, c : c + HALF_W] = mm(z_s[...], w_mask[:, cols])

        def back(k, c):
            cols = slice(k * N + c, k * N + c + HALF_W)
            gm_s[k, :, c : c + HALF_W] = mm_rows(dw_s[slot, k], w_dect[:, cols])

        def masked(k, h, cols):
            for r in range(h * DIL, (h + 1) * DIL, ROWS):
                rows = slice(r, r + ROWS)
                t = jnp.tanh(q_s[k, rows, cols])
                pe = (0.5 * t + 0.5) * enc_ref[m, rows, cols].astype(f32)
                e_s[k, rows, cols] = pe.astype(bf16)
                dq_s[k, rows, cols] = (gm_s[k, rows, cols] * (pe * (1.0 - t))).astype(bf16)

        def wave(k):
            cols = slice(k * N, (k + 1) * N)
            wave_s[k] = (2.0 * mm_t(w_dect[:, cols], e_s[k])).astype(bf16)

        def gated(k):
            cols = slice(k * N, (k + 1) * N)
            rows = slice(0, frames)
            part = mm_t(dq_s[k, rows, :], w_mask[:, cols])
            dz_s[rows, :] = part if k == 0 else dz_s[rows, :] + part

        def dec_grad(k):
            cols = slice(k * N, (k + 1) * N)
            g_dec[:, cols] += mm(dw_s[slot, k], e_s[k])

        def mask_grad(k, c):
            cols = slice(k * N + c, k * N + c + HALF_W)
            g_mask[:, cols] += mm_rows(z_s[...], dq_s[k, :, c : c + HALF_W])

        def norm_back(c):
            dn2_s[:, c : c + HALF_W] = mm_t(dys_s[...], w_rs[c : c + HALF_W, :])

        def out_grad(c):
            g_rs[:, c : c + HALF_W] += mm_rows(dys_s[...], n2_s[slot, :, c : c + HALF_W])

        part = functools.partial
        wide = range(0, HW, HALF_W)
        third = len(ahead) // 3

        def ups(k):
            return [part(logits, k, c) for c in wide] + [part(back, k, c) for c in wide]

        def elementwise(k):
            return [part(masked, k, *t) for t in tiles_of(range(halves))]

        def downs(k):
            return (
                [part(gated, k)]
                + [part(mask_grad, k, c) for c in wide]
                + [part(wave, k), part(dec_grad, k)]
            )

        weave([skip], end_steps(before, 1 - slot))
        row = end_row(before, (m - 1) * nb * KINDS, 1 - slot, row, m > 0)
        weave(ups(0), ahead[:third])
        weave(ups(1), elementwise(0))
        weave(downs(0), elementwise(1))
        weave(downs(1), ahead[third : 2 * third])
        wave_own_ref[m] = jnp.where(core == 0, wave_s[0], wave_s[1])
        wave_other_ref[m] = jnp.where(core == 0, wave_s[1], wave_s[0])
        ds = (dz_s[...] * slope_s[...]).astype(bf16)
        ds_ref[m] = ds
        dys_s[:, 0:B] = dy_ref[m]
        dys_s[:, B : B + SC] = ds
        weave([part(norm_back, c) for c in wide] + [part(out_grad, c) for c in wide], ahead[2 * third :])
        return row

    for step in norm_steps(0, 0):
        step()
    row = jnp.zeros((1, 128), f32)
    for m in range(micro):
        row = body(m, m % 2, row)
    last = micro - 1
    for step in end_steps(last, last % 2):
        step()
    row = end_row(last, last * nb * KINDS, last % 2, row, True)
    for m in range(micro):
        leave(m).wait()
    out_stats[...] = jnp.broadcast_to(row[None], out_stats.shape)


def head(me, lengths, stats, d, feats, enc, dy, own, other, w_rs, w_mask, w_dect, vec):
    micro, frames, _ = feats.shape
    outs = (
        (feats.shape, bf16),
        ((micro, L, frames), bf16),
        ((micro, L, frames), bf16),
        ((micro, frames, SC), bf16),
        (stats.shape, f32),
        ((B + SC, HW), f32),
        ((SC, C * N), f32),
        ((L, C * N), f32),
        ((8, HW), f32),
    )
    return pl.pallas_call(
        head_kernel,
        in_specs=[smem(), smem()] + [vmem()] * 11,
        out_specs=(pl.BlockSpec(memory_space=pl.ANY),) + (vmem(),) * (len(outs) - 1),
        scratch_shapes=[
            pltpu.VMEM((2, SEGS, 128), f32),
            pltpu.VMEM((micro, 5, 8, HW), f32),
            pltpu.VMEM((2, 4, 8, HW), f32),
            pltpu.VMEM((4, 8, HW), f32),
            pltpu.VMEM((2, frames, HW), bf16),
            pltpu.VMEM((2, frames, HW), f32),
            pltpu.VMEM((2, frames, HW), f32),
            pltpu.VMEM((frames, SC), bf16),
            pltpu.VMEM((frames, SC), f32),
            pltpu.VMEM((frames, B + SC), bf16),
            pltpu.VMEM((C, frames, N), f32),
            pltpu.VMEM((C, frames, N), f32),
            pltpu.VMEM((C, frames, N), bf16),
            pltpu.VMEM((C, frames, N), bf16),
            pltpu.VMEM((frames, SC), f32),
            pltpu.VMEM((frames, HW), f32),
            pltpu.VMEM((2, C, L, frames), bf16),
            pltpu.VMEM((C, L, frames), bf16),
            pltpu.VMEM(feats.shape, bf16),
            pltpu.SemaphoreType.DMA((micro,)),
        ],
        out_shape=tuple(jax.ShapeDtypeStruct(s, t) for s, t in outs),
        compiler_params=pltpu.CompilerParams(vmem_limit_bytes=HEAD_MIB * MIB),
        name="head",
    )(me, lengths, stats, d, feats, enc, dy, own, other, w_rs, w_mask, w_dect, vec)


def back_means(seg, stats):
    v = seg.means(stats)
    w = [v] + [pltpu.roll(v, 128 - k, 1) for k in range(1, KINDS)]
    p2, q2 = w[0], w[1]
    return p2, q2, w[2] - p2 * w[3] - q2 * w[4], w[5] - p2 * w[6] - q2 * w[7]


def input_kernel(
    me_ref,
    seg_ref,
    stats1_ref,
    stats2_ref,
    stats3_ref,
    d_ref,
    edge_ref,
    x_ref,
    dy_ref,
    dy_near,
    dy_far,
    ds_ref,
    ds_near,
    ds_far,
    w_in,
    w_rs,
    vec,
    feats_ref,
    g_in,
    g_vec,
    tab,
    par2,
    par1,
    col_s,
    dn2_s,
    dd_s,
    a_s,
    da_s,
    feats_s,
    sems,
):
    micro, frames, _ = d_ref.shape
    nb = frames // BLK
    halves = 2 * nb
    part = functools.partial
    for ref in (g_in, g_vec):
        ref[...] = jnp.zeros_like(ref)
    even = me_ref[0] % 2 == 0
    halo = slice(BLK, BLK + DIL)
    g1, g2 = 1.0 + vec[0:1, :], 1.0 + vec[2:3, :]
    seg = Segments(seg_ref, me_ref, micro, nb, stats1_ref.shape[0])
    tables = seg.norm(stats1_ref[:, 0, :]) + seg.norm(stats2_ref[:, 0, :])
    for k, table in enumerate(tables + back_means(seg, stats3_ref[:, 0, :])):
        tab[k] = table
    for m in range(micro):
        mean1, factor1, mean2, factor2, p2, q2, p1, q1 = [
            [seg.pick(tab.at[k], m, o) for o in range(nb + 2)] for k in range(8)
        ]
        for o in range(nb + 2):
            slope = 0.5 * factor2[o] * factor2[o] * q2[o]
            shift = 0.5 * factor2[o] * p2[o] - slope * mean2[o]
            rows = ((0.5 * factor2[o]) * g2, slope, shift)
            for k, v in enumerate(rows):
                par2[m, k, o : o + 1, :] = jnp.broadcast_to(v, (1, HW))
        for b in range(nb):
            o = b + 1
            scale = factor1[o] * g1
            slope = 0.5 * factor1[o] * factor1[o] * q1[o]
            rows = (
                scale,
                vec[1:2, :] - mean1[o] * scale,
                slope,
                0.5 * factor1[o] * p1[o] - slope * mean1[o],
                mean1[o],
                factor1[o],
                vec[4:5, :] * seg.same[m][o],
                vec[6:7, :] * seg.same[m][o - 1],
                seg.same[m][o],
                seg.same[m][o - 1],
            )
            for k, v in enumerate(rows):
                par1[m, k, b : b + 1, :] = jnp.broadcast_to(v, (1, HW))

    def project(m, slot):
        def side(at, first):
            near = jnp.concatenate([dy_near[m, halo, :], ds_near[m]], axis=1)
            far = jnp.concatenate([dy_far[m, halo, :], ds_far[m]], axis=1)
            dn2_s[at : at + DIL, :] = mm_t(jnp.where(even == first, far, near), w_rs[...])

        def main(c):
            dys = jnp.concatenate([dy_ref[m], ds_ref[m]], axis=1)
            dn2_s[DIL : DIL + frames, c : c + HALF_W] = mm_t(dys, w_rs[c : c + HALF_W, :])

        def hidden(c):
            a_s[slot, :, c : c + HALF_W] = mm(x_ref[m], w_in[:, c : c + HALF_W])

        wide = range(0, HW, HALF_W)
        return (
            [part(main, c) for c in wide]
            + [part(side, 0, True), part(side, DIL + frames, False)]
            + [part(hidden, c) for c in wide]
        )

    def depth_steps(m):
        def step(h, cols):
            o = (h + 1) // 2
            scale, slope, shift = [par2[m, k, o : o + 1, cols] for k in range(3)]
            total = jnp.zeros((8, LANES), f32)
            for r in range(0, DIL, ROWS):
                at = h * DIL + r
                if h == 0:
                    half = edge_ref[m, r : r + ROWS, cols]
                elif h == halves + 1:
                    half = edge_ref[m, DIL + r : DIL + r + ROWS, cols]
                else:
                    half = d_ref[m, at - DIL : at - DIL + ROWS, cols]
                v, sd = slope_parts(half, jnp.tanh(half))
                rows = slice(at, at + ROWS)
                dd = (sd * (dn2_s[rows, cols] * scale - v * slope - shift)).astype(bf16).astype(f32)
                dd_s[rows, cols] = dd
                total = total + fold_rows(dd)
            col_s[h : h + 1, cols] = row_sum(total)

        return [part(step, *t) for t in tiles_of(range(halves + 2))]

    def hidden_steps(m, slot):
        def step(h, cols):
            b = h // 2
            scale, shift, slope, base, mean, factor, k0, k2, hi, lo = [
                par1[m, k, b : b + 1, cols] for k in range(10)
            ]
            k1 = vec[5:6, cols]
            if h % 2 == 0:
                k0, hi = vec[4:5, cols], 1.0
            else:
                k2, lo = vec[6:7, cols], 1.0
            half_scale = 0.5 * scale
            s0 = s1 = s2 = jnp.zeros((8, LANES), f32)
            for r in range(h * DIL, (h + 1) * DIL, ROWS):
                prev, here, nxt = [dd_s[r + q * DIL : r + q * DIL + ROWS, cols] for q in range(3)]
                half = a_s[slot, r : r + ROWS, cols]
                u, su = slope_parts(half, jnp.tanh(half))
                n1 = (u * scale + shift).astype(bf16).astype(f32)
                s0 = s0 + fold_rows(nxt * n1)
                s1 = s1 + fold_rows(here * n1)
                s2 = s2 + fold_rows(prev * n1)
                dn1 = k1 * here + k0 * nxt + k2 * prev
                du = dn1 * half_scale - u * slope - base
                da_s[r : r + ROWS, cols] = (du * su).astype(bf16)
            s0, s1, s2 = [row_sum(v) for v in (s0, s1, s2)]
            prev, here, nxt = [col_s[h + q : h + q + 1, cols] for q in range(3)]
            dn1 = k1 * here + k0 * nxt + k2 * prev
            dn1_u = (k1 * s1 + k0 * s0 + k2 * s2 - shift * dn1) / scale
            rows = (
                (0, (dn1_u - mean * dn1) * factor),
                (1, dn1),
                (4, s0 * hi),
                (5, s1),
                (6, s2 * lo),
                (7, here),
            )
            for k, v in rows:
                g_vec[k : k + 1, cols] += v

        return [part(step, *t) for t in tiles_of(range(halves))]

    def last_steps(m):
        def weight(c):
            g_in[:, c : c + HALF_W] += mm_rows(x_ref[m], da_s[:, c : c + HALF_W])

        def feats(r):
            rows = slice(r, r + BLK)
            grad = dy_ref[m, rows, :].astype(f32) + 2.0 * mm_t(da_s[rows, :], w_in[...])
            feats_s[m, rows, :] = grad.astype(bf16)

        return [part(weight, c) for c in range(0, HW, HALF_W)] + [
            part(feats, r) for r in range(0, frames, BLK)
        ]

    def leave(m):
        return pltpu.make_async_copy(feats_s.at[m], feats_ref.at[m], sems.at[m])

    def body(m, slot, carry):
        run(project(m, 0) + depth_steps(m) + hidden_steps(m, 0) + last_steps(m))
        leave(m).start()
        return carry

    lax.fori_loop(0, micro, lambda m, c: body(m, 0, c), 0)
    for m in range(micro):
        leave(m).wait()


def input_grad(me, lengths, stats, d, edge, feats, dy, near, far, ds, ds_near, ds_far, w_in, w_rs, vec):
    micro, frames, _ = d.shape
    return pl.pallas_call(
        input_kernel,
        out_shape=(
            jax.ShapeDtypeStruct(feats.shape, bf16),
            jax.ShapeDtypeStruct((B, HW), f32),
            jax.ShapeDtypeStruct((8, HW), f32),
        ),
        in_specs=[smem(), smem()] + [vmem()] * 15,
        out_specs=(pl.BlockSpec(memory_space=pl.ANY), vmem(), vmem()),
        scratch_shapes=[
            pltpu.VMEM((8, SEGS, 128), f32),
            pltpu.VMEM((micro, 3, 8, HW), f32),
            pltpu.VMEM((micro, 10, 8, HW), f32),
            pltpu.VMEM((8, HW), f32),
            pltpu.VMEM((frames + 2 * DIL, HW), f32),
            pltpu.VMEM((frames + 2 * DIL, HW), f32),
            pltpu.VMEM((2, frames, HW), f32),
            pltpu.VMEM((frames, HW), bf16),
            pltpu.VMEM(feats.shape, bf16),
            pltpu.SemaphoreType.DMA((micro,)),
        ],
        compiler_params=pltpu.CompilerParams(vmem_limit_bytes=INPUT_MIB * MIB),
        name="input_grad",
    )(me, lengths, *stats, d, edge, feats, dy, near, far, ds, ds_near, ds_far, w_in, w_rs, vec)


def pack_kernel(pos_ref, g_in, g_rs, g_mask, g_dec, vec_a, vec_b, keep_ref, send_ref, t, out, wd):
    for k in range(4):
        cols = slice(128 * k, 128 * k + 128)
        t[pl.ds(R_IN + k, 128, stride=4), :] = g_in[:, cols]
        for c in range(C):
            t[pl.ds(R_MASK + 512 * c + k, 128, stride=4), :] = g_mask[
                :, 512 * c + 128 * k : 512 * c + 128 * k + 128
            ]
        t[pl.ds(R_VEC + k, 8, stride=4), :] = vec_a[:, cols] + vec_b[:, cols]
    t[R_RES : R_RES + 512, :] = g_rs[0:128, :].T
    t[R_SKIP : R_SKIP + 512, :] = g_rs[128:256, :].T
    wd[...] = jnp.concatenate([g_dec[...], jnp.zeros((128 - L, C * N), f32)], axis=0).T
    part = lax.broadcasted_iota(jnp.int32, (64, 128), 1) // L
    for c in range(C):
        rows = jnp.zeros((64, 128), f32)
        for s in range(8):
            piece = pltpu.roll(wd[pl.ds(512 * c + s, 64, stride=8), :], L * s, 1)
            rows = jnp.where(part == s, piece, rows)
        t[R_DEC + 64 * c : R_DEC + 64 * c + 64, :] = rows
    out[...] = jnp.zeros_like(out)
    for i in range(NCH):
        start = pl.multiple_of(pos_ref[i] * 8, 8)
        out[pl.ds(start, 8), :] = t[8 * i : 8 * i + 8, :]
    half = keep_ref.shape[0]
    keep_ref[...] = out[0:half, :]
    send_ref[...] = out[half : 2 * half, :].astype(bf16)


def pack(pos, g_in, g_rs, g_mask, g_dec, vec_a, vec_b, rows):
    return pl.pallas_call(
        pack_kernel,
        out_shape=(
            jax.ShapeDtypeStruct((rows // 2, 128), f32),
            jax.ShapeDtypeStruct((rows // 2, 128), bf16),
        ),
        in_specs=[smem()] + [vmem()] * 6,
        out_specs=(vmem(), vmem()),
        scratch_shapes=[
            pltpu.VMEM((ROWS_ALL, 128), f32),
            pltpu.VMEM((rows, 128), f32),
            pltpu.VMEM((C * N, 128), f32),
        ],
        compiler_params=pltpu.CompilerParams(vmem_limit_bytes=16 * MIB),
        name="pack",
    )(pos, g_in, g_rs, g_mask, g_dec, vec_a, vec_b)


def fold_kernel(n_got, n_next, *refs):
    keep_ref, got = refs[0], refs[1 : 1 + n_got]
    outs = refs[1 + n_got :]
    total = keep_ref[...]
    for g in got:
        total = total + g[...].astype(f32)
    size = total.shape[0] // n_next
    outs[0][...] = total[0:size, :]
    for q in range(1, n_next):
        outs[q][...] = total[q * size : (q + 1) * size, :].astype(bf16)


def fold(keep, got, n_next):
    size = keep.shape[0] // n_next
    outs = [jax.ShapeDtypeStruct((size, 128), f32)]
    outs += [jax.ShapeDtypeStruct((size, 128), bf16)] * (n_next - 1)
    return pl.pallas_call(
        functools.partial(fold_kernel, len(got), n_next),
        out_shape=tuple(outs),
        in_specs=[vmem()] * (1 + len(got)),
        out_specs=tuple(vmem() for _ in outs),
        compiler_params=pltpu.CompilerParams(vmem_limit_bytes=8 * MIB),
        name="fold",
    )(keep, *got)


def adam_kernel(n_got, count_ref, *refs):
    keep_ref, got = refs[0], refs[1 : 1 + n_got]
    master_ref, one_ref, two_ref, new_master, new_one, new_two, buf = refs[1 + n_got :]
    total = keep_ref[...]
    for g in got:
        total = total + g[...].astype(f32)
    buf[...] = total
    slots = master_ref.shape[0]
    used = lax.broadcasted_iota(jnp.int32, (slots, 128), 0) < count_ref[0]
    for j in range(8):
        cols = slice(128 * j, 128 * j + 128)
        grad = buf[pl.ds(j, slots, stride=8), :]
        master = master_ref[:, cols]
        one = beta_one * one_ref[:, cols] + (1.0 - beta_one) * grad
        two = beta_two * two_ref[:, cols] + (1.0 - beta_two) * grad * grad
        unbias_one = one / (1.0 - beta_one**STEP)
        unbias_two = two / (1.0 - beta_two**STEP)
        new = master - learn_rate * (
            unbias_one / (jnp.sqrt(unbias_two) + adam_eps) + weight_decay * master
        )
        new_master[:, cols] = jnp.where(used, new, 0.0)
        new_one[:, cols] = jnp.where(used, one, 0.0)
        new_two[:, cols] = jnp.where(used, two, 0.0)


def adam(count, keep, got, master, one, two):
    out = jax.ShapeDtypeStruct(master.shape, f32)
    return pl.pallas_call(
        functools.partial(adam_kernel, len(got)),
        out_shape=(out, out, out),
        in_specs=[smem()] + [vmem()] * (4 + len(got)),
        out_specs=(vmem(), vmem(), vmem()),
        scratch_shapes=[pltpu.VMEM(keep.shape, f32)],
        compiler_params=pltpu.CompilerParams(vmem_limit_bytes=4 * MIB),
        name="adam",
    )(count, keep, *got, master, one, two)


def local(n_tm, n_src, feats, encoded, seg_lengths, owners, master, moment_one, moment_two, out_cot, wave_cot):
    n_dev = n_tm * n_src
    me = lax.axis_index(AXES)
    core = lax.axis_index("src")
    micro, frames, _ = feats.shape
    nb = frames // BLK
    slots = master.shape[0]


    across = [(i, i + 1) for i in range(1, n_dev - 1, 2)]
    across = across + [(j, i) for i, j in across]

    def ends(at_end, *arrays):
        size = [jnp.where(at_end, v.shape[1] - w, 0) for v, w in arrays]
        rows = [lax.dynamic_slice_in_dim(v, at, w, axis=1) for (v, w), at in zip(arrays, size)]
        return rows[0] if len(rows) == 1 else jnp.concatenate(rows, axis=1)

    owner_ids = owners[:, 0]
    order = jnp.arange(NCH, dtype=jnp.int32)
    earlier = (owner_ids[:, None] == owner_ids[None, :]) & (order[None, :] < order[:, None])
    rank = jnp.sum(earlier.astype(jnp.int32), axis=1)
    pos = relative_block(owner_ids, me, n_dev) * slots + rank
    count = jnp.sum((owner_ids == me).astype(jnp.int32)).reshape(1)
    here = me.astype(jnp.int32).reshape(1)

    cot = jnp.transpose(wave_cot[:, 0], (0, 2, 1))

    def sides(x, dy, other):
        halo = (x, BLK), (dy, DIL)
        return ends(core == 0, *halo), ends(core == 1, *halo), other

    parts, (pos, here, count), (near, far, cot_other) = gather_tiles(
        to_tiles(master), n_dev, (pos, here, count), (feats, out_cot, cot), sides
    )
    near = swap(near, 1, n_dev)
    far = lax.ppermute(far, AXES, across)
    cot_other = swap(cot_other, 1, n_dev)

    w_in, w_rs, w_mask, w_dect, vec, stats = unpack(pos, parts, feats, n_dev)
    stats1 = share_sums(stats, n_dev)
    stats1, near, far, cot_other = lax.optimization_barrier((stats1, near, far, cot_other))
    d, edge, stats = depth(here, seg_lengths, stats1, feats, near, far, w_in, vec)
    stats2 = share_sums(stats, n_dev)
    block_out, wave_own, wave_other, ds, stats, g_rs, g_mask, g_dec, vec_a = head(
        here, seg_lengths, stats2, d, feats, encoded, out_cot, cot, cot_other, w_rs, w_mask, w_dect, vec
    )
    stats3 = share_sums(stats, n_dev)
    ds_near = swap(ends(core == 0, (ds, DIL)), 1, n_dev)
    ds_far = lax.ppermute(ends(core == 1, (ds, DIL)), AXES, across)

    wave_got = swap(wave_other, 1, n_dev)
    waves = jnp.concatenate(
        [jnp.where(core == 0, wave_own, wave_got), jnp.where(core == 0, wave_got, wave_own)], axis=2
    )
    waves = jnp.transpose(waves, (0, 2, 1))[:, None]

    feats_grad, g_in, vec_b = input_grad(
        here, seg_lengths, (stats1, stats2, stats3), d, edge, feats, out_cot, near, far, ds, ds_near, ds_far, w_in, w_rs, vec
    )

    keep, send = pack(pos, g_in, g_rs, g_mask, g_dec, vec_a, vec_b, n_dev * slots * 8)
    received = [swap(send, 1, n_dev)]
    for bits in reversed(stages(n_dev)[:-1]):
        n_next = 1 << len(bits)
        keep, *sends = fold(keep, received, n_next)
        received = [swap(s, spread(bits, k + 1), n_dev) for k, s in enumerate(sends)]
    new_master, new_one, new_two = adam(count, keep, received, master, moment_one, moment_two)
    return block_out, feats_grad, waves, new_master, new_one, new_two


def solution(mesh):
    n_tm, n_src = mesh.shape["tm"], mesh.shape["src"]
    return jax.shard_map(
        functools.partial(local, n_tm, n_src),
        mesh=mesh,
        in_specs=(
            P(None, AXES, None),
            P(None, AXES, None),
            P(),
            P(),
            P(AXES, None),
            P(AXES, None),
            P(AXES, None),
            P(None, AXES, None),
            P(None, "src", "tm", None),
        ),
        out_specs=(
            P(None, AXES, None),
            P(None, AXES, None),
            P(None, "src", "tm", None),
            P(AXES, None),
            P(AXES, None),
            P(AXES, None),
        ),
        check_vma=False,
    )
```
